32 devices in a mesh: item: 4 (over y, x), cent: 8 (over z, core).
Axes of the slice: x: 2, y: 2, z: 4, core: 2. Of those that a mesh axis runs over, the one named last changes fastest.
Arguments:
- vectors: bfloat16 [3072, 1024], P('item'), may hold values from -256 to 256, as said below
- centroids: bfloat16 [8192, 1024], P('cent'), may hold values from -6 to 6, as said below
Outputs:
- centroids_next: bfloat16 [8192, 1024], P(('cent', 'item'))
- log_norm: float32 [3072], P('item')
The draws below stay inside these ranges and needn't reach their ends.
Inputs may be any that keep to these rules, and one draw needn't show every extreme that they name: vectors hold finite values. `centroids`: centroid entries are independent.
All inputs are finite; a program needn't handle non-finite values.
Results may differ from the reference program's by a relative error of at most 0.0085.
Values may be sent and summed in bfloat16 or wider, within the bound.
No kernel may reach another device: no remote copies, remote signals or barrier semaphores. Data moves between devices by JAX's collectives and lax.ppermute only.
A program may use at most 64 MiB of HBM per device.

```python
import math
import jax
import jax.numpy as jnp
from jax import lax

D = 1024
NV_DEV = 768
ITERS = 2
NV = 3072
K = 8192
N_ITEM = 4


BETA = 3.0


def centroid_table(key):
    base = jax.random.normal(jax.random.fold_in(key, 7), (K, D), jnp.float32)
    return jnp.clip(base, -6.0, 6.0)


def draw_centroids(key, part):
    return centroid_table(key).astype(jnp.bfloat16)


def aligned_rows(key):
    table = centroid_table(key)
    keys = jax.random.split(jax.random.fold_in(key, 23), 3)
    first = jax.random.randint(keys[0], (NV,), 0, K)
    second = (first + 1 + jax.random.randint(keys[1], (NV,), 0, K - 1)) % K
    level = 120.0 + 80.0 * (jnp.arange(NV) // 64 % 3).astype(jnp.float32)
    strength = 0.5 + level / (BETA * math.sqrt(D))
    delta = jax.random.uniform(keys[2], (NV,), jnp.float32, 1.5, 2.5)
    near_one = table[first]
    near_two = table[second]
    norm_one = jnp.sum(near_one * near_one, axis=1)
    norm_two = jnp.sum(near_two * near_two, axis=1)
    cross = jnp.sum(near_one * near_two, axis=1)
    scale = BETA / math.sqrt(D)
    weight_two = (strength * norm_one - 0.5 * norm_one - strength * cross + 0.5 * norm_two - delta / scale) / (norm_two - cross)
    return strength[:, None] * near_one + weight_two[:, None] * near_two


def draw_vectors(key, part):
    noise_key = jax.random.fold_in(key, 19)
    base = jnp.clip(jax.random.normal(noise_key, (NV, D), jnp.float32), -6.0, 6.0)
    picked = jnp.arange(NV) % 64 == 0
    result = jnp.where(picked[:, None], aligned_rows(key), base)
    return jnp.clip(result, -256.0, 256.0).astype(jnp.bfloat16)


def setup_inputs(seed: int = 0) -> dict:
    splits = jax.random.split(jax.random.key(seed), 3)
    vectors = draw_vectors(jax.random.fold_in(splits[2], 71), 0)
    centroids = draw_centroids(jax.random.fold_in(splits[2], 71), 0)
    return {"vectors": vectors, "centroids": centroids}


BETA = 3.0

def reference(vectors, centroids):
    current = centroids
    scale = BETA / math.sqrt(D)
    blocks = vectors.reshape(N_ITEM, NV_DEV, D)
    log_rows = jnp.zeros((N_ITEM, NV_DEV), jnp.float32)
    for step in range(ITERS):
        sqnorm = lax.optimization_barrier(jnp.sum(jnp.square(current.astype(jnp.float32)), axis=1))

        def one_block(carry, block):
            sums, mass = carry
            raw = jnp.dot(block, current.T, preferred_element_type=jnp.float32)
            logits = scale * (raw - 0.5 * sqnorm[None, :])
            peak = lax.optimization_barrier(jnp.max(logits, axis=1))
            expo = jnp.exp(logits - peak[:, None])
            total = lax.optimization_barrier(jnp.sum(expo, axis=1))
            resp = (expo / total[:, None]).astype(jnp.bfloat16)
            term = jnp.dot(resp.T, block, preferred_element_type=jnp.float32)
            term = lax.optimization_barrier(term.astype(jnp.bfloat16)).astype(jnp.float32)
            mass = mass + lax.optimization_barrier(jnp.sum(resp.astype(jnp.float32), axis=0))
            return ((sums + term, mass), peak + jnp.log(total))
        start = (jnp.zeros((K, D), jnp.float32), jnp.zeros((K,), jnp.float32))
        (sums, mass), log_rows = lax.scan(one_block, start, blocks)
        current = ((sums + current.astype(jnp.float32)) / (mass + 1.0)[:, None]).astype(jnp.bfloat16)
    return (current, log_rows.reshape(NV))
```

```python
import functools
import math

import jax
import jax.numpy as jnp
from jax import lax
from jax.experimental import pallas as pl
from jax.experimental.pallas import tpu as pltpu
from jax.sharding import PartitionSpec as P

BETA = 3.0
BOTH = ("item", "cent")
VMEM_LIMIT = 56 * 1024 * 1024
NT = (((1,), (1,)), ((), ()))
NN = (((1,), (0,)), ((), ()))
SMALL = 2 * 1024 * 1024


def scores(rows, vectors, scale):
    raw = lax.dot_general(rows, vectors, NT, preferred_element_type=jnp.float32)
    sqnorm = jnp.sum(jnp.square(rows.astype(jnp.float32)), axis=1, keepdims=True)
    return scale * (raw - 0.5 * sqnorm)


def merge(parts, axis):
    peak = jnp.max(parts, axis=axis, keepdims=True)
    total = jnp.sum(jnp.exp(parts - peak), axis=axis, keepdims=True)
    return jnp.squeeze(peak + jnp.log(total), axis)


def partial_kernel(scale, v_ref, c_ref, out_ref, peak, total):
    step = pl.program_id(0)

    @pl.when(step == 0)
    def _():
        peak[...] = jnp.full_like(peak, -jnp.inf)
        total[...] = jnp.zeros_like(total)

    logits = scores(c_ref[...], v_ref[...], scale)
    top = jnp.maximum(peak[...], jnp.max(logits, axis=0, keepdims=True))
    total[...] = total[...] * jnp.exp(peak[...] - top) + jnp.sum(
        jnp.exp(logits - top), axis=0, keepdims=True
    )
    peak[...] = top

    @pl.when(step == pl.num_programs(0) - 1)
    def _():
        out_ref[...] = peak[...] + jnp.log(total[...])


def partial(vectors, centroids, scale):
    nv, dim = vectors.shape
    k = centroids.shape[0]
    rows = min(256, k)
    return pl.pallas_call(
        functools.partial(partial_kernel, scale),
        grid=(k // rows,),
        in_specs=[
            pl.BlockSpec((nv, dim), lambda i: (0, 0)),
            pl.BlockSpec((rows, dim), lambda i: (i, 0)),
        ],
        out_specs=pl.BlockSpec((1, nv), lambda i: (0, 0)),
        out_shape=jax.ShapeDtypeStruct((1, nv), jnp.float32),
        scratch_shapes=[pltpu.VMEM((1, nv), jnp.float32)] * 2,
        compiler_params=pltpu.CompilerParams(vmem_limit_bytes=24 * 1024 * 1024),
        cost_estimate=pl.CostEstimate(
            flops=2 * nv * k * dim, bytes_accessed=2 * (nv + k) * dim, transcendentals=nv * k
        ),
        name="partial_lse",
    )(vectors, centroids)


def block_of(plan, place):
    if plan["exchange"]:
        return lax.axis_index("item") ^ place
    return place


def fetches(plan, pieces, table, sems):
    nv = plan["nv"]
    core = lax.rem(lax.axis_index("cent"), 2)
    result = []
    for place, entries in enumerate(plan["blocks"]):
        base = block_of(plan, place) * nv
        copies = []
        for piece, start, half, offset, rows in entries:
            if half is None:
                lead = 0
            else:
                lead = (core if half else 1 - core) * (nv // 2)
            dst = pl.multiple_of(base + lead + offset, 64)
            src = pieces[piece]
            if start is not None:
                src = src.at[pl.ds(start, rows), :]
            copies.append(pltpu.make_async_copy(src, table.at[pl.ds(dst, rows), :], sems.at[len(copies), place]))
        result.append(copies)
    return result


def first_kernel(plan, scale, lse_ref, c_ref, *refs):
    n = plan["pieces"]
    pieces = refs[:n]
    new_ref, expo_ref, peak_ref, part_ref, table, own, lse, total, mass, sems, own_sem = refs[n:]
    nv, rows = plan["nv"], new_ref.shape[0]
    copies = fetches(plan, pieces, table, sems)
    start = pl.multiple_of(lax.axis_index("item") * rows, rows)
    own_copy = pltpu.make_async_copy(c_ref.at[pl.ds(start, rows), :], own, own_sem)
    own_copy.start()
    for block in copies:
        for copy in block:
            copy.start()
    lse[...] = merge(lse_ref[...], plan["merge_first"]).reshape(lse.shape)
    own_copy.wait()
    for place, block in enumerate(copies):
        for copy in block:
            copy.wait()
        index = block_of(plan, place)
        vectors = table[pl.ds(pl.multiple_of(index * nv, nv), nv), :]
        logits = scores(own[...], vectors, scale)
        resp = jnp.exp(logits - lse[pl.ds(index, 1), :]).astype(jnp.bfloat16)
        term = lax.dot_general(resp, vectors, NN, preferred_element_type=jnp.float32)
        weight = jnp.sum(resp.astype(jnp.float32), axis=1, keepdims=True)
        if place == 0:
            total[...] = term
            mass[...] = weight
        else:
            total[...] += term
            mass[...] += weight
    new_ref[...] = ((total[...] + own[...].astype(jnp.float32)) / (mass[...] + 1.0)).astype(jnp.bfloat16)
    for place in range(len(copies)):
        index = block_of(plan, place)
        vectors = table[pl.ds(pl.multiple_of(index * nv, nv), nv), :]
        logits = scores(new_ref[...], vectors, scale)
        peak = jnp.max(logits, axis=0, keepdims=True)
        expo = jnp.exp(logits - peak)
        expo_ref[place] = expo
        peak_ref[pl.ds(index, 1), :] = peak
        part_ref[pl.ds(index, 1), :] = peak + jnp.log(jnp.sum(expo, axis=0, keepdims=True))


def last_kernel(plan, lse_ref, old_ref, expo_ref, peak_ref, *refs):
    n = plan["pieces"]
    pieces = refs[:n]
    new_ref, norm_ref, table, lse, total, mass, sems = refs[n:]
    nv = plan["nv"]
    copies = fetches(plan, pieces, table, sems)
    for block in copies:
        for copy in block:
            copy.start()
    lse[...] = merge(lse_ref[...], plan["merge_last"]).reshape(lse.shape)
    norm_ref[...] = lse[pl.ds(lax.axis_index("item"), 1), :]
    for place, block in enumerate(copies):
        for copy in block:
            copy.wait()
        index = block_of(plan, place)
        vectors = table[pl.ds(pl.multiple_of(index * nv, nv), nv), :]
        factor = jnp.exp(peak_ref[pl.ds(index, 1), :] - lse[pl.ds(index, 1), :])
        resp = (expo_ref[place] * factor).astype(jnp.bfloat16)
        term = lax.dot_general(resp, vectors, NN, preferred_element_type=jnp.float32)
        weight = jnp.sum(resp.astype(jnp.float32), axis=1, keepdims=True)
        if place == 0:
            total[...] = term
            mass[...] = weight
        else:
            total[...] += term
            mass[...] += weight
    new_ref[...] = ((total[...] + old_ref[...].astype(jnp.float32)) / (mass[...] + 1.0)).astype(jnp.bfloat16)


def send(value, items, cents, item_of, cent_of):
    pairs = [
        (i * cents + c, item_of(i) * cents + cent_of(c)) for i in range(items) for c in range(cents)
    ]
    return lax.ppermute(value, BOTH, pairs)


def gather_vectors(vectors, items, cents):
    nv = vectors.shape[0]
    if items != 4:
        table = lax.all_gather(vectors, "item", axis=0, tiled=True)
        blocks = [[(0, i * nv, None, 0, nv)] for i in range(items)]
        return [table], dict(nv=nv, pieces=1, exchange=False, blocks=blocks)
    quarter = nv // 4
    core = lax.rem(lax.axis_index("cent"), 2)
    q = [lax.dynamic_slice_in_dim(vectors, core * (nv // 2) + s * quarter, quarter, 0) for s in range(2)]
    go = functools.partial(send, items=items, cents=cents)
    stay = lambda c: c
    over_x = lambda v: go(v, item_of=lambda i: i ^ 1, cent_of=stay)
    over_y = lambda v: go(v, item_of=lambda i: i ^ 2, cent_of=stay)
    over_core = lambda v: go(v, item_of=lambda i: i, cent_of=lambda c: c ^ 1)
    x1, y0 = over_x(q[1]), over_y(q[0])
    x0, y1 = over_x(q[0]), over_y(q[1])
    d0, d1 = over_x(y0), over_y(x1)
    pieces = [vectors]
    blocks = [[(0, None, None, 0, nv)]]
    for pair in ((x0, x1), (y0, y1), (d0, d1)):
        entries = []
        for s, value in enumerate(pair):
            entries.append((len(pieces), None, True, s * quarter, quarter))
            pieces.append(value)
            entries.append((len(pieces), None, False, s * quarter, quarter))
            pieces.append(over_core(value))
        blocks.append(entries)
    return pieces, dict(nv=nv, pieces=len(pieces), exchange=True, blocks=blocks)


def shards(vectors, centroids):
    items, cents = lax.axis_size("item"), lax.axis_size("cent")
    nv, dim = vectors.shape
    rows = centroids.shape[0] // items
    scale = BETA / math.sqrt(dim)
    pieces, plan = gather_vectors(vectors, items, cents)

    part = partial(vectors, centroids, scale)
    parts = lax.all_gather(part, BOTH, axis=0, tiled=True).reshape(items, cents, nv)
    plan["merge_first"] = 1
    deep = max(len(b) for b in plan["blocks"])
    table_scratch = pltpu.VMEM((items * nv, dim), jnp.bfloat16)
    any_spec = pl.BlockSpec(memory_space=pl.ANY)
    vmem = pl.BlockSpec(memory_space=pltpu.VMEM)
    flops = 2 * items * nv * rows * dim
    params = pltpu.CompilerParams(vmem_limit_bytes=VMEM_LIMIT)
    fresh, expo, peak, part = pl.pallas_call(
        functools.partial(first_kernel, plan, scale),
        in_specs=[vmem, any_spec] + [any_spec] * len(pieces),
        out_specs=[vmem] * 4,
        out_shape=[
            jax.ShapeDtypeStruct((rows, dim), jnp.bfloat16),
            jax.ShapeDtypeStruct((items, rows, nv), jnp.float32),
            jax.ShapeDtypeStruct((items, nv), jnp.float32),
            jax.ShapeDtypeStruct((items, nv), jnp.float32),
        ],
        scratch_shapes=[
            table_scratch,
            pltpu.VMEM((rows, dim), jnp.bfloat16),
            pltpu.VMEM((items, nv), jnp.float32),
            pltpu.VMEM((rows, dim), jnp.float32),
            pltpu.VMEM((rows, 1), jnp.float32),
            pltpu.SemaphoreType.DMA((deep, items)),
            pltpu.SemaphoreType.DMA,
        ],
        compiler_params=params,
        cost_estimate=pl.CostEstimate(
            flops=3 * flops, bytes_accessed=2 * items * nv * dim, transcendentals=2 * items * nv * rows
        ),
        name="first_iteration",
    )(parts, centroids, *pieces)

    if items * cents * part.size * 4 <= SMALL:
        parts = lax.all_gather(part, BOTH, axis=0, tiled=False)
    else:
        part = merge(lax.all_gather(part, "cent", axis=0, tiled=False), 0)
        parts = lax.all_gather(part, "item", axis=0, tiled=False)
    plan["merge_last"] = 0
    result, norm = pl.pallas_call(
        functools.partial(last_kernel, plan),
        in_specs=[vmem, vmem, vmem, vmem] + [any_spec] * len(pieces),
        out_specs=[vmem] * 2,
        out_shape=[
            jax.ShapeDtypeStruct((rows, dim), jnp.bfloat16),
            jax.ShapeDtypeStruct((1, nv), jnp.float32),
        ],
        scratch_shapes=[
            table_scratch,
            pltpu.VMEM((items, nv), jnp.float32),
            pltpu.VMEM((rows, dim), jnp.float32),
            pltpu.VMEM((rows, 1), jnp.float32),
            pltpu.SemaphoreType.DMA((deep, items)),
        ],
        compiler_params=params,
        cost_estimate=pl.CostEstimate(flops=flops, bytes_accessed=2 * items * nv * dim, transcendentals=0),
        name="last_iteration",
    )(parts, fresh, expo, peak, *pieces)
    return (result, norm.reshape(nv))


def solution(mesh):
    in_specs = (P("item", None), P("cent", None))
    out_specs = (P(("cent", "item"), None), P("item"))
    return jax.shard_map(shards, mesh=mesh, in_specs=in_specs, out_specs=out_specs, check_vma=False)
```

```python
import functools
import math

import jax
import jax.numpy as jnp
from jax import lax
from jax.experimental import pallas as pl
from jax.experimental.pallas import tpu as pltpu
from jax.sharding import PartitionSpec as P

BETA = 3.0
BOTH = ("item", "cent")
MIB = 1024 * 1024
NT = (((1,), (1,)), ((), ()))
NN = (((1,), (0,)), ((), ()))


def scores(rows, vectors, scale):
    raw = lax.dot_general(rows, vectors, NT, preferred_element_type=jnp.float32)
    sqnorm = jnp.sum(jnp.square(rows.astype(jnp.float32)), axis=1, keepdims=True)
    return scale * (raw - 0.5 * sqnorm)


def merge(parts):
    peak = functools.reduce(jnp.maximum, parts)
    terms = [jnp.exp(p - peak) for p in parts]
    while len(terms) > 1:
        terms = [sum(terms[i : i + 2]) for i in range(0, len(terms), 2)]
    return peak + jnp.log(terms[0])


def partial_kernel(scale, v_ref, c_ref, out_ref, peak, total):
    step = pl.program_id(0)

    @pl.when(step == 0)
    def _():
        peak[...] = jnp.full_like(peak, -jnp.inf)
        total[...] = jnp.zeros_like(total)

    logits = scores(c_ref[...], v_ref[...], scale)
    top = jnp.maximum(peak[...], jnp.max(logits, axis=0, keepdims=True))
    total[...] = total[...] * jnp.exp(peak[...] - top) + jnp.sum(
        jnp.exp(logits - top), axis=0, keepdims=True
    )
    peak[...] = top

    @pl.when(step == pl.num_programs(0) - 1)
    def _():
        out_ref[...] = peak[...] + jnp.log(total[...])


def in_hbm(value):
    return pltpu.with_memory_space_constraint(value, pltpu.HBM)


def in_vmem(value):
    return pltpu.with_memory_space_constraint(value, pltpu.VMEM)


def partial(vectors, centroids, scale):
    nv, dim = vectors.shape
    k = centroids.shape[0]
    rows = min(256, k)
    return pl.pallas_call(
        functools.partial(partial_kernel, scale),
        grid=(k // rows,),
        in_specs=[
            pl.BlockSpec((nv, dim), lambda i: (0, 0)),
            pl.BlockSpec((rows, dim), lambda i: (i, 0)),
        ],
        out_specs=pl.BlockSpec((1, nv), lambda i: (0, 0)),
        out_shape=jax.ShapeDtypeStruct((1, nv), jnp.float32),
        scratch_shapes=[pltpu.VMEM((1, nv), jnp.float32)] * 2,
        compiler_params=pltpu.CompilerParams(vmem_limit_bytes=16 * MIB),
        cost_estimate=pl.CostEstimate(
            flops=2 * nv * k * dim, bytes_accessed=2 * (nv + k) * dim, transcendentals=nv * k
        ),
        name="partial_lse",
    )(in_hbm(vectors), in_hbm(centroids))


def fetches(nv, blocks, pieces, table, sems):
    core = lax.rem(lax.axis_index("cent"), 2)
    result = []
    for place, entries in enumerate(blocks):
        copies = []
        for piece, start, mine, offset, rows in entries:
            lead = 0 if mine is None else (core if mine else 1 - core) * (nv // 2)
            dst = pl.multiple_of(place * nv + lead + offset, 64)
            src = pieces[piece] if start is None else pieces[piece].at[pl.ds(start, rows), :]
            copies.append(pltpu.make_async_copy(src, table.at[pl.ds(dst, rows), :], sems.at[len(copies), place]))
        result.append(copies)
    return result


def weigh(resp, vectors):
    term = lax.dot_general(resp, vectors, NN, preferred_element_type=jnp.float32)
    return term, jnp.sum(resp.astype(jnp.float32), axis=1, keepdims=True)


def updated(total, mass, old):
    return ((total + old.astype(jnp.float32)) / (mass + 1.0)).astype(jnp.bfloat16)


def open_kernel(plan, scale, c_ref, *refs):
    nv, blocks = plan["nv"], plan["early"]
    lse, refs = refs[: len(blocks)], refs[len(blocks) :]
    pieces, refs = refs[: plan["n_early"]], refs[plan["n_early"] :]
    table, own, total, mass, sems, own_sem = refs
    rows = own.shape[0]
    start = pl.multiple_of(lax.axis_index("item") * rows, rows)
    own_copy = pltpu.make_async_copy(c_ref.at[pl.ds(start, rows), :], own, own_sem)
    own_copy.start()
    copies = fetches(nv, blocks, pieces, table, sems)
    for block in copies:
        for copy in block:
            copy.start()
    own_copy.wait()
    for place, block in enumerate(copies):
        for copy in block:
            copy.wait()
        vectors = table[pl.ds(place * nv, nv), :]
        resp = jnp.exp(scores(own[...], vectors, scale) - lse[place][...]).astype(jnp.bfloat16)
        term, weight = weigh(resp, vectors)
        total[...] = term if place == 0 else total[...] + term
        mass[...] = weight if place == 0 else mass[...] + weight


def close_kernel(plan, scale, early, own, total, mass, *refs):
    nv, blocks, first = plan["nv"], plan["late"], len(plan["early"])
    lse, refs = refs[: len(blocks)], refs[len(blocks) :]
    pieces, refs = refs[: plan["n_late"]], refs[plan["n_late"] :]
    new_ref, expo_ref, peak_ref, part_ref = refs[:4]
    late = sems = None
    if blocks:
        late, sems = refs[4:]
        copies = fetches(nv, blocks, pieces, late, sems)
        for block in copies:
            for copy in block:
                copy.start()
        sums, weights = total[...], mass[...]
        for place, block in enumerate(copies):
            for copy in block:
                copy.wait()
            vectors = late[pl.ds(place * nv, nv), :]
            resp = jnp.exp(scores(own[...], vectors, scale) - lse[place][...]).astype(jnp.bfloat16)
            term, weight = weigh(resp, vectors)
            sums, weights = sums + term, weights + weight
        new_ref[...] = updated(sums, weights, own[...])
    else:
        new_ref[...] = updated(total[...], mass[...], own[...])
    for place in range(first + len(blocks)):
        vectors = early[pl.ds(place * nv, nv), :] if place < first else late[pl.ds((place - first) * nv, nv), :]
        logits = scores(new_ref[...], vectors, scale)
        peak = jnp.max(logits, axis=0, keepdims=True)
        expo = jnp.exp(logits - peak)
        expo_ref[place] = expo
        peak_ref[pl.ds(place, 1), :] = peak
        part_ref[pl.ds(place, 1), :] = peak + jnp.log(jnp.sum(expo, axis=0, keepdims=True))


def last_kernel(plan, old_ref, expo_ref, peak_ref, *refs):
    nv, n = plan["nv"], plan["n_parts"]
    first, second = len(plan["early"]), len(plan["late"])
    parts, refs = refs[:n], refs[n:]
    early, refs = refs[0], refs[1:]
    late = refs[0] if second else None
    new_ref, norm_ref, total, mass = refs[1:] if second else refs
    for place in range(first + second):
        if n == 1:
            lse = parts[0][pl.ds(place, 1), :]
        else:
            lse = merge([parts[k][pl.ds(place ^ k, 1), :] for k in range(n)])
        if plan["n_parts"] > 1 and place == 0:
            norm_ref[...] = lse.reshape(nv)
        vectors = early[pl.ds(place * nv, nv), :] if place < first else late[pl.ds((place - first) * nv, nv), :]
        factor = jnp.exp(peak_ref[pl.ds(place, 1), :] - lse)
        term, weight = weigh((expo_ref[place] * factor).astype(jnp.bfloat16), vectors)
        total[...] = term if place == 0 else total[...] + term
        mass[...] = weight if place == 0 else mass[...] + weight
    if n == 1:
        norm_ref[...] = parts[0][pl.ds(lax.axis_index("item"), 1), :].reshape(nv)
    new_ref[...] = updated(total[...], mass[...], old_ref[...])


def send(value, items, cents, item_mask, cent_mask):
    pairs = [
        (i * cents + c, (i ^ item_mask) * cents + (c ^ cent_mask)) for i in range(items) for c in range(cents)
    ]
    return lax.ppermute(value, BOTH, pairs)


def shards(vectors, centroids):
    items, cents = lax.axis_size("item"), lax.axis_size("cent")
    nv, dim = vectors.shape
    rows = centroids.shape[0] // items
    scale = BETA / math.sqrt(dim)
    go = functools.partial(send, items=items, cents=cents)
    small = items == 4 and cents == 8
    if small:
        quarter = nv // 4
        core = lax.rem(lax.axis_index("cent"), 2)
        q = [lax.dynamic_slice_in_dim(vectors, core * (nv // 2) + s * quarter, quarter, 0) for s in range(2)]
        x1, y0 = go(q[1], item_mask=1, cent_mask=0), go(q[0], item_mask=2, cent_mask=0)
        x0, y1 = go(q[0], item_mask=1, cent_mask=0), go(q[1], item_mask=2, cent_mask=0)
        part = partial(vectors, centroids, scale)
        x1, y0, part = lax.optimization_barrier((x1, y0, part))
        lse = merge([part] + [go(part, item_mask=0, cent_mask=k) for k in range(1, cents)])
        lses = [lse] + [go(lse, item_mask=k, cent_mask=0) for k in range(1, items)]
        d0, d1 = go(y0, item_mask=1, cent_mask=0), go(x1, item_mask=2, cent_mask=0)

        def pieces_of(pairs, at):
            pieces, blocks = [], []
            for pair in pairs:
                entries = []
                for s, value in enumerate(pair):
                    for mine in (True, False):
                        entries.append((at + len(pieces), None, mine, s * quarter, quarter))
                        pieces.append(value if mine else go(value, item_mask=0, cent_mask=1))
                blocks.append(entries)
            return pieces, blocks

        early, early_blocks = pieces_of(((x0, x1), (y0, y1)), 1)
        early = [vectors] + early
        early_blocks = [[(0, None, None, 0, nv)]] + early_blocks
        late, late_blocks = pieces_of(((d0, d1),), 0)
    else:
        early = [lax.all_gather(vectors, "item", axis=0, tiled=True)]
        early_blocks = [[(0, i * nv, None, 0, nv)] for i in range(items)]
        late, late_blocks = [], []
        part = partial(vectors, centroids, scale)
        parts = lax.all_gather(part, "cent", axis=0, tiled=False)
        lse = lax.all_gather(merge([parts[i] for i in range(cents)]), "item", axis=0, tiled=False)
        lses = [lse[i] for i in range(items)]
    plan = dict(nv=nv, early=early_blocks, late=late_blocks, n_early=len(early), n_late=len(late))

    any_spec = pl.BlockSpec(memory_space=pl.ANY)
    vmem = pl.BlockSpec(memory_space=pltpu.VMEM)
    n_early, n_late = len(early_blocks), len(late_blocks)
    flops = 2 * nv * rows * dim
    params = pltpu.CompilerParams(vmem_limit_bytes=20 * MIB)
    table, own, total, mass = pl.pallas_call(
        functools.partial(open_kernel, plan, scale),
        in_specs=[any_spec] + [vmem] * n_early + [any_spec] * len(early),
        out_specs=[vmem] * 4,
        out_shape=[
            pltpu.VMEM((n_early * nv, dim), jnp.bfloat16),
            pltpu.VMEM((rows, dim), jnp.bfloat16),
            pltpu.VMEM((rows, dim), jnp.float32),
            pltpu.VMEM((rows, 1), jnp.float32),
        ],
        scratch_shapes=[
            pltpu.SemaphoreType.DMA((max(len(b) for b in early_blocks), n_early)),
            pltpu.SemaphoreType.DMA,
        ],
        compiler_params=params,
        cost_estimate=pl.CostEstimate(
            flops=2 * n_early * flops, bytes_accessed=2 * n_early * nv * dim, transcendentals=n_early * nv * rows
        ),
        name="early_blocks",
    )(centroids, *lses[:n_early], *early)

    late_out = [pltpu.VMEM((n_late * nv, dim), jnp.bfloat16)] if n_late else []
    late_sems = [pltpu.SemaphoreType.DMA((max(len(b) for b in late_blocks), n_late))] if n_late else []
    fresh, expo, peak, part, *tables = pl.pallas_call(
        functools.partial(close_kernel, plan, scale),
        in_specs=[vmem] * (4 + n_late) + [any_spec] * len(late),
        out_specs=[vmem] * (4 + len(late_out)),
        out_shape=[
            pltpu.VMEM((rows, dim), jnp.bfloat16),
            pltpu.VMEM((items, rows, nv), jnp.float32),
            pltpu.VMEM((items, nv), jnp.float32),
            pltpu.VMEM((items, nv), jnp.float32),
        ]
        + late_out,
        scratch_shapes=late_sems,
        compiler_params=params,
        cost_estimate=pl.CostEstimate(
            flops=(items + 2 * n_late) * flops,
            bytes_accessed=2 * n_late * nv * dim,
            transcendentals=(items + n_late) * nv * rows,
        ),
        name="late_blocks",
    )(in_vmem(table), in_vmem(own), in_vmem(total), in_vmem(mass), *lses[n_early:], *late)

    if small:
        lse = merge([part] + [go(part, item_mask=0, cent_mask=k) for k in range(1, cents)])
        parts = [lse] + [go(lse, item_mask=k, cent_mask=0) for k in range(1, items)]
    else:
        gathered = lax.all_gather(part, "cent", axis=0, tiled=False)
        lse = merge([gathered[i] for i in range(cents)])
        gathered = lax.all_gather(lse, "item", axis=0, tiled=False)
        parts = [merge([gathered[i] for i in range(items)])]
    plan["n_parts"] = len(parts)
    result, norm = pl.pallas_call(
        functools.partial(last_kernel, plan),
        in_specs=[vmem] * (4 + len(parts) + len(tables)),
        out_specs=[vmem] * 2,
        out_shape=[
            jax.ShapeDtypeStruct((rows, dim), jnp.bfloat16),
            jax.ShapeDtypeStruct((nv,), jnp.float32),
        ],
        scratch_shapes=[pltpu.VMEM((rows, dim), jnp.float32), pltpu.VMEM((rows, 1), jnp.float32)],
        compiler_params=params,
        cost_estimate=pl.CostEstimate(flops=items * flops, bytes_accessed=2 * rows * dim, transcendentals=0),
        name="last_iteration",
    )(in_vmem(fresh), in_vmem(expo), in_vmem(peak), *parts, in_vmem(table), *[in_vmem(t) for t in tables])
    return (result, norm)


def solution(mesh):
    in_specs = (P("item", None), P("cent", None))
    out_specs = (P(("cent", "item"), None), P("item"))
    return jax.shard_map(shards, mesh=mesh, in_specs=in_specs, out_specs=out_specs, check_vma=False)
```

```python
import functools
import math

import jax
import jax.numpy as jnp
from jax import lax
from jax.experimental import pallas as pl
from jax.experimental.pallas import tpu as pltpu
from jax.sharding import PartitionSpec as P

BETA = 3.0
BOTH = ("item", "cent")
MIB = 1024 * 1024
NT = (((1,), (1,)), ((), ()))
NN = (((1,), (0,)), ((), ()))


def scores(rows, vectors, scale):
    raw = lax.dot_general(rows, vectors, NT, preferred_element_type=jnp.float32)
    sqnorm = jnp.sum(jnp.square(rows.astype(jnp.float32)), axis=1, keepdims=True)
    return scale * (raw - 0.5 * sqnorm)


def merge(parts):
    peak = functools.reduce(jnp.maximum, parts)
    terms = [jnp.exp(p - peak) for p in parts]
    while len(terms) > 1:
        terms = [sum(terms[i : i + 2]) for i in range(0, len(terms), 2)]
    return peak + jnp.log(terms[0])


def partial_kernel(scale, v_ref, c_ref, out_ref, peak, total):
    step = pl.program_id(0)

    @pl.when(step == 0)
    def _():
        peak[...] = jnp.full_like(peak, -jnp.inf)
        total[...] = jnp.zeros_like(total)

    logits = scores(c_ref[...], v_ref[...], scale)
    top = jnp.maximum(peak[...], jnp.max(logits, axis=0, keepdims=True))
    total[...] = total[...] * jnp.exp(peak[...] - top) + jnp.sum(
        jnp.exp(logits - top), axis=0, keepdims=True
    )
    peak[...] = top

    @pl.when(step == pl.num_programs(0) - 1)
    def _():
        out_ref[...] = peak[...] + jnp.log(total[...])


def in_hbm(value):
    return pltpu.with_memory_space_constraint(value, pltpu.HBM)


def in_vmem(value):
    return pltpu.with_memory_space_constraint(value, pltpu.VMEM)


def partial(vectors, centroids, scale):
    nv, dim = vectors.shape
    k = centroids.shape[0]
    rows = min(256, k)
    return pl.pallas_call(
        functools.partial(partial_kernel, scale),
        grid=(k // rows,),
        in_specs=[
            pl.BlockSpec((nv, dim), lambda i: (0, 0)),
            pl.BlockSpec((rows, dim), lambda i: (i, 0)),
        ],
        out_specs=pl.BlockSpec((1, nv), lambda i: (0, 0)),
        out_shape=jax.ShapeDtypeStruct((1, nv), jnp.float32),
        scratch_shapes=[pltpu.VMEM((1, nv), jnp.float32)] * 2,
        compiler_params=pltpu.CompilerParams(vmem_limit_bytes=16 * MIB),
        cost_estimate=pl.CostEstimate(
            flops=2 * nv * k * dim, bytes_accessed=2 * (nv + k) * dim, transcendentals=nv * k
        ),
        name="partial_lse",
    )(in_hbm(vectors), in_hbm(centroids))


def fetches(nv, blocks, pieces, table, sems):
    core = lax.rem(lax.axis_index("cent"), 2)
    result = []
    for place, entries in enumerate(blocks):
        copies = []
        for piece, start, mine, offset, rows in entries:
            lead = 0 if mine is None else (core if mine else 1 - core) * (nv // 2)
            dst = pl.multiple_of(place * nv + lead + offset, 64)
            src = pieces[piece] if start is None else pieces[piece].at[pl.ds(start, rows), :]
            copies.append(pltpu.make_async_copy(src, table.at[pl.ds(dst, rows), :], sems.at[len(copies), place]))
        result.append(copies)
    return result


def weigh(resp, vectors):
    term = lax.dot_general(resp, vectors, NN, preferred_element_type=jnp.float32)
    return term, jnp.sum(resp.astype(jnp.float32), axis=1, keepdims=True)


def updated(total, mass, old):
    return ((total + old.astype(jnp.float32)) / (mass + 1.0)).astype(jnp.bfloat16)


def index_of(plan, place):
    return lax.axis_index("item") ^ place if plan["exchange"] else place


def row_lse(plan, parts, place):
    cents = plan["cents"]
    rows = parts[pl.ds(pl.multiple_of(index_of(plan, place) * cents, cents), cents), :]
    peak = jnp.max(rows, axis=0, keepdims=True)
    return peak + jnp.log(jnp.sum(jnp.exp(rows - peak), axis=0, keepdims=True))


def open_kernel(plan, scale, c_ref, parts, *refs):
    nv, blocks = plan["nv"], plan["early"]
    pieces, refs = refs[: plan["n_early"]], refs[plan["n_early"] :]
    table, own, total, mass, sems, own_sem = refs
    rows = own.shape[0]
    start = pl.multiple_of(lax.axis_index("item") * rows, rows)
    own_copy = pltpu.make_async_copy(c_ref.at[pl.ds(start, rows), :], own, own_sem)
    own_copy.start()
    copies = fetches(nv, blocks, pieces, table, sems)
    for block in copies:
        for copy in block:
            copy.start()
    own_copy.wait()
    for place, block in enumerate(copies):
        for copy in block:
            copy.wait()
        vectors = table[pl.ds(place * nv, nv), :]
        resp = jnp.exp(scores(own[...], vectors, scale) - row_lse(plan, parts, place)).astype(jnp.bfloat16)
        term, weight = weigh(resp, vectors)
        total[...] = term if place == 0 else total[...] + term
        mass[...] = weight if place == 0 else mass[...] + weight


def close_kernel(plan, scale, early, own, total, mass, parts, *refs):
    nv, blocks, first = plan["nv"], plan["late"], len(plan["early"])
    pieces, refs = refs[: plan["n_late"]], refs[plan["n_late"] :]
    new_ref, expo_ref, peak_ref, part_ref = refs[:4]
    late = sems = None
    if blocks:
        late, sems = refs[4:]
        copies = fetches(nv, blocks, pieces, late, sems)
        for block in copies:
            for copy in block:
                copy.start()
        sums, weights = total[...], mass[...]
        for place, block in enumerate(copies):
            for copy in block:
                copy.wait()
            vectors = late[pl.ds(place * nv, nv), :]
            resp = jnp.exp(scores(own[...], vectors, scale) - row_lse(plan, parts, first + place)).astype(jnp.bfloat16)
            term, weight = weigh(resp, vectors)
            sums, weights = sums + term, weights + weight
        new_ref[...] = updated(sums, weights, own[...])
    else:
        new_ref[...] = updated(total[...], mass[...], own[...])
    for place in range(first + len(blocks)):
        vectors = early[pl.ds(place * nv, nv), :] if place < first else late[pl.ds((place - first) * nv, nv), :]
        logits = scores(new_ref[...], vectors, scale)
        peak = jnp.max(logits, axis=0, keepdims=True)
        expo = jnp.exp(logits - peak)
        expo_ref[place] = expo
        peak_ref[pl.ds(place, 1), :] = peak
        part_ref[pl.ds(index_of(plan, place), 1), :] = peak + jnp.log(jnp.sum(expo, axis=0, keepdims=True))


def last_kernel(plan, old_ref, expo_ref, peak_ref, parts, *refs):
    nv = plan["nv"]
    first, second = len(plan["early"]), len(plan["late"])
    early, refs = refs[0], refs[1:]
    late = refs[0] if second else None
    new_ref, norm_ref, lse_ref, total, mass = refs[1:] if second else refs
    lse_ref[...] = merge([parts[i] for i in range(parts.shape[0])])
    norm_ref[...] = lse_ref[pl.ds(lax.axis_index("item"), 1), :].reshape(nv)
    for place in range(first + second):
        lse = lse_ref[pl.ds(index_of(plan, place), 1), :]
        vectors = early[pl.ds(place * nv, nv), :] if place < first else late[pl.ds((place - first) * nv, nv), :]
        factor = jnp.exp(peak_ref[pl.ds(place, 1), :] - lse)
        term, weight = weigh((expo_ref[place] * factor).astype(jnp.bfloat16), vectors)
        total[...] = term if place == 0 else total[...] + term
        mass[...] = weight if place == 0 else mass[...] + weight
    new_ref[...] = updated(total[...], mass[...], old_ref[...])


def send(value, items, cents, item_mask, cent_mask):
    pairs = [
        (i * cents + c, (i ^ item_mask) * cents + (c ^ cent_mask)) for i in range(items) for c in range(cents)
    ]
    return lax.ppermute(value, BOTH, pairs)


def everyone(value, axes):
    n = lax.axis_size(axes)
    return lax.all_to_all(jnp.broadcast_to(value, (n,) + value.shape), axes, 0, 0, tiled=True)


def shards(vectors, centroids):
    items, cents = lax.axis_size("item"), lax.axis_size("cent")
    nv, dim = vectors.shape
    rows = centroids.shape[0] // items
    scale = BETA / math.sqrt(dim)
    go = functools.partial(send, items=items, cents=cents)
    small = items == 4 and cents == 8
    if small:
        quarter = nv // 4
        core = lax.rem(lax.axis_index("cent"), 2)
        q = [lax.dynamic_slice_in_dim(vectors, core * (nv // 2) + s * quarter, quarter, 0) for s in range(2)]
        x1, y0 = go(q[1], item_mask=1, cent_mask=0), go(q[0], item_mask=2, cent_mask=0)
        x0, y1 = go(q[0], item_mask=1, cent_mask=0), go(q[1], item_mask=2, cent_mask=0)
        part = partial(vectors, centroids, scale)
        parts = everyone(part, BOTH).reshape(items * cents, nv)
        x0, x1, y0, y1 = [lax.optimization_barrier((piece, parts))[0] for piece in (x0, x1, y0, y1)]
        d0, d1 = go(y0, item_mask=1, cent_mask=0), go(x1, item_mask=2, cent_mask=0)

        def pieces_of(pairs, at):
            pieces, blocks = [], []
            for pair in pairs:
                entries = []
                for s, value in enumerate(pair):
                    for mine in (True, False):
                        entries.append((at + len(pieces), None, mine, s * quarter, quarter))
                        pieces.append(value if mine else go(value, item_mask=0, cent_mask=1))
                blocks.append(entries)
            return pieces, blocks

        early, early_blocks = pieces_of(((x0, x1), (y0, y1)), 1)
        early = [vectors] + early
        early_blocks = [[(0, None, None, 0, nv)]] + early_blocks
        late, late_blocks = pieces_of(((d0, d1),), 0)
    else:
        early = [lax.all_gather(vectors, "item", axis=0, tiled=True)]
        early_blocks = [[(0, i * nv, None, 0, nv)] for i in range(items)]
        late, late_blocks = [], []
        part = partial(vectors, centroids, scale)
        parts = lax.all_gather(part, BOTH, axis=0, tiled=True)
    plan = dict(nv=nv, cents=cents, exchange=small, early=early_blocks, late=late_blocks, n_early=len(early), n_late=len(late))

    any_spec = pl.BlockSpec(memory_space=pl.ANY)
    vmem = pl.BlockSpec(memory_space=pltpu.VMEM)
    n_early, n_late = len(early_blocks), len(late_blocks)
    flops = 2 * nv * rows * dim
    params = pltpu.CompilerParams(vmem_limit_bytes=20 * MIB)
    table, own, total, mass = pl.pallas_call(
        functools.partial(open_kernel, plan, scale),
        in_specs=[any_spec, vmem] + [any_spec] * len(early),
        out_specs=[vmem] * 4,
        out_shape=[
            pltpu.VMEM((n_early * nv, dim), jnp.bfloat16),
            pltpu.VMEM((rows, dim), jnp.bfloat16),
            pltpu.VMEM((rows, dim), jnp.float32),
            pltpu.VMEM((rows, 1), jnp.float32),
        ],
        scratch_shapes=[
            pltpu.SemaphoreType.DMA((max(len(b) for b in early_blocks), n_early)),
            pltpu.SemaphoreType.DMA,
        ],
        compiler_params=params,
        cost_estimate=pl.CostEstimate(
            flops=2 * n_early * flops, bytes_accessed=2 * n_early * nv * dim, transcendentals=n_early * nv * rows
        ),
        name="early_blocks",
    )(centroids, parts, *early)

    late_out = [pltpu.VMEM((n_late * nv, dim), jnp.bfloat16)] if n_late else []
    late_sems = [pltpu.SemaphoreType.DMA((max(len(b) for b in late_blocks), n_late))] if n_late else []
    fresh, expo, peak, part, *tables = pl.pallas_call(
        functools.partial(close_kernel, plan, scale),
        in_specs=[vmem] * 5 + [any_spec] * len(late),
        out_specs=[vmem] * (4 + len(late_out)),
        out_shape=[
            pltpu.VMEM((rows, dim), jnp.bfloat16),
            pltpu.VMEM((items, rows, nv), jnp.float32),
            pltpu.VMEM((items, nv), jnp.float32),
            pltpu.VMEM((items, nv), jnp.float32),
        ]
        + late_out,
        scratch_shapes=late_sems,
        compiler_params=params,
        cost_estimate=pl.CostEstimate(
            flops=(items + 2 * n_late) * flops,
            bytes_accessed=2 * n_late * nv * dim,
            transcendentals=(items + n_late) * nv * rows,
        ),
        name="late_blocks",
    )(in_vmem(table), in_vmem(own), in_vmem(total), in_vmem(mass), parts, *late)

    if small:
        gathered = everyone(part, "cent")
        parts = everyone(merge([gathered[i] for i in range(cents)]), "item")
    else:
        gathered = lax.all_gather(part, "cent", axis=0, tiled=False)
        parts = lax.all_gather(merge([gathered[i] for i in range(cents)]), "item", axis=0, tiled=False)
    result, norm = pl.pallas_call(
        functools.partial(last_kernel, plan),
        in_specs=[vmem] * (5 + len(tables)),
        out_specs=[vmem] * 2,
        out_shape=[
            jax.ShapeDtypeStruct((rows, dim), jnp.bfloat16),
            jax.ShapeDtypeStruct((nv,), jnp.float32),
        ],
        scratch_shapes=[
            pltpu.VMEM((items, nv), jnp.float32),
            pltpu.VMEM((rows, dim), jnp.float32),
            pltpu.VMEM((rows, 1), jnp.float32),
        ],
        compiler_params=params,
        cost_estimate=pl.CostEstimate(flops=items * flops, bytes_accessed=2 * rows * dim, transcendentals=0),
        name="last_iteration",
    )(in_vmem(fresh), in_vmem(expo), in_vmem(peak), parts, in_vmem(table), *[in_vmem(t) for t in tables])
    return (result, norm)


def solution(mesh):
    in_specs = (P("item", None), P("cent", None))
    out_specs = (P(("cent", "item"), None), P("item"))
    return jax.shard_map(shards, mesh=mesh, in_specs=in_specs, out_specs=out_specs, check_vma=False)
```

```python
import functools
import math

import jax
import jax.numpy as jnp
from jax import lax
from jax.experimental import pallas as pl
from jax.experimental.pallas import tpu as pltpu
from jax.sharding import PartitionSpec as P

BETA = 3.0
BOTH = ("item", "cent")
MIB = 1024 * 1024
NT = (((1,), (1,)), ((), ()))
NN = (((1,), (0,)), ((), ()))


def scores(rows, vectors, scale):
    raw = lax.dot_general(rows, vectors, NT, preferred_element_type=jnp.float32)
    sqnorm = jnp.sum(jnp.square(rows.astype(jnp.float32)), axis=1, keepdims=True)
    return scale * (raw - 0.5 * sqnorm)


def merge(parts):
    peak = functools.reduce(jnp.maximum, parts)
    terms = [jnp.exp(p - peak) for p in parts]
    while len(terms) > 1:
        terms = [sum(terms[i : i + 2]) for i in range(0, len(terms), 2)]
    return peak + jnp.log(terms[0])


def partial_kernel(scale, v_ref, c_ref, out_ref, peak, total):
    step = pl.program_id(0)

    @pl.when(step == 0)
    def _():
        peak[...] = jnp.full_like(peak, -jnp.inf)
        total[...] = jnp.zeros_like(total)

    logits = scores(c_ref[...], v_ref[...], scale)
    top = jnp.maximum(peak[...], jnp.max(logits, axis=0, keepdims=True))
    total[...] = total[...] * jnp.exp(peak[...] - top) + jnp.sum(
        jnp.exp(logits - top), axis=0, keepdims=True
    )
    peak[...] = top

    @pl.when(step == pl.num_programs(0) - 1)
    def _():
        out_ref[...] = peak[...] + jnp.log(total[...])


def in_hbm(value):
    return pltpu.with_memory_space_constraint(value, pltpu.HBM)


def in_vmem(value):
    return pltpu.with_memory_space_constraint(value, pltpu.VMEM)


def partial(vectors, centroids, scale):
    nv, dim = vectors.shape
    k = centroids.shape[0]
    rows = min(256, k)
    return pl.pallas_call(
        functools.partial(partial_kernel, scale),
        grid=(k // rows,),
        in_specs=[
            pl.BlockSpec((nv, dim), lambda i: (0, 0)),
            pl.BlockSpec((rows, dim), lambda i: (i, 0)),
        ],
        out_specs=pl.BlockSpec((1, nv), lambda i: (0, 0)),
        out_shape=jax.ShapeDtypeStruct((1, nv), jnp.float32),
        scratch_shapes=[pltpu.VMEM((1, nv), jnp.float32)] * 2,
        compiler_params=pltpu.CompilerParams(vmem_limit_bytes=16 * MIB),
        cost_estimate=pl.CostEstimate(
            flops=2 * nv * k * dim, bytes_accessed=2 * (nv + k) * dim, transcendentals=nv * k
        ),
        name="partial_lse",
    )(in_hbm(vectors), in_hbm(centroids))


def fetches(nv, blocks, pieces, table, sems):
    core = lax.rem(lax.axis_index("cent"), 2)
    result = []
    for place, entries in enumerate(blocks):
        copies = []
        for piece, start, mine, offset, rows in entries:
            lead = 0 if mine is None else (core if mine else 1 - core) * (nv // 2)
            dst = pl.multiple_of(place * nv + lead + offset, 64)
            src = pieces[piece] if start is None else pieces[piece].at[pl.ds(start, rows), :]
            copies.append(pltpu.make_async_copy(src, table.at[pl.ds(dst, rows), :], sems.at[len(copies), place]))
        result.append(copies)
    return result


def weigh(resp, vectors):
    term = lax.dot_general(resp, vectors, NN, preferred_element_type=jnp.float32)
    return term, jnp.sum(resp.astype(jnp.float32), axis=1, keepdims=True)


def updated(total, mass, old):
    return ((total + old.astype(jnp.float32)) / (mass + 1.0)).astype(jnp.bfloat16)


def index_of(plan, place):
    return lax.axis_index("item") ^ place if plan["exchange"] else place


def open_kernel(plan, scale, c_ref, parts, *refs):
    nv, blocks = plan["nv"], plan["early"]
    pieces, refs = refs[: plan["n_early"]], refs[plan["n_early"] :]
    table, own, total, mass, done, sems, own_sem = refs
    done[...] = jnp.zeros_like(done)
    rows = own.shape[0]
    start = pl.multiple_of(lax.axis_index("item") * rows, rows)
    own_copy = pltpu.make_async_copy(c_ref.at[pl.ds(start, rows), :], own, own_sem)
    own_copy.start()
    copies = fetches(nv, blocks, pieces, table, sems)
    for block in copies:
        for copy in block:
            copy.start()
    own_copy.wait()
    for place, block in enumerate(copies):
        for copy in block:
            copy.wait()
        vectors = table[pl.ds(place * nv, nv), :]
        resp = jnp.exp(scores(own[...], vectors, scale) - parts[pl.ds(place, 1), :]).astype(jnp.bfloat16)
        term, weight = weigh(resp, vectors)
        total[...] = term if place == 0 else total[...] + term
        mass[...] = weight if place == 0 else mass[...] + weight


def close_kernel(plan, scale, early, own, total, mass, parts, *refs):
    nv, blocks, first = plan["nv"], plan["late"], len(plan["early"])
    pieces, refs = refs[: plan["n_late"]], refs[plan["n_late"] :]
    new_ref, expo_ref, peak_ref, part_ref = refs[:4]
    late = sems = None
    if blocks:
        late, sems = refs[4:]
        copies = fetches(nv, blocks, pieces, late, sems)
        for block in copies:
            for copy in block:
                copy.start()
        sums, weights = total[...], mass[...]
        for place, block in enumerate(copies):
            for copy in block:
                copy.wait()
            vectors = late[pl.ds(place * nv, nv), :]
            resp = jnp.exp(scores(own[...], vectors, scale) - parts[pl.ds(first + place, 1), :]).astype(jnp.bfloat16)
            term, weight = weigh(resp, vectors)
            sums, weights = sums + term, weights + weight
        new_ref[...] = updated(sums, weights, own[...])
    else:
        new_ref[...] = updated(total[...], mass[...], own[...])
    for place in range(first + len(blocks)):
        vectors = early[pl.ds(place * nv, nv), :] if place < first else late[pl.ds((place - first) * nv, nv), :]
        logits = scores(new_ref[...], vectors, scale)
        peak = jnp.max(logits, axis=0, keepdims=True)
        expo = jnp.exp(logits - peak)
        expo_ref[place] = expo
        peak_ref[pl.ds(place, 1), :] = peak
        part_ref[pl.ds(index_of(plan, place), 1), :] = peak + jnp.log(jnp.sum(expo, axis=0, keepdims=True))


def last_kernel(plan, old_ref, expo_ref, peak_ref, parts, *refs):
    nv = plan["nv"]
    first, second = len(plan["early"]), len(plan["late"])
    early, refs = refs[0], refs[1:]
    late = refs[0] if second else None
    new_ref, norm_ref, lse_ref, total, mass = refs[1:] if second else refs
    lse_ref[...] = merge([parts[i] for i in range(parts.shape[0])])
    norm_ref[...] = lse_ref[pl.ds(lax.axis_index("item"), 1), :].reshape(nv)
    for place in range(first + second):
        lse = lse_ref[pl.ds(index_of(plan, place), 1), :]
        vectors = early[pl.ds(place * nv, nv), :] if place < first else late[pl.ds((place - first) * nv, nv), :]
        factor = jnp.exp(peak_ref[pl.ds(place, 1), :] - lse)
        term, weight = weigh((expo_ref[place] * factor).astype(jnp.bfloat16), vectors)
        total[...] = term if place == 0 else total[...] + term
        mass[...] = weight if place == 0 else mass[...] + weight
    new_ref[...] = updated(total[...], mass[...], old_ref[...])


def send(value, items, cents, item_mask, cent_mask):
    pairs = [
        (i * cents + c, (i ^ item_mask) * cents + (c ^ cent_mask)) for i in range(items) for c in range(cents)
    ]
    return lax.ppermute(value, BOTH, pairs)


def butterfly(part, go, cents):
    mask = 1
    while mask < cents:
        part = merge([part, go(part, item_mask=0, cent_mask=mask)])
        mask *= 2
    return part


def after(value, *others):
    return lax.optimization_barrier((value, *others))[0]


def shards(vectors, centroids):
    items, cents = lax.axis_size("item"), lax.axis_size("cent")
    nv, dim = vectors.shape
    rows = centroids.shape[0] // items
    scale = BETA / math.sqrt(dim)
    go = functools.partial(send, items=items, cents=cents)
    small = items == 4 and cents == 8
    if small:
        half, quarter = nv // 2, nv // 4
        core = lax.rem(lax.axis_index("cent"), 2)
        own_half = lax.dynamic_slice_in_dim(vectors, core * half, half, 0)
        over_x, over_y = go(own_half, item_mask=1, cent_mask=0), go(own_half, item_mask=2, cent_mask=0)
        lse = butterfly(partial(vectors, centroids, scale), go, cents)
        over_x, over_y = after(over_x, lse), after(over_y, lse)
        d0 = go(over_y[:quarter], item_mask=1, cent_mask=0)
        d1 = go(over_x[quarter:], item_mask=2, cent_mask=0)
        parts = jnp.concatenate([lse, go(lse, item_mask=1, cent_mask=0)], axis=0)
        parts = jnp.concatenate([parts, go(parts, item_mask=2, cent_mask=0)], axis=0)

        def pieces_of(values, at):
            pieces, blocks = [], []
            for block in values:
                entries = []
                for s, value in enumerate(block):
                    for mine in (True, False):
                        entries.append((at + len(pieces), None, mine, s * quarter, value.shape[0]))
                        pieces.append(value if mine else go(value, item_mask=0, cent_mask=1))
                blocks.append(entries)
            return pieces, blocks

        early, early_blocks = pieces_of([[after(over_x, parts)], [after(over_y, parts)]], 1)
        early = [vectors] + early
        early_blocks = [[(0, None, None, 0, nv)]] + early_blocks
    else:
        early = [lax.all_gather(vectors, "item", axis=0, tiled=True)]
        early_blocks = [[(0, i * nv, None, 0, nv)] for i in range(items)]
        part = partial(vectors, centroids, scale)
        parts = lax.all_gather(part, "cent", axis=0, tiled=False)
        parts = lax.all_gather(merge([parts[i] for i in range(cents)]), "item", axis=0, tiled=True)
    plan = dict(nv=nv, exchange=small, early=early_blocks, n_early=len(early))

    any_spec = pl.BlockSpec(memory_space=pl.ANY)
    vmem = pl.BlockSpec(memory_space=pltpu.VMEM)
    n_early = len(early_blocks)
    flops = 2 * nv * rows * dim
    params = pltpu.CompilerParams(vmem_limit_bytes=20 * MIB)
    table, own, total, mass, done = pl.pallas_call(
        functools.partial(open_kernel, plan, scale),
        in_specs=[any_spec, vmem] + [any_spec] * len(early),
        out_specs=[vmem] * 5,
        out_shape=[
            pltpu.VMEM((n_early * nv, dim), jnp.bfloat16),
            pltpu.VMEM((rows, dim), jnp.bfloat16),
            pltpu.VMEM((rows, dim), jnp.float32),
            pltpu.VMEM((rows, 1), jnp.float32),
            jax.ShapeDtypeStruct((8, 128), jnp.float32),
        ],
        scratch_shapes=[
            pltpu.SemaphoreType.DMA((max(len(b) for b in early_blocks), n_early)),
            pltpu.SemaphoreType.DMA,
        ],
        compiler_params=params,
        cost_estimate=pl.CostEstimate(
            flops=2 * n_early * flops, bytes_accessed=2 * n_early * nv * dim, transcendentals=n_early * nv * rows
        ),
        name="early_blocks",
    )(centroids, parts, *early)

    late, late_blocks = pieces_of([[after(d0, done), after(d1, done)]], 0) if small else ([], [])
    n_late = len(late_blocks)
    plan = dict(plan, late=late_blocks, n_late=len(late))
    late_out = [pltpu.VMEM((n_late * nv, dim), jnp.bfloat16)] if n_late else []
    late_sems = [pltpu.SemaphoreType.DMA((max(len(b) for b in late_blocks), n_late))] if n_late else []
    fresh, expo, peak, part, *tables = pl.pallas_call(
        functools.partial(close_kernel, plan, scale),
        in_specs=[vmem] * 5 + [any_spec] * len(late),
        out_specs=[vmem] * (4 + len(late_out)),
        out_shape=[
            pltpu.VMEM((rows, dim), jnp.bfloat16),
            pltpu.VMEM((items, rows, nv), jnp.float32),
            pltpu.VMEM((items, nv), jnp.float32),
            pltpu.VMEM((items, nv), jnp.float32),
        ]
        + late_out,
        scratch_shapes=late_sems,
        compiler_params=params,
        cost_estimate=pl.CostEstimate(
            flops=(items + 2 * n_late) * flops,
            bytes_accessed=2 * n_late * nv * dim,
            transcendentals=(items + n_late) * nv * rows,
        ),
        name="late_blocks",
    )(in_vmem(table), in_vmem(own), in_vmem(total), in_vmem(mass), parts, *late)

    if small:
        parts = butterfly(part, go, cents)
        for mask in (1, 2):
            parts = merge([parts, go(parts, item_mask=mask, cent_mask=0)])
        parts = parts[None]
    else:
        gathered = lax.all_gather(part, "cent", axis=0, tiled=False)
        parts = lax.all_gather(merge([gathered[i] for i in range(cents)]), "item", axis=0, tiled=False)
    result, norm = pl.pallas_call(
        functools.partial(last_kernel, plan),
        in_specs=[vmem] * (5 + len(tables)),
        out_specs=[vmem] * 2,
        out_shape=[
            jax.ShapeDtypeStruct((rows, dim), jnp.bfloat16),
            jax.ShapeDtypeStruct((nv,), jnp.float32),
        ],
        scratch_shapes=[
            pltpu.VMEM((items, nv), jnp.float32),
            pltpu.VMEM((rows, dim), jnp.float32),
            pltpu.VMEM((rows, 1), jnp.float32),
        ],
        compiler_params=params,
        cost_estimate=pl.CostEstimate(flops=items * flops, bytes_accessed=2 * rows * dim, transcendentals=0),
        name="last_iteration",
    )(in_vmem(fresh), in_vmem(expo), in_vmem(peak), parts, in_vmem(table), *[in_vmem(t) for t in tables])
    return (result, norm)


def solution(mesh):
    in_specs = (P("item", None), P("cent", None))
    out_specs = (P(("cent", "item"), None), P("item"))
    return jax.shard_map(shards, mesh=mesh, in_specs=in_specs, out_specs=out_specs, check_vma=False)
```

```python
import functools
import math

import jax
import jax.numpy as jnp
from jax import lax
from jax.experimental import pallas as pl
from jax.experimental.pallas import tpu as pltpu
from jax.sharding import PartitionSpec as P

BETA = 3.0
BOTH = ("item", "cent")
MIB = 1024 * 1024
NT = (((1,), (1,)), ((), ()))
NN = (((1,), (0,)), ((), ()))


def scores(rows, vectors, scale):
    raw = lax.dot_general(rows, vectors, NT, preferred_element_type=jnp.float32)
    sqnorm = jnp.sum(jnp.square(rows.astype(jnp.float32)), axis=1, keepdims=True)
    return scale * (raw - 0.5 * sqnorm)


def merge(parts):
    peak = functools.reduce(jnp.maximum, parts)
    terms = [jnp.exp(p - peak) for p in parts]
    while len(terms) > 1:
        terms = [sum(terms[i : i + 2]) for i in range(0, len(terms), 2)]
    return peak + jnp.log(terms[0])


def in_vmem(value):
    return pltpu.with_memory_space_constraint(value, pltpu.VMEM)


def partial_kernel(scale, rows, v_ref, c_ref, out_ref):
    parts = []
    for start in range(0, c_ref.shape[0], rows):
        logits = scores(c_ref[start : start + rows, :], v_ref[...], scale)
        peak = jnp.max(logits, axis=0, keepdims=True)
        parts.append(peak + jnp.log(jnp.sum(jnp.exp(logits - peak), axis=0, keepdims=True)))
    out_ref[...] = merge(parts)


def partial(vectors, centroids, scale):
    nv, dim = vectors.shape
    k = centroids.shape[0]
    vmem = pl.BlockSpec(memory_space=pltpu.VMEM)
    return pl.pallas_call(
        functools.partial(partial_kernel, scale, min(256, k)),
        in_specs=[vmem, vmem],
        out_specs=vmem,
        out_shape=jax.ShapeDtypeStruct((1, nv), jnp.float32),
        compiler_params=pltpu.CompilerParams(vmem_limit_bytes=16 * MIB),
        cost_estimate=pl.CostEstimate(
            flops=2 * nv * k * dim, bytes_accessed=2 * (nv + k) * dim, transcendentals=nv * k
        ),
        name="partial_lse",
    )(in_vmem(vectors), in_vmem(centroids))


def core_index():
    return lax.rem(lax.axis_index("cent"), 2)


def index_of(plan, place):
    if not plan["exchange"]:
        return place
    mask = (0, 1 + core_index(), 2 - core_index(), 3)[place]
    return lax.axis_index("item") ^ mask


def local(plan, place, row):
    if not plan["exchange"] or place != 3:
        return row
    half = row.shape[1] // 2
    swapped = jnp.concatenate([row[:, half:], row[:, :half]], axis=1)
    return jnp.where(core_index() == 1, swapped, row)


def segments(block):
    offset = 0
    for operand, start, rows in block:
        yield operand, start, rows, offset
        offset += rows


def weigh(resp, vectors):
    term = lax.dot_general(resp, vectors, NN, preferred_element_type=jnp.float32)
    return term, jnp.sum(resp.astype(jnp.float32), axis=1, keepdims=True)


def updated(total, mass, old):
    return ((total + old.astype(jnp.float32)) / (mass + 1.0)).astype(jnp.bfloat16)


def absorb(blocks, first, plan, scale, own, parts, pieces, total, mass):
    for place, block in enumerate(blocks, first):
        lse = local(plan, place, parts[pl.ds(place, 1), :])
        for operand, start, rows, offset in segments(block):
            vectors = pieces[operand][pl.ds(start, rows), :]
            logits = scores(own, vectors, scale)
            resp = jnp.exp(logits - lse[:, offset : offset + rows]).astype(jnp.bfloat16)
            term, weight = weigh(resp, vectors)
            total = term if total is None else total + term
            mass = weight if mass is None else mass + weight
    return total, mass


def early_kernel(plan, scale, c_ref, parts, *refs):
    pieces, (total, mass, done) = refs[:-3], refs[-3:]
    done[...] = jnp.zeros_like(done)
    rows = total.shape[0]
    start = pl.multiple_of(lax.axis_index("item") * rows, rows)
    own = c_ref[pl.ds(start, rows), :]
    total[...], mass[...] = absorb(plan["early"], 0, plan, scale, own, parts, pieces, None, None)


def late_kernel(plan, scale, c_ref, parts, total, mass, *refs):
    pieces, (new_ref, expo_ref, peak_ref, part_ref) = refs[:-4], refs[-4:]
    rows = new_ref.shape[0]
    start = pl.multiple_of(lax.axis_index("item") * rows, rows)
    own = c_ref[pl.ds(start, rows), :]
    first = len(plan["early"])
    sums, weights = absorb(plan["late"], first, plan, scale, own, parts, pieces, total[...], mass[...])
    new_ref[...] = updated(sums, weights, own)
    for place, block in enumerate(plan["early"] + plan["late"]):
        peaks, sums = [], []
        for operand, start, count, offset in segments(block):
            logits = scores(new_ref[...], pieces[operand][pl.ds(start, count), :], scale)
            peak = jnp.max(logits, axis=0, keepdims=True)
            expo = jnp.exp(logits - peak)
            expo_ref[place, :, offset : offset + count] = expo
            peaks.append(peak)
            sums.append(jnp.sum(expo, axis=0, keepdims=True))
        peak, total_expo = jnp.concatenate(peaks, axis=1), jnp.concatenate(sums, axis=1)
        peak_ref[pl.ds(place, 1), :] = peak
        part_ref[pl.ds(index_of(plan, place), 1), :] = local(plan, place, peak + jnp.log(total_expo))


def last_kernel(plan, old_ref, expo_ref, peak_ref, parts, *refs):
    pieces, (new_ref, norm_ref, lse_ref) = refs[:-3], refs[-3:]
    lse_ref[...] = merge([parts[i] for i in range(parts.shape[0])])
    norm_ref[...] = lse_ref[pl.ds(lax.axis_index("item"), 1), :].reshape(norm_ref.shape)
    total = mass = None
    for place, block in enumerate(plan["early"] + plan["late"]):
        lse = local(plan, place, lse_ref[pl.ds(index_of(plan, place), 1), :])
        factor = jnp.exp(peak_ref[pl.ds(place, 1), :] - lse)
        resp = (expo_ref[place] * factor).astype(jnp.bfloat16)
        for operand, start, count, offset in segments(block):
            term, weight = weigh(resp[:, offset : offset + count], pieces[operand][pl.ds(start, count), :])
            total = term if total is None else total + term
            mass = weight if mass is None else mass + weight
    new_ref[...] = updated(total, mass, old_ref[...])


def send(value, items, cents, item_mask, cent_mask=0):
    masks = item_mask if isinstance(item_mask, tuple) else (item_mask, item_mask)
    pairs = [
        (i * cents + c, (i ^ masks[c % 2]) * cents + (c ^ cent_mask)) for i in range(items) for c in range(cents)
    ]
    return lax.ppermute(value, BOTH, pairs)


def merge_cent(part, go):
    part = merge([part, go(part, 0, 1)])
    return merge([part] + [go(part, 0, mask) for mask in (2, 4, 6)])


def after(value, *others):
    anywhere = pl.BlockSpec(memory_space=pl.ANY)
    return pl.pallas_call(
        lambda *refs: None,
        in_specs=[anywhere] * (1 + len(others)),
        out_specs=anywhere,
        out_shape=jax.ShapeDtypeStruct(value.shape, value.dtype),
        input_output_aliases={0: 0},
        name="after",
    )(value, *others)


def shards(vectors, centroids):
    items, cents = lax.axis_size("item"), lax.axis_size("cent")
    nv, dim = vectors.shape
    rows = centroids.shape[0] // items
    scale = BETA / math.sqrt(dim)

    def go(value, item_mask, cent_mask=0):
        return send(value, items, cents, item_mask, cent_mask)

    small = items == 4 and cents == 8
    part = partial(vectors, centroids, scale)
    if small:
        half = nv // 2
        near = go(vectors, (1, 2))
        lse = merge_cent(part, go)
        near = after(near, lse)
        give = lax.dynamic_slice_in_dim(near, core_index() * half, half, 0)
        far = go(give, (2, 1))
        parts = jnp.concatenate([lse, go(lse, (1, 2)), go(lse, (2, 1)), go(lse, 3)], axis=0)
        cross = go(near, 0, 1)
        early = [vectors, near, cross]
        early_blocks = [[(i, 0, nv)] for i in range(3)]
    else:
        early = [lax.all_gather(vectors, "item", axis=0, tiled=True)]
        early_blocks = [[(0, i * nv, nv)] for i in range(items)]
        parts = lax.all_gather(part, "cent", axis=0, tiled=False)
        parts = lax.all_gather(merge([parts[i] for i in range(cents)]), "item", axis=0, tiled=True)
    early = [in_vmem(piece) for piece in early]
    centroids = in_vmem(centroids)
    plan = dict(exchange=small, early=early_blocks)

    vmem = pl.BlockSpec(memory_space=pltpu.VMEM)
    n_early = len(early_blocks)
    flops = 2 * nv * rows * dim
    params = pltpu.CompilerParams(vmem_limit_bytes=20 * MIB)
    total, mass, done = pl.pallas_call(
        functools.partial(early_kernel, plan, scale),
        in_specs=[vmem] * (2 + len(early)),
        out_specs=[vmem] * 3,
        out_shape=[
            pltpu.VMEM((rows, dim), jnp.float32),
            pltpu.VMEM((rows, 1), jnp.float32),
            jax.ShapeDtypeStruct((8, 128), jnp.float32),
        ],
        compiler_params=params,
        cost_estimate=pl.CostEstimate(
            flops=2 * n_early * flops, bytes_accessed=2 * n_early * nv * dim, transcendentals=n_early * nv * rows
        ),
        name="early_blocks",
    )(centroids, parts, *early)

    late, late_blocks = [], []
    if small:
        far = after(far, done)
        late = [in_vmem(far), in_vmem(go(far, 0, 1))]
        late_blocks = [[(3, 0, half), (4, 0, half)]]
    plan["late"] = late_blocks
    n_late = len(late_blocks)
    pieces = early + late
    fresh, expo, peak, part = pl.pallas_call(
        functools.partial(late_kernel, plan, scale),
        in_specs=[vmem] * (4 + len(pieces)),
        out_specs=[vmem] * 4,
        out_shape=[
            pltpu.VMEM((rows, dim), jnp.bfloat16),
            pltpu.VMEM((items, rows, nv), jnp.float32),
            pltpu.VMEM((items, nv), jnp.float32),
            pltpu.VMEM((items, nv), jnp.float32),
        ],
        compiler_params=params,
        cost_estimate=pl.CostEstimate(
            flops=(items + 2 * n_late) * flops,
            bytes_accessed=2 * n_late * nv * dim,
            transcendentals=(items + n_late) * nv * rows,
        ),
        name="late_blocks",
    )(centroids, parts, in_vmem(total), in_vmem(mass), *pieces)

    if small:
        lse = merge_cent(part, go)
        parts = merge([lse] + [go(lse, mask) for mask in (1, 2, 3)])[None]
    else:
        gathered = lax.all_gather(part, "cent", axis=0, tiled=False)
        parts = lax.all_gather(merge([gathered[i] for i in range(cents)]), "item", axis=0, tiled=False)
    result, norm = pl.pallas_call(
        functools.partial(last_kernel, plan),
        in_specs=[vmem] * (4 + len(pieces)),
        out_specs=[vmem] * 2,
        out_shape=[
            jax.ShapeDtypeStruct((rows, dim), jnp.bfloat16),
            jax.ShapeDtypeStruct((nv,), jnp.float32),
        ],
        scratch_shapes=[pltpu.VMEM((items, nv), jnp.float32)],
        compiler_params=params,
        cost_estimate=pl.CostEstimate(flops=items * flops, bytes_accessed=2 * rows * dim, transcendentals=0),
        name="last_iteration",
    )(in_vmem(fresh), in_vmem(expo), in_vmem(peak), parts, *pieces)
    return (result, norm)


def solution(mesh):
    in_specs = (P("item", None), P("cent", None))
    out_specs = (P(("cent", "item"), None), P("item"))
    return jax.shard_map(shards, mesh=mesh, in_specs=in_specs, out_specs=out_specs, check_vma=False)
```

```python
import functools
import math

import jax
import jax.numpy as jnp
from jax import lax
from jax.experimental import pallas as pl
from jax.experimental.pallas import tpu as pltpu
from jax.sharding import PartitionSpec as P

BETA = 3.0
BOTH = ("item", "cent")
MIB = 1024 * 1024
NT = (((1,), (1,)), ((), ()))
NN = (((1,), (0,)), ((), ()))


def scores(rows, vectors, scale):
    raw = lax.dot_general(rows, vectors, NT, preferred_element_type=jnp.float32)
    sqnorm = jnp.sum(jnp.square(rows.astype(jnp.float32)), axis=1, keepdims=True)
    return scale * (raw - 0.5 * sqnorm)


def merge(parts):
    peak = functools.reduce(jnp.maximum, parts)
    terms = [jnp.exp(p - peak) for p in parts]
    while len(terms) > 1:
        terms = [sum(terms[i : i + 2]) for i in range(0, len(terms), 2)]
    return peak + jnp.log(terms[0])


def in_hbm(value):
    return pltpu.with_memory_space_constraint(value, pltpu.HBM)


def in_vmem(value):
    return pltpu.with_memory_space_constraint(value, pltpu.VMEM)


def partial_kernel(scale, rows, v_hbm, c_hbm, out_ref, v_ref, own_ref, c_ref, sems):
    nv, k, own = v_ref.shape[0], c_ref.shape[0], own_ref.shape[0]
    start = pl.multiple_of(lax.axis_index("item") * own, own)
    own_copy = pltpu.make_async_copy(c_hbm.at[pl.ds(start, own), :], own_ref, sems.at[0])
    third = nv // 3
    v_copies = [
        pltpu.make_async_copy(
            v_hbm.at[pl.ds(i * third, third), :], v_ref.at[pl.ds(i * third, third), :], sems.at[1 + i]
        )
        for i in range(3)
    ]
    c_copies = [
        pltpu.make_async_copy(c_hbm.at[pl.ds(i * rows, rows), :], c_ref.at[pl.ds(i * rows, rows), :], sems.at[4 + i])
        for i in range(k // rows)
    ]
    for copy in v_copies + c_copies + [own_copy]:
        copy.start()
    for copy in v_copies:
        copy.wait()
    parts = []
    for i, copy in enumerate(c_copies):
        copy.wait()
        logits = scores(c_ref[i * rows : (i + 1) * rows, :], v_ref[...], scale)
        peak = jnp.max(logits, axis=0, keepdims=True)
        parts.append(peak + jnp.log(jnp.sum(jnp.exp(logits - peak), axis=0, keepdims=True)))
    own_copy.wait()
    out_ref[...] = merge(parts)


def partial(vectors, centroids, own, scale):
    nv, dim = vectors.shape
    k = centroids.shape[0]
    rows = min(256, k)
    vmem = pl.BlockSpec(memory_space=pltpu.VMEM)
    hbm = pl.BlockSpec(memory_space=pl.ANY)
    return pl.pallas_call(
        functools.partial(partial_kernel, scale, rows),
        in_specs=[hbm, hbm],
        out_specs=[vmem] * 3,
        out_shape=[
            jax.ShapeDtypeStruct((1, nv), jnp.float32),
            pltpu.VMEM((nv, dim), jnp.bfloat16),
            pltpu.VMEM((own, dim), jnp.bfloat16),
        ],
        scratch_shapes=[pltpu.VMEM((k, dim), jnp.bfloat16), pltpu.SemaphoreType.DMA((4 + k // rows,))],
        compiler_params=pltpu.CompilerParams(vmem_limit_bytes=12 * MIB),
        cost_estimate=pl.CostEstimate(
            flops=2 * nv * k * dim, bytes_accessed=2 * (nv + k) * dim, transcendentals=nv * k
        ),
        name="partial_lse",
    )(in_hbm(vectors), in_hbm(centroids))


def core_index():
    return lax.rem(lax.axis_index("cent"), 2)


def index_of(plan, place):
    if not plan["exchange"]:
        return place
    mask = (0, 1 + core_index(), 2 - core_index(), 3)[place]
    return lax.axis_index("item") ^ mask


def fetches(nv, blocks, pieces, table, sems):
    result = []
    for place, entries in enumerate(blocks):
        copies = []
        for piece, start, mine, rows in entries:
            lead = 0 if mine is None else (core_index() if mine else 1 - core_index()) * (nv // 2)
            dst = pl.multiple_of(place * nv + lead, 64)
            src = pieces[piece].at[pl.ds(start, rows), :]
            copies.append(pltpu.make_async_copy(src, table.at[pl.ds(dst, rows), :], sems.at[len(copies), place]))
        result.append(copies)
    for copies in result:
        for copy in copies:
            copy.start()
    return result


def weigh(resp, vectors):
    term = lax.dot_general(resp, vectors, NN, preferred_element_type=jnp.float32)
    return term, jnp.sum(resp.astype(jnp.float32), axis=1, keepdims=True)


def updated(total, mass, old):
    return ((total + old.astype(jnp.float32)) / (mass + 1.0)).astype(jnp.bfloat16)


def absorb(own, vectors, lse, scale, total, mass):
    resp = jnp.exp(scores(own, vectors, scale) - lse).astype(jnp.bfloat16)
    term, weight = weigh(resp, vectors)
    return (term, weight) if total is None else (total + term, mass + weight)


def early_kernel(plan, scale, own_ref, parts, home, *refs):
    pieces, (table, total, mass, done, sems) = refs[:-5], refs[-5:]
    nv = home.shape[0]
    copies = fetches(nv, plan["early"], pieces, table, sems)
    done[...] = jnp.zeros_like(done)
    own = own_ref[...]
    sums = weights = None
    if plan["home"]:
        sums, weights = absorb(own, home[...], parts[pl.ds(0, 1), :], scale, sums, weights)
    for i, block in enumerate(copies):
        for copy in block:
            copy.wait()
        place = i + plan["home"]
        vectors = table[pl.ds(i * nv, nv), :]
        sums, weights = absorb(own, vectors, parts[pl.ds(place, 1), :], scale, sums, weights)
    total[...], mass[...] = sums, weights


def vectors_of(plan, place, home, tables):
    nv = home.shape[0]
    if place < plan["home"]:
        return home[...]
    place -= plan["home"]
    early = len(plan["early"])
    if place < early:
        return tables[0][pl.ds(place * nv, nv), :]
    return tables[1][pl.ds((place - early) * nv, nv), :]


def late_kernel(plan, scale, own_ref, parts, total, mass, home, table, *refs):
    n = plan["n_late"]
    pieces, refs = refs[:n], refs[n:]
    new_ref, expo_ref, peak_ref, part_ref = refs[:4]
    tables = [table]
    sums, weights = total[...], mass[...]
    own = own_ref[...]
    if n:
        late, sems = refs[4:]
        tables.append(late)
        copies = fetches(home.shape[0], plan["late"], pieces, late, sems)
        for i, block in enumerate(copies):
            for copy in block:
                copy.wait()
            place = plan["places"] - len(copies) + i
            vectors = vectors_of(plan, place, home, tables)
            sums, weights = absorb(own, vectors, parts[pl.ds(place, 1), :], scale, sums, weights)
    new_ref[...] = updated(sums, weights, own)
    for place in range(plan["places"]):
        logits = scores(new_ref[...], vectors_of(plan, place, home, tables), scale)
        peak = jnp.max(logits, axis=0, keepdims=True)
        expo = jnp.exp(logits - peak)
        expo_ref[place] = expo
        peak_ref[pl.ds(place, 1), :] = peak
        part_ref[pl.ds(index_of(plan, place), 1), :] = peak + jnp.log(jnp.sum(expo, axis=0, keepdims=True))


def last_kernel(plan, old_ref, expo_ref, peak_ref, parts, home, *refs):
    tables, (new_ref, norm_ref, lse_ref) = refs[:-3], refs[-3:]
    lse_ref[...] = merge([parts[i] for i in range(parts.shape[0])])
    norm_ref[...] = lse_ref[pl.ds(lax.axis_index("item"), 1), :].reshape(norm_ref.shape)
    total = mass = None
    for place in range(plan["places"]):
        factor = jnp.exp(peak_ref[pl.ds(place, 1), :] - lse_ref[pl.ds(index_of(plan, place), 1), :])
        resp = (expo_ref[place] * factor).astype(jnp.bfloat16)
        term, weight = weigh(resp, vectors_of(plan, place, home, tables))
        total = term if total is None else total + term
        mass = weight if mass is None else mass + weight
    new_ref[...] = updated(total, mass, old_ref[...])


def send(value, items, cents, item_mask, cent_mask=0):
    masks = item_mask if isinstance(item_mask, tuple) else (item_mask, item_mask)
    pairs = [
        (i * cents + c, (i ^ masks[c % 2]) * cents + (c ^ cent_mask)) for i in range(items) for c in range(cents)
    ]
    return lax.ppermute(value, BOTH, pairs)


def merge_cent(part, go):
    part = merge([part, go(part, 0, 1)])
    return merge([part] + [go(part, 0, mask) for mask in (2, 4, 6)])


def after(value, *others):
    vmem = pl.BlockSpec(memory_space=pltpu.VMEM)
    return pl.pallas_call(
        lambda *refs: None,
        in_specs=[vmem] + [pl.BlockSpec(memory_space=pl.ANY)] * len(others),
        out_specs=vmem,
        out_shape=pltpu.VMEM(value.shape, value.dtype),
        input_output_aliases={0: 0},
        name="after",
    )(in_vmem(value), *others)


def shards(vectors, centroids):
    items, cents = lax.axis_size("item"), lax.axis_size("cent")
    nv, dim = vectors.shape
    rows = centroids.shape[0] // items
    scale = BETA / math.sqrt(dim)

    def go(value, item_mask, cent_mask=0):
        return send(value, items, cents, item_mask, cent_mask)

    small = items == 4 and cents == 8
    if small:
        half = nv // 2
        core = core_index()
        first = go(lax.dynamic_slice_in_dim(vectors, core * half, half, 0), (1, 2))
        second = go(lax.dynamic_slice_in_dim(vectors, (1 - core) * half, half, 0), (1, 2))
        part, home, own = partial(vectors, centroids, rows, scale)
        lse = merge_cent(part, go)
        parts = jnp.concatenate([lse, go(lse, (1, 2)), go(lse, (2, 1)), go(lse, 3)], axis=0)
        first, second = after(first, parts), after(second, parts)
        far = go(first, (2, 1))
        early = [first, second, go(first, 0, 1), go(second, 0, 1)]
        early_blocks = [[(0, 0, True, half), (1, 0, False, half)], [(2, 0, False, half), (3, 0, True, half)]]
        plan = dict(exchange=True, home=1, places=4)
    else:
        part, home, own = partial(vectors, centroids, rows, scale)
        early = [lax.all_gather(vectors, "item", axis=0, tiled=True)]
        early_blocks = [[(0, i * nv, None, nv)] for i in range(items)]
        parts = lax.all_gather(part, "cent", axis=0, tiled=False)
        parts = lax.all_gather(merge([parts[i] for i in range(cents)]), "item", axis=0, tiled=True)
        plan = dict(exchange=False, home=0, places=items)
    plan["early"] = early_blocks

    vmem = pl.BlockSpec(memory_space=pltpu.VMEM)
    hbm = pl.BlockSpec(memory_space=pl.ANY)
    n_early = len(early_blocks)
    flops = 2 * nv * rows * dim
    params = pltpu.CompilerParams(vmem_limit_bytes=16 * MIB)
    table, total, mass, done = pl.pallas_call(
        functools.partial(early_kernel, plan, scale),
        in_specs=[vmem] * 3 + [hbm] * len(early),
        out_specs=[vmem] * 4,
        out_shape=[
            pltpu.VMEM((n_early * nv, dim), jnp.bfloat16),
            pltpu.VMEM((rows, dim), jnp.float32),
            pltpu.VMEM((rows, 1), jnp.float32),
            jax.ShapeDtypeStruct((8, 128), jnp.float32),
        ],
        scratch_shapes=[pltpu.SemaphoreType.DMA((max(len(b) for b in early_blocks), n_early))],
        compiler_params=params,
        cost_estimate=pl.CostEstimate(
            flops=2 * n_early * flops, bytes_accessed=2 * n_early * nv * dim, transcendentals=n_early * nv * rows
        ),
        name="early_blocks",
    )(in_vmem(own), parts, in_vmem(home), *early)

    late, late_blocks = [], []
    if small:
        far = after(far, done)
        late = [far, go(far, 0, 1)]
        late_blocks = [[(0, 0, True, half), (1, 0, False, half)]]
    plan["late"], plan["n_late"] = late_blocks, len(late)
    n_late = len(late_blocks)
    late_out = [pltpu.VMEM((n_late * nv, dim), jnp.bfloat16)] if n_late else []
    fresh, expo, peak, part, *tables = pl.pallas_call(
        functools.partial(late_kernel, plan, scale),
        in_specs=[vmem] * 6 + [hbm] * len(late),
        out_specs=[vmem] * (4 + len(late_out)),
        out_shape=[
            pltpu.VMEM((rows, dim), jnp.bfloat16),
            pltpu.VMEM((items, rows, nv), jnp.float32),
            pltpu.VMEM((items, nv), jnp.float32),
            pltpu.VMEM((items, nv), jnp.float32),
        ]
        + late_out,
        scratch_shapes=[pltpu.SemaphoreType.DMA((2, n_late))] if n_late else [],
        compiler_params=params,
        cost_estimate=pl.CostEstimate(
            flops=(items + 2 * n_late) * flops,
            bytes_accessed=2 * n_late * nv * dim,
            transcendentals=(items + n_late) * nv * rows,
        ),
        name="late_blocks",
    )(in_vmem(own), parts, in_vmem(total), in_vmem(mass), in_vmem(home), in_vmem(table), *late)

    if small:
        lse = merge_cent(part, go)
        parts = merge([lse] + [go(lse, mask) for mask in (1, 2, 3)])[None]
    else:
        gathered = lax.all_gather(part, "cent", axis=0, tiled=False)
        parts = lax.all_gather(merge([gathered[i] for i in range(cents)]), "item", axis=0, tiled=False)
    result, norm = pl.pallas_call(
        functools.partial(last_kernel, plan),
        in_specs=[vmem] * (6 + len(tables)),
        out_specs=[vmem] * 2,
        out_shape=[
            jax.ShapeDtypeStruct((rows, dim), jnp.bfloat16),
            jax.ShapeDtypeStruct((nv,), jnp.float32),
        ],
        scratch_shapes=[pltpu.VMEM((items, nv), jnp.float32)],
        compiler_params=params,
        cost_estimate=pl.CostEstimate(flops=items * flops, bytes_accessed=2 * rows * dim, transcendentals=0),
        name="last_iteration",
    )(in_vmem(fresh), in_vmem(expo), in_vmem(peak), parts, in_vmem(home), in_vmem(table), *[in_vmem(t) for t in tables])
    return (result, norm)


def solution(mesh):
    in_specs = (P("item", None), P("cent", None))
    out_specs = (P(("cent", "item"), None), P("item"))
    return jax.shard_map(shards, mesh=mesh, in_specs=in_specs, out_specs=out_specs, check_vma=False)
```

```python
import functools
import math

import jax
import jax.numpy as jnp
from jax import lax
from jax.experimental import pallas as pl
from jax.experimental.pallas import tpu as pltpu
from jax.sharding import PartitionSpec as P

BETA = 3.0
BOTH = ("item", "cent")
MIB = 1024 * 1024
NT = (((1,), (1,)), ((), ()))
NN = (((1,), (0,)), ((), ()))


def scores(rows, vectors, scale):
    raw = lax.dot_general(rows, vectors, NT, preferred_element_type=jnp.float32)
    sqnorm = jnp.sum(jnp.square(rows.astype(jnp.float32)), axis=1, keepdims=True)
    return scale * (raw - 0.5 * sqnorm)


def merge(parts):
    peak = functools.reduce(jnp.maximum, parts)
    terms = [jnp.exp(p - peak) for p in parts]
    while len(terms) > 1:
        terms = [sum(terms[i : i + 2]) for i in range(0, len(terms), 2)]
    return peak + jnp.log(terms[0])


def in_hbm(value):
    return pltpu.with_memory_space_constraint(value, pltpu.HBM)


def in_vmem(value):
    return pltpu.with_memory_space_constraint(value, pltpu.VMEM)


def load_kernel(v_hbm, c_hbm, v_ref, c_ref, mine_ref, other_ref, v_sems, c_sems):
    half = mine_ref.shape[0]
    v_count, c_count = v_sems.shape[0], c_sems.shape[0]
    v_rows, c_rows = v_ref.shape[0] // v_count, c_ref.shape[0] // c_count
    copies = [
        pltpu.make_async_copy(
            v_hbm.at[pl.ds(i * v_rows, v_rows), :], v_ref.at[pl.ds(i * v_rows, v_rows), :], v_sems.at[i]
        )
        for i in range(v_count)
    ] + [
        pltpu.make_async_copy(
            c_hbm.at[pl.ds(i * c_rows, c_rows), :], c_ref.at[pl.ds(i * c_rows, c_rows), :], c_sems.at[i]
        )
        for i in range(c_count)
    ]
    for copy in copies:
        copy.start()
    for copy in copies[:v_count]:
        copy.wait()
    core = core_index()
    mine_ref[...] = v_ref[pl.ds(pl.multiple_of(core * half, half), half), :]
    other_ref[...] = v_ref[pl.ds(pl.multiple_of((1 - core) * half, half), half), :]
    for copy in copies[v_count:]:
        copy.wait()


def load(vectors, centroids):
    nv, dim = vectors.shape
    k = centroids.shape[0]
    vmem = pl.BlockSpec(memory_space=pltpu.VMEM)
    hbm = pl.BlockSpec(memory_space=pl.ANY)
    return pl.pallas_call(
        load_kernel,
        in_specs=[hbm, hbm],
        out_specs=[vmem] * 4,
        out_shape=[
            pltpu.VMEM((nv, dim), jnp.bfloat16),
            pltpu.VMEM((k, dim), jnp.bfloat16),
            pltpu.VMEM((nv // 2, dim), jnp.bfloat16),
            pltpu.VMEM((nv // 2, dim), jnp.bfloat16),
        ],
        scratch_shapes=[pltpu.SemaphoreType.DMA((6,)), pltpu.SemaphoreType.DMA((8,))],
        compiler_params=pltpu.CompilerParams(vmem_limit_bytes=4 * MIB),
        cost_estimate=pl.CostEstimate(flops=0, bytes_accessed=4 * (nv + k) * dim, transcendentals=0),
        name="load",
    )(in_hbm(vectors), in_hbm(centroids))


def partial_kernel(scale, rows, v_ref, c_ref, out_ref):
    parts = []
    for start in range(0, c_ref.shape[0], rows):
        logits = scores(c_ref[start : start + rows, :], v_ref[...], scale)
        peak = jnp.max(logits, axis=0, keepdims=True)
        parts.append(peak + jnp.log(jnp.sum(jnp.exp(logits - peak), axis=0, keepdims=True)))
    out_ref[...] = merge(parts)


def partial(vectors, centroids, scale):
    nv, dim = vectors.shape
    k = centroids.shape[0]
    vmem = pl.BlockSpec(memory_space=pltpu.VMEM)
    return pl.pallas_call(
        functools.partial(partial_kernel, scale, min(256, k)),
        in_specs=[vmem, vmem],
        out_specs=vmem,
        out_shape=jax.ShapeDtypeStruct((1, nv), jnp.float32),
        compiler_params=pltpu.CompilerParams(vmem_limit_bytes=12 * MIB),
        cost_estimate=pl.CostEstimate(
            flops=2 * nv * k * dim, bytes_accessed=2 * (nv + k) * dim, transcendentals=nv * k
        ),
        name="partial_lse",
    )(in_vmem(vectors), in_vmem(centroids))


def core_index():
    return lax.rem(lax.axis_index("cent"), 2)


def index_of(plan, place):
    if not plan["exchange"]:
        return place
    mask = (0, 1 + core_index(), 2 - core_index(), 3)[place]
    return lax.axis_index("item") ^ mask


def fetches(nv, blocks, pieces, table, sems):
    result = []
    for place, entries in enumerate(blocks):
        copies = []
        for piece, start, mine, rows in entries:
            lead = 0 if mine is None else (core_index() if mine else 1 - core_index()) * (nv // 2)
            dst = pl.multiple_of(place * nv + lead, 64)
            src = pieces[piece].at[pl.ds(start, rows), :]
            copies.append(pltpu.make_async_copy(src, table.at[pl.ds(dst, rows), :], sems.at[len(copies), place]))
        result.append(copies)
    for copies in result:
        for copy in copies:
            copy.start()
    return result


def weigh(resp, vectors):
    term = lax.dot_general(resp, vectors, NN, preferred_element_type=jnp.float32)
    return term, jnp.sum(resp.astype(jnp.float32), axis=1, keepdims=True)


def updated(total, mass, old):
    return ((total + old.astype(jnp.float32)) / (mass + 1.0)).astype(jnp.bfloat16)


def absorb(own, vectors, lse, scale, total, mass):
    resp = jnp.exp(scores(own, vectors, scale) - lse).astype(jnp.bfloat16)
    term, weight = weigh(resp, vectors)
    return (term, weight) if total is None else (total + term, mass + weight)


def own_rows(c_ref, rows):
    return c_ref[pl.ds(pl.multiple_of(lax.axis_index("item") * rows, rows), rows), :]


def early_kernel(plan, scale, c_ref, home, *refs):
    n = plan["n_early"]
    parts, pieces, (table, total, mass, done, sems) = refs[:n], refs[n:-5], refs[-5:]
    nv = home.shape[0]
    copies = fetches(nv, plan["early"], pieces, table, sems)
    done[...] = jnp.zeros_like(done)
    own = own_rows(c_ref, total.shape[0])
    sums = weights = None
    if plan["home"]:
        sums, weights = absorb(own, home[...], parts[0][...], scale, sums, weights)
    for i, block in enumerate(copies):
        for copy in block:
            copy.wait()
        place = i + plan["home"]
        vectors = table[pl.ds(i * nv, nv), :]
        sums, weights = absorb(own, vectors, parts[place][...], scale, sums, weights)
    total[...], mass[...] = sums, weights


def vectors_of(plan, place, home, tables):
    nv = home.shape[0]
    if place < plan["home"]:
        return home[...]
    place -= plan["home"]
    early = len(plan["early"])
    if place < early:
        return tables[0][pl.ds(place * nv, nv), :]
    return tables[1][pl.ds((place - early) * nv, nv), :]


def late_kernel(plan, scale, c_ref, total, mass, home, table, *refs):
    n, late_places = plan["n_late"], len(plan["late"])
    parts, refs = refs[:late_places], refs[late_places:]
    pieces, refs = refs[:n], refs[n:]
    new_ref, expo_ref, peak_ref, part_ref = refs[:4]
    tables = [table]
    sums, weights = total[...], mass[...]
    own = own_rows(c_ref, new_ref.shape[0])
    if n:
        late, sems = refs[4:]
        tables.append(late)
        copies = fetches(home.shape[0], plan["late"], pieces, late, sems)
        for i, block in enumerate(copies):
            for copy in block:
                copy.wait()
            place = plan["places"] - len(copies) + i
            vectors = vectors_of(plan, place, home, tables)
            sums, weights = absorb(own, vectors, parts[i][...], scale, sums, weights)
    new_ref[...] = updated(sums, weights, own)
    for place in range(plan["places"]):
        logits = scores(new_ref[...], vectors_of(plan, place, home, tables), scale)
        peak = jnp.max(logits, axis=0, keepdims=True)
        expo = jnp.exp(logits - peak)
        expo_ref[place] = expo
        peak_ref[pl.ds(place, 1), :] = peak
        part_ref[pl.ds(index_of(plan, place), 1), :] = peak + jnp.log(jnp.sum(expo, axis=0, keepdims=True))


def last_kernel(plan, old_ref, expo_ref, peak_ref, parts, home, *refs):
    tables, (new_ref, norm_ref, lse_ref) = refs[:-3], refs[-3:]
    lse_ref[...] = merge([parts[i] for i in range(parts.shape[0])])
    norm_ref[...] = lse_ref[pl.ds(lax.axis_index("item"), 1), :].reshape(norm_ref.shape)
    total = mass = None
    for place in range(plan["places"]):
        factor = jnp.exp(peak_ref[pl.ds(place, 1), :] - lse_ref[pl.ds(index_of(plan, place), 1), :])
        resp = (expo_ref[place] * factor).astype(jnp.bfloat16)
        term, weight = weigh(resp, vectors_of(plan, place, home, tables))
        total = term if total is None else total + term
        mass = weight if mass is None else mass + weight
    new_ref[...] = updated(total, mass, old_ref[...])


def send(value, items, cents, item_mask, cent_mask=0):
    masks = item_mask if isinstance(item_mask, tuple) else (item_mask, item_mask)
    pairs = [
        (i * cents + c, (i ^ masks[c % 2]) * cents + (c ^ cent_mask)) for i in range(items) for c in range(cents)
    ]
    return lax.ppermute(value, BOTH, pairs)


def merge_cent(part, go):
    part = merge([part, go(part, 0, 1)])
    return merge([part] + [go(part, 0, mask) for mask in (2, 4, 6)])


def after(value, *others):
    vmem = pl.BlockSpec(memory_space=pltpu.VMEM)
    return pl.pallas_call(
        lambda *refs: None,
        in_specs=[vmem] + [pl.BlockSpec(memory_space=pl.ANY)] * len(others),
        out_specs=vmem,
        out_shape=pltpu.VMEM(value.shape, value.dtype),
        input_output_aliases={0: 0},
        compiler_params=pltpu.CompilerParams(vmem_limit_bytes=2 * MIB),
        name="after",
    )(in_vmem(value), *others)


def shards(vectors, centroids):
    items, cents = lax.axis_size("item"), lax.axis_size("cent")
    nv, dim = vectors.shape
    rows = centroids.shape[0] // items
    scale = BETA / math.sqrt(dim)

    def go(value, item_mask, cent_mask=0):
        return send(value, items, cents, item_mask, cent_mask)

    small = items == 4 and cents == 8
    home, centroids, mine, other = load(vectors, centroids)
    if small:
        half = nv // 2
        first, second = go(mine, (1, 2)), go(other, (1, 2))
        lse = merge_cent(partial(home, centroids, scale), go)
        parts = [lse, go(lse, (1, 2)), go(lse, (2, 1)), go(lse, 3)]
        first, second = after(first, *parts), after(second, *parts)
        far = go(first, (2, 1))
        early = [first, second, go(first, 0, 1), go(second, 0, 1)]
        early_blocks = [[(0, 0, True, half), (1, 0, False, half)], [(2, 0, False, half), (3, 0, True, half)]]
        plan = dict(exchange=True, home=1, places=4)
    else:
        early = [lax.all_gather(vectors, "item", axis=0, tiled=True)]
        early_blocks = [[(0, i * nv, None, nv)] for i in range(items)]
        part = partial(home, centroids, scale)
        parts = lax.all_gather(part, "cent", axis=0, tiled=False)
        parts = lax.all_gather(merge([parts[i] for i in range(cents)]), "item", axis=0, tiled=False)
        parts = [parts[i] for i in range(items)]
        plan = dict(exchange=False, home=0, places=items)
    plan["early"] = early_blocks
    plan["n_early"] = n_parts = plan["home"] + len(early_blocks)

    vmem = pl.BlockSpec(memory_space=pltpu.VMEM)
    hbm = pl.BlockSpec(memory_space=pl.ANY)
    n_early = len(early_blocks)
    flops = 2 * nv * rows * dim
    params = pltpu.CompilerParams(vmem_limit_bytes=16 * MIB)
    table, total, mass, done = pl.pallas_call(
        functools.partial(early_kernel, plan, scale),
        in_specs=[vmem] * (2 + n_parts) + [hbm] * len(early),
        out_specs=[vmem] * 4,
        out_shape=[
            pltpu.VMEM((n_early * nv, dim), jnp.bfloat16),
            pltpu.VMEM((rows, dim), jnp.float32),
            pltpu.VMEM((rows, 1), jnp.float32),
            jax.ShapeDtypeStruct((8, 128), jnp.float32),
        ],
        scratch_shapes=[pltpu.SemaphoreType.DMA((max(len(b) for b in early_blocks), n_early))],
        compiler_params=params,
        cost_estimate=pl.CostEstimate(
            flops=2 * n_early * flops, bytes_accessed=2 * n_early * nv * dim, transcendentals=n_early * nv * rows
        ),
        name="early_blocks",
    )(in_vmem(centroids), in_vmem(home), *parts[:n_parts], *early)

    late, late_blocks = [], []
    if small:
        far = after(far, done)
        late = [far, go(far, 0, 1)]
        late_blocks = [[(0, 0, True, half), (1, 0, False, half)]]
    plan["late"], plan["n_late"] = late_blocks, len(late)
    n_late = len(late_blocks)
    late_out = [pltpu.VMEM((n_late * nv, dim), jnp.bfloat16)] if n_late else []
    fresh, expo, peak, part, *tables = pl.pallas_call(
        functools.partial(late_kernel, plan, scale),
        in_specs=[vmem] * (5 + n_late) + [hbm] * len(late),
        out_specs=[vmem] * (4 + len(late_out)),
        out_shape=[
            pltpu.VMEM((rows, dim), jnp.bfloat16),
            pltpu.VMEM((items, rows, nv), jnp.float32),
            pltpu.VMEM((items, nv), jnp.float32),
            pltpu.VMEM((items, nv), jnp.float32),
        ]
        + late_out,
        scratch_shapes=[pltpu.SemaphoreType.DMA((2, n_late))] if n_late else [],
        compiler_params=params,
        cost_estimate=pl.CostEstimate(
            flops=(items + 2 * n_late) * flops,
            bytes_accessed=2 * n_late * nv * dim,
            transcendentals=(items + n_late) * nv * rows,
        ),
        name="late_blocks",
    )(in_vmem(centroids), in_vmem(total), in_vmem(mass), in_vmem(home), in_vmem(table), *parts[n_parts:], *late)

    if small:
        lse = merge_cent(part, go)
        parts = merge([lse] + [go(lse, mask) for mask in (1, 2, 3)])[None]
    else:
        gathered = lax.all_gather(part, "cent", axis=0, tiled=False)
        parts = lax.all_gather(merge([gathered[i] for i in range(cents)]), "item", axis=0, tiled=False)
    result, norm = pl.pallas_call(
        functools.partial(last_kernel, plan),
        in_specs=[vmem] * (6 + len(tables)),
        out_specs=[vmem] * 2,
        out_shape=[
            jax.ShapeDtypeStruct((rows, dim), jnp.bfloat16),
            jax.ShapeDtypeStruct((nv,), jnp.float32),
        ],
        scratch_shapes=[pltpu.VMEM((items, nv), jnp.float32)],
        compiler_params=params,
        cost_estimate=pl.CostEstimate(flops=items * flops, bytes_accessed=2 * rows * dim, transcendentals=0),
        name="last_iteration",
    )(in_vmem(fresh), in_vmem(expo), in_vmem(peak), parts, in_vmem(home), in_vmem(table), *[in_vmem(t) for t in tables])
    return (result, norm)


def solution(mesh):
    in_specs = (P("item", None), P("cent", None))
    out_specs = (P(("cent", "item"), None), P("item"))
    return jax.shard_map(shards, mesh=mesh, in_specs=in_specs, out_specs=out_specs, check_vma=False)
```

```python
import functools
import math

import jax
import jax.numpy as jnp
from jax import lax
from jax.experimental import pallas as pl
from jax.experimental.pallas import tpu as pltpu
from jax.sharding import PartitionSpec as P

BETA = 3.0
BOTH = ("item", "cent")
MIB = 1024 * 1024
NT = (((1,), (1,)), ((), ()))
NN = (((1,), (0,)), ((), ()))


def scores(rows, vectors, scale):
    raw = lax.dot_general(rows, vectors, NT, preferred_element_type=jnp.float32)
    sqnorm = jnp.sum(jnp.square(rows.astype(jnp.float32)), axis=1, keepdims=True)
    return scale * (raw - 0.5 * sqnorm)


def merge(parts):
    peak = functools.reduce(jnp.maximum, parts)
    terms = [jnp.exp(p - peak) for p in parts]
    while len(terms) > 1:
        terms = [sum(terms[i : i + 2]) for i in range(0, len(terms), 2)]
    return peak + jnp.log(terms[0])


def in_hbm(value):
    return pltpu.with_memory_space_constraint(value, pltpu.HBM)


def in_vmem(value):
    return pltpu.with_memory_space_constraint(value, pltpu.VMEM)


def copy_rows(pairs, sems):
    copies = [pltpu.make_async_copy(src, dst, sems.at[i]) for i, (src, dst) in enumerate(pairs)]
    for copy in copies:
        copy.start()
    for copy in copies:
        copy.wait()


def core_index():
    return lax.rem(lax.axis_index("cent"), 2)


def pair_index():
    return lax.rem(lax.axis_index("cent") // 2, 2)


def leads(nv, core):
    half, quarter = nv // 2, nv // 4
    rest = (1 - core) * half
    direct = rest + pair_index() * quarter
    swapped = rest + (1 - pair_index()) * quarter
    return [pl.multiple_of(lead, 64) for lead in (core * half, direct, swapped)]


def outgoing_kernel(v_hbm, half_ref, quarter_ref, sems):
    half_lead, direct, _ = leads(v_hbm.shape[0], core_index())
    rows = quarter_ref.shape[0]
    copy_rows(
        [
            (v_hbm.at[pl.ds(direct, rows), :], quarter_ref),
            (v_hbm.at[pl.ds(half_lead, rows), :], half_ref.at[pl.ds(0, rows), :]),
            (v_hbm.at[pl.ds(half_lead + rows, rows), :], half_ref.at[pl.ds(rows, rows), :]),
        ],
        sems,
    )


def outgoing(vectors):
    nv, dim = vectors.shape
    vmem = pl.BlockSpec(memory_space=pltpu.VMEM)
    return pl.pallas_call(
        outgoing_kernel,
        in_specs=[pl.BlockSpec(memory_space=pl.ANY)],
        out_specs=[vmem] * 2,
        out_shape=[pltpu.VMEM((nv // 2, dim), jnp.bfloat16), pltpu.VMEM((nv // 4, dim), jnp.bfloat16)],
        scratch_shapes=[pltpu.SemaphoreType.DMA((3,))],
        compiler_params=pltpu.CompilerParams(vmem_limit_bytes=2 * MIB),
        cost_estimate=pl.CostEstimate(flops=0, bytes_accessed=2 * nv * dim, transcendentals=0),
        name="outgoing",
    )(in_hbm(vectors))


def load_kernel(v_hbm, c_hbm, v_ref, c_ref, sems):
    pairs = []
    for src, dst, count in ((v_hbm, v_ref, 6), (c_hbm, c_ref, 8)):
        rows = dst.shape[0] // count
        pairs += [(src.at[pl.ds(i * rows, rows), :], dst.at[pl.ds(i * rows, rows), :]) for i in range(count)]
    copy_rows(pairs, sems)


def load(vectors, centroids):
    vmem = pl.BlockSpec(memory_space=pltpu.VMEM)
    hbm = pl.BlockSpec(memory_space=pl.ANY)
    return pl.pallas_call(
        load_kernel,
        in_specs=[hbm, hbm],
        out_specs=[vmem] * 2,
        out_shape=[pltpu.VMEM(vectors.shape, jnp.bfloat16), pltpu.VMEM(centroids.shape, jnp.bfloat16)],
        scratch_shapes=[pltpu.SemaphoreType.DMA((14,))],
        compiler_params=pltpu.CompilerParams(vmem_limit_bytes=2 * MIB),
        cost_estimate=pl.CostEstimate(
            flops=0, bytes_accessed=4 * (vectors.size + centroids.size), transcendentals=0
        ),
        name="load",
    )(in_hbm(vectors), in_hbm(centroids))


def partial_kernel(scale, rows, v_ref, c_ref, out_ref):
    parts = []
    for start in range(0, c_ref.shape[0], rows):
        logits = scores(c_ref[start : start + rows, :], v_ref[...], scale)
        peak = jnp.max(logits, axis=0, keepdims=True)
        parts.append(peak + jnp.log(jnp.sum(jnp.exp(logits - peak), axis=0, keepdims=True)))
    part = merge(parts)
    for i in range(out_ref.shape[0]):
        out_ref[i] = part


def partial(vectors, centroids, scale, copies):
    nv, dim = vectors.shape
    k = centroids.shape[0]
    vmem = pl.BlockSpec(memory_space=pltpu.VMEM)
    return pl.pallas_call(
        functools.partial(partial_kernel, scale, min(256, k)),
        in_specs=[vmem, vmem],
        out_specs=vmem,
        out_shape=jax.ShapeDtypeStruct((copies, 1, nv), jnp.float32),
        compiler_params=pltpu.CompilerParams(vmem_limit_bytes=12 * MIB),
        cost_estimate=pl.CostEstimate(
            flops=2 * nv * k * dim, bytes_accessed=2 * (nv + k) * dim, transcendentals=nv * k
        ),
        name="partial_lse",
    )(in_vmem(vectors), in_vmem(centroids))


def index_of(plan, place):
    if not plan["exchange"]:
        return place
    mask = (0, 1 + core_index(), 2 - core_index(), 3)[place]
    return lax.axis_index("item") ^ mask


def row_lse(plan, parts, place):
    n = plan["cents"]
    first = index_of(plan, place) * n
    return merge([parts[first + i] for i in range(n)])


def weigh(resp, vectors):
    term = lax.dot_general(resp, vectors, NN, preferred_element_type=jnp.float32)
    return term, jnp.sum(resp.astype(jnp.float32), axis=1, keepdims=True)


def updated(total, mass, old):
    return ((total + old.astype(jnp.float32)) / (mass + 1.0)).astype(jnp.bfloat16)


def own_rows(c_ref, rows):
    return c_ref[pl.ds(pl.multiple_of(lax.axis_index("item") * rows, rows), rows), :]


def absorb(own, vectors, lse, scale, total, mass):
    resp = jnp.exp(scores(own, vectors, scale) - lse).astype(jnp.bfloat16)
    term, weight = weigh(resp, vectors)
    return (term, weight) if total is None else (total + term, mass + weight)


def own_rows(c_ref, rows):
    return c_ref[pl.ds(pl.multiple_of(lax.axis_index("item") * rows, rows), rows), :]


def early_kernel(plan, scale, c_ref, parts, *refs):
    n = plan["pieces"]
    pieces, arrived, outs = refs[:n], refs[n : n + plan["arrived"]], refs[n + plan["arrived"] :]
    total, mass, done = outs[:3]
    done[...] = jnp.zeros_like(done)
    own = own_rows(c_ref, total.shape[0])
    if arrived:
        table, nv = outs[3], plan["nv"]
        core = core_index()
        half_lead, direct, swapped = leads(nv, core)
        places = [half_lead, direct, swapped]
        half_lead, direct, swapped = leads(nv, 1 - core)
        places += [nv + half_lead, nv + half_lead + nv // 4, nv + direct, nv + swapped]
        for lead, ref in zip(places, arrived):
            table[pl.ds(pl.multiple_of(lead, 64), ref.shape[0]), :] = ref[...]
        pieces += (table,)
    sums = weights = None
    for place in range(plan["early"]):
        vectors = vectors_of(plan, place, pieces)
        sums, weights = absorb(own, vectors, row_lse(plan, parts, place), scale, sums, weights)
    total[...], mass[...] = sums, weights


def vectors_of(plan, place, pieces):
    operand, start = plan["blocks"][place]
    return pieces[operand][pl.ds(start, plan["nv"]), :]


def late_kernel(plan, scale, c_ref, parts, total, mass, *refs):
    n, early = plan["pieces"], plan["early"]
    pieces, refs = refs[:n], refs[n:]
    sums, weights = total[...], mass[...]
    if early < plan["places"]:
        mine, other, new_ref, expo_ref, peak_ref, part_ref, block = refs
        pieces += (block,)
        half = mine.shape[0]
        block[pl.ds(pl.multiple_of(core_index() * half, half), half), :] = mine[...]
        block[pl.ds(pl.multiple_of((1 - core_index()) * half, half), half), :] = other[...]
    else:
        new_ref, expo_ref, peak_ref, part_ref = refs
    own = own_rows(c_ref, new_ref.shape[0])
    for place in range(early, plan["places"]):
        vectors = vectors_of(plan, place, pieces)
        sums, weights = absorb(own, vectors, row_lse(plan, parts, place), scale, sums, weights)
    new_ref[...] = updated(sums, weights, own)
    for place in range(plan["places"]):
        logits = scores(new_ref[...], vectors_of(plan, place, pieces), scale)
        peak = jnp.max(logits, axis=0, keepdims=True)
        expo = jnp.exp(logits - peak)
        expo_ref[place] = expo
        peak_ref[pl.ds(place, 1), :] = peak
        part_ref[pl.ds(index_of(plan, place), 1), :] = peak + jnp.log(jnp.sum(expo, axis=0, keepdims=True))


def last_kernel(plan, old_ref, expo_ref, peak_ref, parts, *refs):
    pieces, (new_ref, norm_ref, lse_ref) = refs[:-3], refs[-3:]
    lse_ref[...] = merge([parts[i] for i in range(parts.shape[0])])
    norm_ref[...] = lse_ref[pl.ds(lax.axis_index("item"), 1), :].reshape(norm_ref.shape)
    total = mass = None
    for place in range(plan["places"]):
        factor = jnp.exp(peak_ref[pl.ds(place, 1), :] - lse_ref[pl.ds(index_of(plan, place), 1), :])
        resp = (expo_ref[place] * factor).astype(jnp.bfloat16)
        term, weight = weigh(resp, vectors_of(plan, place, pieces))
        total = term if total is None else total + term
        mass = weight if mass is None else mass + weight
    new_ref[...] = updated(total, mass, old_ref[...])


def send(value, items, cents, item_mask, cent_mask=0):
    masks = item_mask if isinstance(item_mask, tuple) else (item_mask, item_mask)
    pairs = [
        (i * cents + c, (i ^ masks[c % 2]) * cents + (c ^ cent_mask)) for i in range(items) for c in range(cents)
    ]
    return lax.ppermute(value, BOTH, pairs)


def merge_cent(part, go):
    part = merge([part, go(part, 0, 1)])
    return merge([part] + [go(part, 0, mask) for mask in (2, 4, 6)])


def after(value, *others):
    vmem = pl.BlockSpec(memory_space=pltpu.VMEM)
    return pl.pallas_call(
        lambda *refs: None,
        in_specs=[vmem] + [pl.BlockSpec(memory_space=pl.ANY)] * len(others),
        out_specs=vmem,
        out_shape=pltpu.VMEM(value.shape, value.dtype),
        input_output_aliases={0: 0},
        compiler_params=pltpu.CompilerParams(vmem_limit_bytes=2 * MIB),
        name="after",
    )(in_vmem(value), *others)


def shards(vectors, centroids):
    items, cents = lax.axis_size("item"), lax.axis_size("cent")
    nv, dim = vectors.shape
    rows = centroids.shape[0] // items
    scale = BETA / math.sqrt(dim)

    def go(value, item_mask, cent_mask=0):
        return send(value, items, cents, item_mask, cent_mask)

    small = items == 4 and cents == 8
    if small:
        half, quarter = outgoing(vectors)
        near_quarter, near_half = go(quarter, (1, 2)), go(half, (1, 2))
        home, centroids = load(vectors, centroids)
        part = partial(home, centroids, scale, items * cents)
        parts = lax.all_to_all(part, BOTH, 0, 0, tiled=True)
        near_quarter, near_half = after(near_quarter, part), after(near_half, part)
        swapped = go(near_quarter, 0, 2)
        far = go(near_half, (2, 1))
        over = [near_half[: nv // 4], near_half[nv // 4 :], near_quarter, swapped]
        near = [near_half, near_quarter, swapped] + [go(piece, 0, 1) for piece in over]
        pieces = [home]
        plan = dict(exchange=True, cents=cents, early=3, blocks=[(0, 0), (1, 0), (1, nv), (2, 0)])
    else:
        home, centroids = load(vectors, centroids)
        parts = lax.all_gather(partial(home, centroids, scale, 1)[0], "cent", axis=0, tiled=False)
        parts = merge([parts[i] for i in range(cents)])
        parts = lax.all_gather(parts, "item", axis=0, tiled=False)
        pieces = [lax.all_gather(vectors, "item", axis=0, tiled=True)]
        near = []
        plan = dict(exchange=False, cents=1, early=items, blocks=[(0, i * nv) for i in range(items)])
    plan.update(nv=nv, places=items, pieces=len(pieces), arrived=len(near))
    pieces = [in_vmem(piece) for piece in pieces]
    centroids = in_vmem(centroids)

    vmem = pl.BlockSpec(memory_space=pltpu.VMEM)
    flops = 2 * nv * rows * dim
    early, late = plan["early"], items - plan["early"]
    params = pltpu.CompilerParams(vmem_limit_bytes=16 * MIB)
    tables = [pltpu.VMEM((2 * nv, dim), jnp.bfloat16)] if near else []
    total, mass, done, *table = pl.pallas_call(
        functools.partial(early_kernel, dict(plan), scale),
        in_specs=[vmem] * (2 + len(pieces) + len(near)),
        out_specs=[vmem] * (3 + len(tables)),
        out_shape=[
            pltpu.VMEM((rows, dim), jnp.float32),
            pltpu.VMEM((rows, 1), jnp.float32),
            jax.ShapeDtypeStruct((8, 128), jnp.float32),
        ]
        + tables,
        compiler_params=params,
        cost_estimate=pl.CostEstimate(flops=0, bytes_accessed=0, transcendentals=0),
        name="early_blocks",
    )(centroids, parts, *pieces, *[in_vmem(piece) for piece in near])
    pieces += [in_vmem(piece) for piece in table]
    plan["pieces"] = len(pieces)

    arrived = []
    if late:
        far = after(far, done)
        arrived = [in_vmem(far), in_vmem(go(far, 0, 1))]
    fresh, expo, peak, part, *block = pl.pallas_call(
        functools.partial(late_kernel, dict(plan), scale),
        in_specs=[vmem] * (4 + len(pieces) + len(arrived)),
        out_specs=[vmem] * (4 + late),
        out_shape=[
            pltpu.VMEM((rows, dim), jnp.bfloat16),
            pltpu.VMEM((items, rows, nv), jnp.float32),
            pltpu.VMEM((items, nv), jnp.float32),
            pltpu.VMEM((items, nv), jnp.float32),
        ]
        + [pltpu.VMEM((nv, dim), jnp.bfloat16)] * late,
        compiler_params=params,
        cost_estimate=pl.CostEstimate(
            flops=(items + 2 * late) * flops,
            bytes_accessed=2 * late * nv * dim,
            transcendentals=(items + late) * nv * rows,
        ),
        name="late_blocks",
    )(centroids, parts, in_vmem(total), in_vmem(mass), *pieces, *arrived)
    pieces += [in_vmem(piece) for piece in block]

    if small:
        lse = merge_cent(part, go)
        parts = merge([lse] + [go(lse, mask) for mask in (1, 2, 3)])[None]
    else:
        gathered = lax.all_gather(part, "cent", axis=0, tiled=False)
        parts = lax.all_gather(merge([gathered[i] for i in range(cents)]), "item", axis=0, tiled=False)
    result, norm = pl.pallas_call(
        functools.partial(last_kernel, dict(plan)),
        in_specs=[vmem] * (4 + len(pieces)),
        out_specs=[vmem] * 2,
        out_shape=[
            jax.ShapeDtypeStruct((rows, dim), jnp.bfloat16),
            jax.ShapeDtypeStruct((nv,), jnp.float32),
        ],
        scratch_shapes=[pltpu.VMEM((items, nv), jnp.float32)],
        compiler_params=params,
        cost_estimate=pl.CostEstimate(flops=items * flops, bytes_accessed=2 * rows * dim, transcendentals=0),
        name="last_iteration",
    )(in_vmem(fresh), in_vmem(expo), in_vmem(peak), parts, *pieces)
    return (result, norm)


def solution(mesh):
    in_specs = (P("item", None), P("cent", None))
    out_specs = (P(("cent", "item"), None), P("item"))
    return jax.shard_map(shards, mesh=mesh, in_specs=in_specs, out_specs=out_specs, check_vma=False)
```

```python
import functools
import math

import jax
import jax.numpy as jnp
from jax import lax
from jax.experimental import pallas as pl
from jax.experimental.pallas import tpu as pltpu
from jax.sharding import PartitionSpec as P

BETA = 3.0
BOTH = ("item", "cent")
MIB = 1024 * 1024
NT = (((1,), (1,)), ((), ()))
NN = (((1,), (0,)), ((), ()))


def scores(rows, vectors, scale):
    raw = lax.dot_general(rows, vectors, NT, preferred_element_type=jnp.float32)
    sqnorm = jnp.sum(jnp.square(rows.astype(jnp.float32)), axis=1, keepdims=True)
    return scale * (raw - 0.5 * sqnorm)


def merge(parts):
    peak = functools.reduce(jnp.maximum, parts)
    terms = [jnp.exp(p - peak) for p in parts]
    while len(terms) > 1:
        terms = [sum(terms[i : i + 2]) for i in range(0, len(terms), 2)]
    return peak + jnp.log(terms[0])


def in_hbm(value):
    return pltpu.with_memory_space_constraint(value, pltpu.HBM)


def in_vmem(value):
    return pltpu.with_memory_space_constraint(value, pltpu.VMEM)


def copy_rows(pairs, sems):
    copies = [pltpu.make_async_copy(src, dst, sems.at[i]) for i, (src, dst) in enumerate(pairs)]
    for copy in copies:
        copy.start()
    for copy in copies:
        copy.wait()


def core_index():
    return lax.rem(lax.axis_index("cent"), 2)


def pair_index():
    return lax.rem(lax.axis_index("cent") // 2, 2)


def leads(nv, core):
    half, quarter = nv // 2, nv // 4
    rest = (1 - core) * half
    direct = rest + pair_index() * quarter
    swapped = rest + (1 - pair_index()) * quarter
    return [pl.multiple_of(lead, 64) for lead in (core * half, direct, swapped)]


def outgoing_kernel(v_hbm, half_ref, quarter_ref, sems):
    half_lead, direct, _ = leads(v_hbm.shape[0], core_index())
    rows = quarter_ref.shape[0]
    copy_rows(
        [
            (v_hbm.at[pl.ds(direct, rows), :], quarter_ref),
            (v_hbm.at[pl.ds(half_lead, rows), :], half_ref.at[pl.ds(0, rows), :]),
            (v_hbm.at[pl.ds(half_lead + rows, rows), :], half_ref.at[pl.ds(rows, rows), :]),
        ],
        sems,
    )


def outgoing(vectors):
    nv, dim = vectors.shape
    vmem = pl.BlockSpec(memory_space=pltpu.VMEM)
    return pl.pallas_call(
        outgoing_kernel,
        in_specs=[pl.BlockSpec(memory_space=pl.ANY)],
        out_specs=[vmem] * 2,
        out_shape=[pltpu.VMEM((nv // 2, dim), jnp.bfloat16), pltpu.VMEM((nv // 4, dim), jnp.bfloat16)],
        scratch_shapes=[pltpu.SemaphoreType.DMA((3,))],
        compiler_params=pltpu.CompilerParams(vmem_limit_bytes=2 * MIB),
        cost_estimate=pl.CostEstimate(flops=0, bytes_accessed=2 * nv * dim, transcendentals=0),
        name="outgoing",
    )(in_hbm(vectors))


def load_kernel(v_hbm, c_hbm, v_ref, c_ref, sems):
    pairs = []
    for src, dst, count in ((v_hbm, v_ref, 6), (c_hbm, c_ref, 8)):
        rows = dst.shape[0] // count
        pairs += [(src.at[pl.ds(i * rows, rows), :], dst.at[pl.ds(i * rows, rows), :]) for i in range(count)]
    copy_rows(pairs, sems)


def load(vectors, centroids):
    vmem = pl.BlockSpec(memory_space=pltpu.VMEM)
    hbm = pl.BlockSpec(memory_space=pl.ANY)
    return pl.pallas_call(
        load_kernel,
        in_specs=[hbm, hbm],
        out_specs=[vmem] * 2,
        out_shape=[pltpu.VMEM(vectors.shape, jnp.bfloat16), pltpu.VMEM(centroids.shape, jnp.bfloat16)],
        scratch_shapes=[pltpu.SemaphoreType.DMA((14,))],
        compiler_params=pltpu.CompilerParams(vmem_limit_bytes=2 * MIB),
        cost_estimate=pl.CostEstimate(
            flops=0, bytes_accessed=4 * (vectors.size + centroids.size), transcendentals=0
        ),
        name="load",
    )(in_hbm(vectors), in_hbm(centroids))


def partial_kernel(scale, rows, v_ref, c_ref, out_ref):
    parts = []
    for start in range(0, c_ref.shape[0], rows):
        logits = scores(c_ref[start : start + rows, :], v_ref[...], scale)
        peak = jnp.max(logits, axis=0, keepdims=True)
        parts.append(peak + jnp.log(jnp.sum(jnp.exp(logits - peak), axis=0, keepdims=True)))
    out_ref[...] = merge(parts)


def partial(vectors, centroids, scale):
    nv, dim = vectors.shape
    k = centroids.shape[0]
    vmem = pl.BlockSpec(memory_space=pltpu.VMEM)
    return pl.pallas_call(
        functools.partial(partial_kernel, scale, min(256, k)),
        in_specs=[vmem, vmem],
        out_specs=vmem,
        out_shape=jax.ShapeDtypeStruct((1, nv), jnp.float32),
        compiler_params=pltpu.CompilerParams(vmem_limit_bytes=12 * MIB),
        cost_estimate=pl.CostEstimate(
            flops=2 * nv * k * dim, bytes_accessed=2 * (nv + k) * dim, transcendentals=nv * k
        ),
        name="partial_lse",
    )(in_vmem(vectors), in_vmem(centroids))


def index_of(plan, place):
    if not plan["exchange"]:
        return place
    mask = (0, 1 + core_index(), 2 - core_index(), 3)[place]
    return lax.axis_index("item") ^ mask


def weigh(resp, vectors):
    term = lax.dot_general(resp, vectors, NN, preferred_element_type=jnp.float32)
    return term, jnp.sum(resp.astype(jnp.float32), axis=1, keepdims=True)


def updated(total, mass, old):
    return ((total + old.astype(jnp.float32)) / (mass + 1.0)).astype(jnp.bfloat16)


def own_rows(c_ref, rows):
    return c_ref[pl.ds(pl.multiple_of(lax.axis_index("item") * rows, rows), rows), :]


def absorb(own, vectors, lse, scale, total, mass):
    resp = jnp.exp(scores(own, vectors, scale) - lse).astype(jnp.bfloat16)
    term, weight = weigh(resp, vectors)
    return (term, weight) if total is None else (total + term, mass + weight)


def own_rows(c_ref, rows):
    return c_ref[pl.ds(pl.multiple_of(lax.axis_index("item") * rows, rows), rows), :]


def early_kernel(plan, scale, c_ref, *refs):
    n = plan["pieces"]
    rows, refs = refs[: plan["early"]], refs[plan["early"] :]
    pieces, arrived, outs = refs[:n], refs[n : n + plan["arrived"]], refs[n + plan["arrived"] :]
    total, mass = outs[:2]
    own = own_rows(c_ref, total.shape[0])
    if arrived:
        table, nv = outs[2], plan["nv"]
        core = core_index()
        half_lead, direct, swapped = leads(nv, core)
        places = [half_lead, direct, swapped]
        half_lead, direct, swapped = leads(nv, 1 - core)
        places += [nv + half_lead, nv + half_lead + nv // 4, nv + direct, nv + swapped]
        for lead, ref in zip(places, arrived):
            table[pl.ds(pl.multiple_of(lead, 64), ref.shape[0]), :] = ref[...]
        pieces += (table,)
    sums = weights = None
    for place in range(plan["early"]):
        vectors = vectors_of(plan, place, pieces)
        sums, weights = absorb(own, vectors, rows[place][...], scale, sums, weights)
    total[...], mass[...] = sums, weights


def vectors_of(plan, place, pieces):
    operand, start = plan["blocks"][place]
    return pieces[operand][pl.ds(start, plan["nv"]), :]


def late_kernel(plan, scale, c_ref, total, mass, *refs):
    n, early = plan["pieces"], plan["early"]
    rows, refs = refs[: plan["places"] - early], refs[plan["places"] - early :]
    pieces, refs = refs[:n], refs[n:]
    sums, weights = total[...], mass[...]
    if early < plan["places"]:
        mine, other, new_ref, expo_ref, peak_ref, part_ref, block = refs
        pieces += (block,)
        half = mine.shape[0]
        block[pl.ds(pl.multiple_of(core_index() * half, half), half), :] = mine[...]
        block[pl.ds(pl.multiple_of((1 - core_index()) * half, half), half), :] = other[...]
    else:
        new_ref, expo_ref, peak_ref, part_ref = refs
    own = own_rows(c_ref, new_ref.shape[0])
    for place in range(early, plan["places"]):
        vectors = vectors_of(plan, place, pieces)
        sums, weights = absorb(own, vectors, rows[place - early][...], scale, sums, weights)
    new_ref[...] = updated(sums, weights, own)
    for place in range(plan["places"]):
        logits = scores(new_ref[...], vectors_of(plan, place, pieces), scale)
        peak = jnp.max(logits, axis=0, keepdims=True)
        expo = jnp.exp(logits - peak)
        expo_ref[place] = expo
        peak_ref[pl.ds(place, 1), :] = peak
        part_ref[pl.ds(index_of(plan, place), 1), :] = peak + jnp.log(jnp.sum(expo, axis=0, keepdims=True))


def last_kernel(plan, old_ref, expo_ref, peak_ref, parts, *refs):
    pieces, (new_ref, norm_ref, lse_ref) = refs[:-3], refs[-3:]
    lse_ref[...] = merge([parts[i] for i in range(parts.shape[0])])
    norm_ref[...] = lse_ref[pl.ds(lax.axis_index("item"), 1), :].reshape(norm_ref.shape)
    total = mass = None
    for place in range(plan["places"]):
        factor = jnp.exp(peak_ref[pl.ds(place, 1), :] - lse_ref[pl.ds(index_of(plan, place), 1), :])
        resp = (expo_ref[place] * factor).astype(jnp.bfloat16)
        term, weight = weigh(resp, vectors_of(plan, place, pieces))
        total = term if total is None else total + term
        mass = weight if mass is None else mass + weight
    new_ref[...] = updated(total, mass, old_ref[...])


def send(value, items, cents, item_mask, cent_mask=0):
    masks = item_mask if isinstance(item_mask, tuple) else (item_mask, item_mask)
    pairs = [
        (i * cents + c, (i ^ masks[c % 2]) * cents + (c ^ cent_mask)) for i in range(items) for c in range(cents)
    ]
    return lax.ppermute(value, BOTH, pairs)


def merge_cent(part, go):
    part = merge([part, go(part, 0, 1)])
    return merge([part] + [go(part, 0, mask) for mask in (2, 4, 6)])


def after(value, *others):
    vmem = pl.BlockSpec(memory_space=pltpu.VMEM)
    return pl.pallas_call(
        lambda *refs: None,
        in_specs=[vmem] + [pl.BlockSpec(memory_space=pl.ANY)] * len(others),
        out_specs=vmem,
        out_shape=pltpu.VMEM(value.shape, value.dtype),
        input_output_aliases={0: 0},
        compiler_params=pltpu.CompilerParams(vmem_limit_bytes=2 * MIB),
        name="after",
    )(in_vmem(value), *others)


def shards(vectors, centroids):
    items, cents = lax.axis_size("item"), lax.axis_size("cent")
    nv, dim = vectors.shape
    rows = centroids.shape[0] // items
    scale = BETA / math.sqrt(dim)

    def go(value, item_mask, cent_mask=0):
        return send(value, items, cents, item_mask, cent_mask)

    small = items == 4 and cents == 8
    if small:
        half, quarter = outgoing(vectors)
        near_quarter, near_half = go(quarter, (1, 2)), go(half, (1, 2))
        home, centroids = load(vectors, centroids)
        lse = merge_cent(partial(home, centroids, scale), go)
        parts = [lse, go(lse, (1, 2)), go(lse, (2, 1)), go(lse, 3)]
        near_quarter, near_half = after(near_quarter, lse), after(near_half, lse)
        swapped = go(near_quarter, 0, 2)
        far = go(near_half, (2, 1))
        over = [near_half[: nv // 4], near_half[nv // 4 :], near_quarter, swapped]
        near = [near_half, near_quarter, swapped] + [go(piece, 0, 1) for piece in over]
        pieces = [home]
        plan = dict(exchange=True, early=3, blocks=[(0, 0), (1, 0), (1, nv), (2, 0)])
    else:
        home, centroids = load(vectors, centroids)
        parts = lax.all_gather(partial(home, centroids, scale), "cent", axis=0, tiled=False)
        parts = merge([parts[i] for i in range(cents)])
        parts = lax.all_gather(parts, "item", axis=0, tiled=False)
        parts = [parts[i] for i in range(items)]
        pieces = [lax.all_gather(vectors, "item", axis=0, tiled=True)]
        near = []
        plan = dict(exchange=False, early=items, blocks=[(0, i * nv) for i in range(items)])
    plan.update(nv=nv, places=items, pieces=len(pieces), arrived=len(near))
    pieces = [in_vmem(piece) for piece in pieces]
    centroids = in_vmem(centroids)

    vmem = pl.BlockSpec(memory_space=pltpu.VMEM)
    flops = 2 * nv * rows * dim
    early, late = plan["early"], items - plan["early"]
    params = pltpu.CompilerParams(vmem_limit_bytes=16 * MIB)
    tables = [pltpu.VMEM((2 * nv, dim), jnp.bfloat16)] if near else []
    total, mass, *table = pl.pallas_call(
        functools.partial(early_kernel, dict(plan), scale),
        in_specs=[vmem] * (1 + early + len(pieces) + len(near)),
        out_specs=[vmem] * (2 + len(tables)),
        out_shape=[
            pltpu.VMEM((rows, dim), jnp.float32),
            pltpu.VMEM((rows, 1), jnp.float32),
        ]
        + tables,
        compiler_params=params,
        cost_estimate=pl.CostEstimate(flops=0, bytes_accessed=0, transcendentals=0),
        name="early_blocks",
    )(centroids, *parts[:early], *pieces, *[in_vmem(piece) for piece in near])
    pieces += [in_vmem(piece) for piece in table]
    plan["pieces"] = len(pieces)

    arrived = []
    if late:
        far = after(far, *parts[1:], *near[3:])
        arrived = [in_vmem(far), in_vmem(go(far, 0, 1))]
    fresh, expo, peak, part, *block = pl.pallas_call(
        functools.partial(late_kernel, dict(plan), scale),
        in_specs=[vmem] * (3 + late + len(pieces) + len(arrived)),
        out_specs=[vmem] * (4 + late),
        out_shape=[
            pltpu.VMEM((rows, dim), jnp.bfloat16),
            pltpu.VMEM((items, rows, nv), jnp.float32),
            pltpu.VMEM((items, nv), jnp.float32),
            pltpu.VMEM((items, nv), jnp.float32),
        ]
        + [pltpu.VMEM((nv, dim), jnp.bfloat16)] * late,
        compiler_params=params,
        cost_estimate=pl.CostEstimate(
            flops=(items + 2 * late) * flops,
            bytes_accessed=2 * late * nv * dim,
            transcendentals=(items + late) * nv * rows,
        ),
        name="late_blocks",
    )(centroids, in_vmem(total), in_vmem(mass), *parts[early:], *pieces, *arrived)
    pieces += [in_vmem(piece) for piece in block]

    if small:
        lse = merge_cent(part, go)
        parts = merge([lse] + [go(lse, mask) for mask in (1, 2, 3)])[None]
    else:
        gathered = lax.all_gather(part, "cent", axis=0, tiled=False)
        parts = lax.all_gather(merge([gathered[i] for i in range(cents)]), "item", axis=0, tiled=False)
    result, norm = pl.pallas_call(
        functools.partial(last_kernel, dict(plan)),
        in_specs=[vmem] * (4 + len(pieces)),
        out_specs=[vmem] * 2,
        out_shape=[
            jax.ShapeDtypeStruct((rows, dim), jnp.bfloat16),
            jax.ShapeDtypeStruct((nv,), jnp.float32),
        ],
        scratch_shapes=[pltpu.VMEM((items, nv), jnp.float32)],
        compiler_params=params,
        cost_estimate=pl.CostEstimate(flops=items * flops, bytes_accessed=2 * rows * dim, transcendentals=0),
        name="last_iteration",
    )(in_vmem(fresh), in_vmem(expo), in_vmem(peak), parts, *pieces)
    return (result, norm)


def solution(mesh):
    in_specs = (P("item", None), P("cent", None))
    out_specs = (P(("cent", "item"), None), P("item"))
    return jax.shard_map(shards, mesh=mesh, in_specs=in_specs, out_specs=out_specs, check_vma=False)
```

```python
import functools
import math

import jax
import jax.numpy as jnp
from jax import lax
from jax.experimental import pallas as pl
from jax.experimental.pallas import tpu as pltpu
from jax.sharding import PartitionSpec as P

BETA = 3.0
BOTH = ("item", "cent")
MIB = 1024 * 1024
NT = (((1,), (1,)), ((), ()))
NN = (((1,), (0,)), ((), ()))


def scores(rows, vectors, scale):
    raw = lax.dot_general(rows, vectors, NT, preferred_element_type=jnp.float32)
    sqnorm = jnp.sum(jnp.square(rows.astype(jnp.float32)), axis=1, keepdims=True)
    return scale * (raw - 0.5 * sqnorm)


def merge(parts):
    peak = functools.reduce(jnp.maximum, parts)
    terms = [jnp.exp(p - peak) for p in parts]
    while len(terms) > 1:
        terms = [sum(terms[i : i + 2]) for i in range(0, len(terms), 2)]
    return peak + jnp.log(terms[0])


def in_hbm(value):
    return pltpu.with_memory_space_constraint(value, pltpu.HBM)


def in_vmem(value):
    return pltpu.with_memory_space_constraint(value, pltpu.VMEM)


def copy_rows(pairs, sems):
    copies = [pltpu.make_async_copy(src, dst, sems.at[i]) for i, (src, dst) in enumerate(pairs)]
    for copy in copies:
        copy.start()
    for copy in copies:
        copy.wait()


def core_index():
    return lax.rem(lax.axis_index("cent"), 2)


def pair_index():
    return lax.rem(lax.axis_index("cent") // 2, 2)


def leads(nv, core):
    half, quarter = nv // 2, nv // 4
    rest = (1 - core) * half
    direct = rest + pair_index() * quarter
    swapped = rest + (1 - pair_index()) * quarter
    return [pl.multiple_of(lead, 64) for lead in (core * half, direct, swapped)]


def outgoing_kernel(v_hbm, half_ref, quarter_ref, sems):
    half_lead, direct, _ = leads(v_hbm.shape[0], core_index())
    rows = quarter_ref.shape[0]
    copy_rows(
        [
            (v_hbm.at[pl.ds(direct, rows), :], quarter_ref),
            (v_hbm.at[pl.ds(half_lead, rows), :], half_ref.at[pl.ds(0, rows), :]),
            (v_hbm.at[pl.ds(half_lead + rows, rows), :], half_ref.at[pl.ds(rows, rows), :]),
        ],
        sems,
    )


def outgoing(vectors):
    nv, dim = vectors.shape
    vmem = pl.BlockSpec(memory_space=pltpu.VMEM)
    return pl.pallas_call(
        outgoing_kernel,
        in_specs=[pl.BlockSpec(memory_space=pl.ANY)],
        out_specs=[vmem] * 2,
        out_shape=[pltpu.VMEM((nv // 2, dim), jnp.bfloat16), pltpu.VMEM((nv // 4, dim), jnp.bfloat16)],
        scratch_shapes=[pltpu.SemaphoreType.DMA((3,))],
        compiler_params=pltpu.CompilerParams(vmem_limit_bytes=2 * MIB),
        cost_estimate=pl.CostEstimate(flops=0, bytes_accessed=2 * nv * dim, transcendentals=0),
        name="outgoing",
    )(in_hbm(vectors))


def load_kernel(v_hbm, c_hbm, v_ref, c_ref, sems):
    pairs = []
    for src, dst, count in ((v_hbm, v_ref, 6), (c_hbm, c_ref, 8)):
        rows = dst.shape[0] // count
        pairs += [(src.at[pl.ds(i * rows, rows), :], dst.at[pl.ds(i * rows, rows), :]) for i in range(count)]
    copy_rows(pairs, sems)


def load(vectors, centroids):
    vmem = pl.BlockSpec(memory_space=pltpu.VMEM)
    hbm = pl.BlockSpec(memory_space=pl.ANY)
    return pl.pallas_call(
        load_kernel,
        in_specs=[hbm, hbm],
        out_specs=[vmem] * 2,
        out_shape=[pltpu.VMEM(vectors.shape, jnp.bfloat16), pltpu.VMEM(centroids.shape, jnp.bfloat16)],
        scratch_shapes=[pltpu.SemaphoreType.DMA((14,))],
        compiler_params=pltpu.CompilerParams(vmem_limit_bytes=2 * MIB),
        cost_estimate=pl.CostEstimate(
            flops=0, bytes_accessed=4 * (vectors.size + centroids.size), transcendentals=0
        ),
        name="load",
    )(in_hbm(vectors), in_hbm(centroids))


def partial_kernel(scale, rows, v_ref, c_ref, out_ref):
    parts = []
    for start in range(0, c_ref.shape[0], rows):
        logits = scores(c_ref[start : start + rows, :], v_ref[...], scale)
        peak = jnp.max(logits, axis=0, keepdims=True)
        parts.append(peak + jnp.log(jnp.sum(jnp.exp(logits - peak), axis=0, keepdims=True)))
    out_ref[...] = merge(parts)


def partial(vectors, centroids, scale):
    nv, dim = vectors.shape
    k = centroids.shape[0]
    vmem = pl.BlockSpec(memory_space=pltpu.VMEM)
    return pl.pallas_call(
        functools.partial(partial_kernel, scale, min(256, k)),
        in_specs=[vmem, vmem],
        out_specs=vmem,
        out_shape=jax.ShapeDtypeStruct((1, nv), jnp.float32),
        compiler_params=pltpu.CompilerParams(vmem_limit_bytes=12 * MIB),
        cost_estimate=pl.CostEstimate(
            flops=2 * nv * k * dim, bytes_accessed=2 * (nv + k) * dim, transcendentals=nv * k
        ),
        name="partial_lse",
    )(in_vmem(vectors), in_vmem(centroids))


def index_of(plan, place):
    if not plan["exchange"]:
        return place
    mask = (0, 1 + core_index(), 2 - core_index(), 3)[place]
    return lax.axis_index("item") ^ mask


def weigh(resp, vectors):
    term = lax.dot_general(resp, vectors, NN, preferred_element_type=jnp.float32)
    return term, jnp.sum(resp.astype(jnp.float32), axis=1, keepdims=True)


def updated(total, mass, old):
    return ((total + old.astype(jnp.float32)) / (mass + 1.0)).astype(jnp.bfloat16)


def own_rows(c_ref, rows):
    return c_ref[pl.ds(pl.multiple_of(lax.axis_index("item") * rows, rows), rows), :]


def absorb(own, vectors, lse, scale, total, mass):
    resp = jnp.exp(scores(own, vectors, scale) - lse).astype(jnp.bfloat16)
    term, weight = weigh(resp, vectors)
    return (term, weight) if total is None else (total + term, mass + weight)


def own_rows(c_ref, rows):
    return c_ref[pl.ds(pl.multiple_of(lax.axis_index("item") * rows, rows), rows), :]


def home_kernel(scale, c_ref, home, row, _, total, mass):
    own = own_rows(c_ref, total.shape[0])
    total[...], mass[...] = absorb(own, home[...], row[...], scale, None, None)


def early_kernel(plan, scale, c_ref, *refs):
    n = plan["pieces"]
    first = plan["first"]
    sums = weights = None
    if first:
        sums, weights, refs = refs[0][...], refs[1][...], refs[2:]
    rows, refs = refs[: plan["early"] - first], refs[plan["early"] - first :]
    pieces, arrived, outs = refs[:n], refs[n : n + plan["arrived"]], refs[n + plan["arrived"] :]
    total, mass = outs[:2]
    own = own_rows(c_ref, total.shape[0])
    if arrived:
        table, nv = outs[2], plan["nv"]
        core = core_index()
        half_lead, direct, swapped = leads(nv, core)
        places = [half_lead, direct, swapped]
        half_lead, direct, swapped = leads(nv, 1 - core)
        places += [nv + half_lead, nv + half_lead + nv // 4, nv + direct, nv + swapped]
        for lead, ref in zip(places, arrived):
            table[pl.ds(pl.multiple_of(lead, 64), ref.shape[0]), :] = ref[...]
        pieces += (table,)
    for place in range(first, plan["early"]):
        vectors = vectors_of(plan, place, pieces)
        sums, weights = absorb(own, vectors, rows[place - first][...], scale, sums, weights)
    total[...], mass[...] = sums, weights


def vectors_of(plan, place, pieces):
    operand, start = plan["blocks"][place]
    return pieces[operand][pl.ds(start, plan["nv"]), :]


def late_kernel(plan, scale, c_ref, total, mass, *refs):
    n, early = plan["pieces"], plan["early"]
    rows, refs = refs[: plan["places"] - early], refs[plan["places"] - early :]
    pieces, refs = refs[:n], refs[n:]
    sums, weights = total[...], mass[...]
    if early < plan["places"]:
        mine, other, new_ref, expo_ref, peak_ref, part_ref, block = refs
        pieces += (block,)
        half = mine.shape[0]
        block[pl.ds(pl.multiple_of(core_index() * half, half), half), :] = mine[...]
        block[pl.ds(pl.multiple_of((1 - core_index()) * half, half), half), :] = other[...]
    else:
        new_ref, expo_ref, peak_ref, part_ref = refs
    own = own_rows(c_ref, new_ref.shape[0])
    for place in range(early, plan["places"]):
        vectors = vectors_of(plan, place, pieces)
        sums, weights = absorb(own, vectors, rows[place - early][...], scale, sums, weights)
    new_ref[...] = updated(sums, weights, own)
    for place in range(plan["places"]):
        logits = scores(new_ref[...], vectors_of(plan, place, pieces), scale)
        peak = jnp.max(logits, axis=0, keepdims=True)
        expo = jnp.exp(logits - peak)
        expo_ref[place] = expo
        peak_ref[pl.ds(place, 1), :] = peak
        part_ref[pl.ds(index_of(plan, place), 1), :] = peak + jnp.log(jnp.sum(expo, axis=0, keepdims=True))


def last_kernel(plan, old_ref, expo_ref, peak_ref, parts, *refs):
    pieces, (new_ref, norm_ref, lse_ref) = refs[:-3], refs[-3:]
    lse_ref[...] = merge([parts[i] for i in range(parts.shape[0])])
    norm_ref[...] = lse_ref[pl.ds(lax.axis_index("item"), 1), :].reshape(norm_ref.shape)
    total = mass = None
    for place in range(plan["places"]):
        factor = jnp.exp(peak_ref[pl.ds(place, 1), :] - lse_ref[pl.ds(index_of(plan, place), 1), :])
        resp = (expo_ref[place] * factor).astype(jnp.bfloat16)
        term, weight = weigh(resp, vectors_of(plan, place, pieces))
        total = term if total is None else total + term
        mass = weight if mass is None else mass + weight
    new_ref[...] = updated(total, mass, old_ref[...])


def send(value, items, cents, item_mask, cent_mask=0):
    masks = item_mask if isinstance(item_mask, tuple) else (item_mask, item_mask)
    pairs = [
        (i * cents + c, (i ^ masks[c % 2]) * cents + (c ^ cent_mask)) for i in range(items) for c in range(cents)
    ]
    return lax.ppermute(value, BOTH, pairs)


def merge_cent(part, go):
    part = merge([part, go(part, 0, 1)])
    return merge([part] + [go(part, 0, mask) for mask in (2, 4, 6)])


def after(value, *others):
    vmem = pl.BlockSpec(memory_space=pltpu.VMEM)
    return pl.pallas_call(
        lambda *refs: None,
        in_specs=[vmem] + [pl.BlockSpec(memory_space=pl.ANY)] * len(others),
        out_specs=vmem,
        out_shape=pltpu.VMEM(value.shape, value.dtype),
        input_output_aliases={0: 0},
        compiler_params=pltpu.CompilerParams(vmem_limit_bytes=2 * MIB),
        name="after",
    )(in_vmem(value), *others)


def shards(vectors, centroids):
    items, cents = lax.axis_size("item"), lax.axis_size("cent")
    nv, dim = vectors.shape
    rows = centroids.shape[0] // items
    scale = BETA / math.sqrt(dim)

    def go(value, item_mask, cent_mask=0):
        return send(value, items, cents, item_mask, cent_mask)

    small = items == 4 and cents == 8
    if small:
        half, quarter = outgoing(vectors)
        near_quarter, near_half = go(quarter, (1, 2)), go(half, (1, 2))
        home, centroids = load(vectors, centroids)
        lse = merge_cent(partial(home, centroids, scale), go)
        parts = [lse, go(lse, (1, 2)), go(lse, (2, 1)), go(lse, 3)]
        near_quarter, near_half = after(near_quarter, lse), after(near_half, lse)
        swapped = go(near_quarter, 0, 2)
        far = go(near_half, (2, 1))
        over = [near_half[: nv // 4], near_half[nv // 4 :], near_quarter, swapped]
        near = [near_half, near_quarter, swapped] + [go(piece, 0, 1) for piece in over]
        pieces = [home]
        plan = dict(exchange=True, first=1, early=3, blocks=[(0, 0), (1, 0), (1, nv), (2, 0)])
    else:
        home, centroids = load(vectors, centroids)
        parts = lax.all_gather(partial(home, centroids, scale), "cent", axis=0, tiled=False)
        parts = merge([parts[i] for i in range(cents)])
        parts = lax.all_gather(parts, "item", axis=0, tiled=False)
        parts = [parts[i] for i in range(items)]
        pieces = [lax.all_gather(vectors, "item", axis=0, tiled=True)]
        near = []
        plan = dict(exchange=False, first=0, early=items, blocks=[(0, i * nv) for i in range(items)])
    plan.update(nv=nv, places=items, pieces=len(pieces), arrived=len(near))
    pieces = [in_vmem(piece) for piece in pieces]
    centroids = in_vmem(centroids)

    vmem = pl.BlockSpec(memory_space=pltpu.VMEM)
    flops = 2 * nv * rows * dim
    early, late = plan["early"], items - plan["early"]
    params = pltpu.CompilerParams(vmem_limit_bytes=16 * MIB)
    tables = [pltpu.VMEM((2 * nv, dim), jnp.bfloat16)] if near else []
    begun = []
    if plan["first"]:
        begun = pl.pallas_call(
            functools.partial(home_kernel, scale),
            in_specs=[vmem] * 3 + [pl.BlockSpec(memory_space=pl.ANY)],
            out_specs=[vmem] * 2,
            out_shape=[pltpu.VMEM((rows, dim), jnp.float32), pltpu.VMEM((rows, 1), jnp.float32)],
            compiler_params=params,
            cost_estimate=pl.CostEstimate(flops=2 * flops, bytes_accessed=2 * nv * dim, transcendentals=nv * rows),
            name="home_block",
        )(centroids, pieces[0], parts[0], parts[3])
        begun = [in_vmem(value) for value in begun]
    total, mass, *table = pl.pallas_call(
        functools.partial(early_kernel, dict(plan), scale),
        in_specs=[vmem] * (1 + len(begun) + early - plan["first"] + len(pieces) + len(near)),
        out_specs=[vmem] * (2 + len(tables)),
        out_shape=[
            pltpu.VMEM((rows, dim), jnp.float32),
            pltpu.VMEM((rows, 1), jnp.float32),
        ]
        + tables,
        compiler_params=params,
        cost_estimate=pl.CostEstimate(flops=0, bytes_accessed=0, transcendentals=0),
        name="early_blocks",
    )(centroids, *begun, *parts[plan["first"] : early], *pieces, *[in_vmem(piece) for piece in near])
    pieces += [in_vmem(piece) for piece in table]
    plan["pieces"] = len(pieces)

    arrived = []
    if late:
        far = after(far, *parts[1:])
        arrived = [in_vmem(far), in_vmem(go(far, 0, 1))]
    fresh, expo, peak, part, *block = pl.pallas_call(
        functools.partial(late_kernel, dict(plan), scale),
        in_specs=[vmem] * (3 + late + len(pieces) + len(arrived)),
        out_specs=[vmem] * (4 + late),
        out_shape=[
            pltpu.VMEM((rows, dim), jnp.bfloat16),
            pltpu.VMEM((items, rows, nv), jnp.float32),
            pltpu.VMEM((items, nv), jnp.float32),
            pltpu.VMEM((items, nv), jnp.float32),
        ]
        + [pltpu.VMEM((nv, dim), jnp.bfloat16)] * late,
        compiler_params=params,
        cost_estimate=pl.CostEstimate(
            flops=(items + 2 * late) * flops,
            bytes_accessed=2 * late * nv * dim,
            transcendentals=(items + late) * nv * rows,
        ),
        name="late_blocks",
    )(centroids, in_vmem(total), in_vmem(mass), *parts[early:], *pieces, *arrived)
    pieces += [in_vmem(piece) for piece in block]

    if small:
        lse = merge_cent(part, go)
        parts = merge([lse] + [go(lse, mask) for mask in (1, 2, 3)])[None]
    else:
        gathered = lax.all_gather(part, "cent", axis=0, tiled=False)
        parts = lax.all_gather(merge([gathered[i] for i in range(cents)]), "item", axis=0, tiled=False)
    result, norm = pl.pallas_call(
        functools.partial(last_kernel, dict(plan)),
        in_specs=[vmem] * (4 + len(pieces)),
        out_specs=[vmem] * 2,
        out_shape=[
            jax.ShapeDtypeStruct((rows, dim), jnp.bfloat16),
            jax.ShapeDtypeStruct((nv,), jnp.float32),
        ],
        scratch_shapes=[pltpu.VMEM((items, nv), jnp.float32)],
        compiler_params=params,
        cost_estimate=pl.CostEstimate(flops=items * flops, bytes_accessed=2 * rows * dim, transcendentals=0),
        name="last_iteration",
    )(in_vmem(fresh), in_vmem(expo), in_vmem(peak), parts, *pieces)
    return (result, norm)


def solution(mesh):
    in_specs = (P("item", None), P("cent", None))
    out_specs = (P(("cent", "item"), None), P("item"))
    return jax.shard_map(shards, mesh=mesh, in_specs=in_specs, out_specs=out_specs, check_vma=False)
```

```python
import functools
import math

import jax
import jax.numpy as jnp
from jax import lax
from jax.experimental import pallas as pl
from jax.experimental.pallas import tpu as pltpu
from jax.sharding import PartitionSpec as P

BETA = 3.0
BOTH = ("item", "cent")
MIB = 1024 * 1024
NT = (((1,), (1,)), ((), ()))
NN = (((1,), (0,)), ((), ()))


def scores(rows, vectors, scale):
    raw = lax.dot_general(rows, vectors, NT, preferred_element_type=jnp.float32)
    sqnorm = jnp.sum(jnp.square(rows.astype(jnp.float32)), axis=1, keepdims=True)
    return scale * (raw - 0.5 * sqnorm)


def merge(parts):
    peak = functools.reduce(jnp.maximum, parts)
    terms = [jnp.exp(p - peak) for p in parts]
    while len(terms) > 1:
        terms = [sum(terms[i : i + 2]) for i in range(0, len(terms), 2)]
    return peak + jnp.log(terms[0])


def in_hbm(value):
    return pltpu.with_memory_space_constraint(value, pltpu.HBM)


def in_vmem(value):
    return pltpu.with_memory_space_constraint(value, pltpu.VMEM)


def copy_rows(pairs, sems):
    copies = [pltpu.make_async_copy(src, dst, sems.at[i]) for i, (src, dst) in enumerate(pairs)]
    for copy in copies:
        copy.start()
    for copy in copies:
        copy.wait()


def core_index():
    return lax.rem(lax.axis_index("cent"), 2)


def pair_index():
    return lax.rem(lax.axis_index("cent") // 2, 2)


def leads(nv, core):
    half, quarter = nv // 2, nv // 4
    rest = (1 - core) * half
    direct = rest + pair_index() * quarter
    swapped = rest + (1 - pair_index()) * quarter
    return [pl.multiple_of(lead, 64) for lead in (core * half, direct, swapped)]


def outgoing_kernel(v_hbm, out_ref, sems):
    half_lead, direct, _ = leads(v_hbm.shape[0], core_index())
    rows = out_ref.shape[0] // 3
    starts = (half_lead, half_lead + rows, direct)
    copy_rows(
        [
            (v_hbm.at[pl.ds(pl.multiple_of(start, 64), rows), :], out_ref.at[pl.ds(i * rows, rows), :])
            for i, start in enumerate(starts)
        ],
        sems,
    )


def outgoing(vectors):
    nv, dim = vectors.shape
    return pl.pallas_call(
        outgoing_kernel,
        in_specs=[pl.BlockSpec(memory_space=pl.ANY)],
        out_specs=pl.BlockSpec(memory_space=pltpu.VMEM),
        out_shape=pltpu.VMEM((3 * (nv // 4), dim), jnp.bfloat16),
        scratch_shapes=[pltpu.SemaphoreType.DMA((3,))],
        compiler_params=pltpu.CompilerParams(vmem_limit_bytes=2 * MIB),
        cost_estimate=pl.CostEstimate(flops=0, bytes_accessed=2 * nv * dim, transcendentals=0),
        name="outgoing",
    )(in_hbm(vectors))


def load_kernel(v_hbm, c_hbm, v_ref, c_ref, sems):
    pairs = []
    for src, dst, count in ((v_hbm, v_ref, 6), (c_hbm, c_ref, 8)):
        rows = dst.shape[0] // count
        pairs += [(src.at[pl.ds(i * rows, rows), :], dst.at[pl.ds(i * rows, rows), :]) for i in range(count)]
    copy_rows(pairs, sems)


def load(vectors, centroids):
    vmem = pl.BlockSpec(memory_space=pltpu.VMEM)
    hbm = pl.BlockSpec(memory_space=pl.ANY)
    return pl.pallas_call(
        load_kernel,
        in_specs=[hbm, hbm],
        out_specs=[vmem] * 2,
        out_shape=[pltpu.VMEM(vectors.shape, jnp.bfloat16), pltpu.VMEM(centroids.shape, jnp.bfloat16)],
        scratch_shapes=[pltpu.SemaphoreType.DMA((14,))],
        compiler_params=pltpu.CompilerParams(vmem_limit_bytes=2 * MIB),
        cost_estimate=pl.CostEstimate(
            flops=0, bytes_accessed=4 * (vectors.size + centroids.size), transcendentals=0
        ),
        name="load",
    )(in_hbm(vectors), in_hbm(centroids))


def partial_kernel(scale, rows, v_ref, c_ref, out_ref):
    parts = []
    for start in range(0, c_ref.shape[0], rows):
        logits = scores(c_ref[start : start + rows, :], v_ref[...], scale)
        peak = jnp.max(logits, axis=0, keepdims=True)
        parts.append(peak + jnp.log(jnp.sum(jnp.exp(logits - peak), axis=0, keepdims=True)))
    out_ref[...] = merge(parts)


def partial(vectors, centroids, scale):
    nv, dim = vectors.shape
    k = centroids.shape[0]
    vmem = pl.BlockSpec(memory_space=pltpu.VMEM)
    return pl.pallas_call(
        functools.partial(partial_kernel, scale, min(256, k)),
        in_specs=[vmem, vmem],
        out_specs=vmem,
        out_shape=jax.ShapeDtypeStruct((1, nv), jnp.float32),
        compiler_params=pltpu.CompilerParams(vmem_limit_bytes=12 * MIB),
        cost_estimate=pl.CostEstimate(
            flops=2 * nv * k * dim, bytes_accessed=2 * (nv + k) * dim, transcendentals=nv * k
        ),
        name="partial_lse",
    )(in_vmem(vectors), in_vmem(centroids))


def index_of(plan, place):
    if not plan["exchange"]:
        return place
    mask = (0, 1 + core_index(), 2 - core_index(), 3)[place]
    return lax.axis_index("item") ^ mask


def weigh(resp, vectors):
    term = lax.dot_general(resp, vectors, NN, preferred_element_type=jnp.float32)
    return term, jnp.sum(resp.astype(jnp.float32), axis=1, keepdims=True)


def updated(total, mass, old):
    return ((total + old.astype(jnp.float32)) / (mass + 1.0)).astype(jnp.bfloat16)


def own_rows(c_ref, rows):
    return c_ref[pl.ds(pl.multiple_of(lax.axis_index("item") * rows, rows), rows), :]


def absorb(own, vectors, lse, scale, total, mass):
    resp = jnp.exp(scores(own, vectors, scale) - lse).astype(jnp.bfloat16)
    term, weight = weigh(resp, vectors)
    return (term, weight) if total is None else (total + term, mass + weight)


def own_rows(c_ref, rows):
    return c_ref[pl.ds(pl.multiple_of(lax.axis_index("item") * rows, rows), rows), :]


def home_kernel(scale, c_ref, home, row, _, total, mass):
    own = own_rows(c_ref, total.shape[0])
    total[...], mass[...] = absorb(own, home[...], row[...], scale, None, None)


def early_kernel(plan, scale, c_ref, *refs):
    n = plan["pieces"]
    first = plan["first"]
    sums = weights = None
    if first:
        sums, weights, refs = refs[0][...], refs[1][...], refs[2:]
    rows, refs = refs[: plan["early"] - first], refs[plan["early"] - first :]
    pieces, arrived, outs = refs[:n], refs[n : n + plan["arrived"]], refs[n + plan["arrived"] :]
    total, mass = outs[:2]
    own = own_rows(c_ref, total.shape[0])
    if arrived:
        table, nv = outs[2], plan["nv"]
        core = core_index()
        half_lead, direct, swapped = leads(nv, core)
        quarter = nv // 4
        near, arrived = arrived[0], arrived[1:]
        table[pl.ds(half_lead, 2 * quarter), :] = near[: 2 * quarter, :]
        table[pl.ds(direct, quarter), :] = near[2 * quarter :, :]
        places = [swapped]
        half_lead, direct, swapped = leads(nv, 1 - core)
        places += [nv + half_lead, nv + half_lead + quarter, nv + direct, nv + swapped]
        for lead, ref in zip(places, arrived):
            table[pl.ds(pl.multiple_of(lead, 64), quarter), :] = ref[...]
        pieces += (table,)
    for place in range(first, plan["early"]):
        vectors = vectors_of(plan, place, pieces)
        sums, weights = absorb(own, vectors, rows[place - first][...], scale, sums, weights)
    total[...], mass[...] = sums, weights


def vectors_of(plan, place, pieces):
    operand, start = plan["blocks"][place]
    return pieces[operand][pl.ds(start, plan["nv"]), :]


def late_kernel(plan, scale, c_ref, total, mass, *refs):
    n, early = plan["pieces"], plan["early"]
    rows, refs = refs[: plan["places"] - early], refs[plan["places"] - early :]
    pieces, refs = refs[:n], refs[n:]
    sums, weights = total[...], mass[...]
    if early < plan["places"]:
        mine, other, new_ref, expo_ref, peak_ref, part_ref, block = refs
        pieces += (block,)
        half = mine.shape[0]
        block[pl.ds(pl.multiple_of(core_index() * half, half), half), :] = mine[...]
        block[pl.ds(pl.multiple_of((1 - core_index()) * half, half), half), :] = other[...]
    else:
        new_ref, expo_ref, peak_ref, part_ref = refs
    own = own_rows(c_ref, new_ref.shape[0])
    for place in range(early, plan["places"]):
        vectors = vectors_of(plan, place, pieces)
        sums, weights = absorb(own, vectors, rows[place - early][...], scale, sums, weights)
    new_ref[...] = updated(sums, weights, own)
    for place in range(plan["places"]):
        logits = scores(new_ref[...], vectors_of(plan, place, pieces), scale)
        peak = jnp.max(logits, axis=0, keepdims=True)
        expo = jnp.exp(logits - peak)
        expo_ref[place] = expo
        peak_ref[pl.ds(place, 1), :] = peak
        part_ref[pl.ds(index_of(plan, place), 1), :] = peak + jnp.log(jnp.sum(expo, axis=0, keepdims=True))


def last_kernel(plan, old_ref, expo_ref, peak_ref, parts, *refs):
    pieces, (new_ref, norm_ref, lse_ref) = refs[:-3], refs[-3:]
    lse_ref[...] = merge([parts[i] for i in range(parts.shape[0])])
    norm_ref[...] = lse_ref[pl.ds(lax.axis_index("item"), 1), :].reshape(norm_ref.shape)
    total = mass = None
    for place in range(plan["places"]):
        factor = jnp.exp(peak_ref[pl.ds(place, 1), :] - lse_ref[pl.ds(index_of(plan, place), 1), :])
        resp = (expo_ref[place] * factor).astype(jnp.bfloat16)
        term, weight = weigh(resp, vectors_of(plan, place, pieces))
        total = term if total is None else total + term
        mass = weight if mass is None else mass + weight
    new_ref[...] = updated(total, mass, old_ref[...])


def send(value, items, cents, item_mask, cent_mask=0):
    masks = item_mask if isinstance(item_mask, tuple) else (item_mask, item_mask)
    pairs = [
        (i * cents + c, (i ^ masks[c % 2]) * cents + (c ^ cent_mask)) for i in range(items) for c in range(cents)
    ]
    return lax.ppermute(value, BOTH, pairs)


def merge_cent(part, go):
    part = merge([part, go(part, 0, 1)])
    return merge([part] + [go(part, 0, mask) for mask in (2, 4, 6)])


def after(value, *others):
    vmem = pl.BlockSpec(memory_space=pltpu.VMEM)
    return pl.pallas_call(
        lambda *refs: None,
        in_specs=[vmem] + [pl.BlockSpec(memory_space=pl.ANY)] * len(others),
        out_specs=vmem,
        out_shape=pltpu.VMEM(value.shape, value.dtype),
        input_output_aliases={0: 0},
        compiler_params=pltpu.CompilerParams(vmem_limit_bytes=2 * MIB),
        name="after",
    )(in_vmem(value), *others)


def shards(vectors, centroids):
    items, cents = lax.axis_size("item"), lax.axis_size("cent")
    nv, dim = vectors.shape
    rows = centroids.shape[0] // items
    scale = BETA / math.sqrt(dim)

    def go(value, item_mask, cent_mask=0):
        return send(value, items, cents, item_mask, cent_mask)

    small = items == 4 and cents == 8
    if small:
        near = go(outgoing(vectors), (1, 2))
        home, centroids = load(vectors, centroids)
        lse = merge_cent(partial(home, centroids, scale), go)
        parts = [lse, go(lse, (1, 2)), go(lse, (2, 1)), go(lse, 3)]
        near = after(near, lse)
        quarters = [near[i : i + nv // 4] for i in range(0, near.shape[0], nv // 4)]
        swapped = go(quarters[2], 0, 2)
        far = go(near[: nv // 2], (2, 1))
        near = [near, swapped] + [go(piece, 0, 1) for piece in quarters + [swapped]]
        pieces = [home]
        plan = dict(exchange=True, first=1, early=3, blocks=[(0, 0), (1, 0), (1, nv), (2, 0)])
    else:
        home, centroids = load(vectors, centroids)
        parts = lax.all_gather(partial(home, centroids, scale), "cent", axis=0, tiled=False)
        parts = merge([parts[i] for i in range(cents)])
        parts = lax.all_gather(parts, "item", axis=0, tiled=False)
        parts = [parts[i] for i in range(items)]
        pieces = [lax.all_gather(vectors, "item", axis=0, tiled=True)]
        near = []
        plan = dict(exchange=False, first=0, early=items, blocks=[(0, i * nv) for i in range(items)])
    plan.update(nv=nv, places=items, pieces=len(pieces), arrived=len(near))
    pieces = [in_vmem(piece) for piece in pieces]
    centroids = in_vmem(centroids)

    vmem = pl.BlockSpec(memory_space=pltpu.VMEM)
    flops = 2 * nv * rows * dim
    early, late = plan["early"], items - plan["early"]
    params = pltpu.CompilerParams(vmem_limit_bytes=16 * MIB)
    tables = [pltpu.VMEM((2 * nv, dim), jnp.bfloat16)] if near else []
    begun = []
    if plan["first"]:
        begun = pl.pallas_call(
            functools.partial(home_kernel, scale),
            in_specs=[vmem] * 3 + [pl.BlockSpec(memory_space=pl.ANY)],
            out_specs=[vmem] * 2,
            out_shape=[pltpu.VMEM((rows, dim), jnp.float32), pltpu.VMEM((rows, 1), jnp.float32)],
            compiler_params=params,
            cost_estimate=pl.CostEstimate(flops=2 * flops, bytes_accessed=2 * nv * dim, transcendentals=nv * rows),
            name="home_block",
        )(centroids, pieces[0], parts[0], near[2])
        begun = [in_vmem(value) for value in begun]
    total, mass, *table = pl.pallas_call(
        functools.partial(early_kernel, dict(plan), scale),
        in_specs=[vmem] * (1 + len(begun) + early - plan["first"] + len(pieces) + len(near)),
        out_specs=[vmem] * (2 + len(tables)),
        out_shape=[
            pltpu.VMEM((rows, dim), jnp.float32),
            pltpu.VMEM((rows, 1), jnp.float32),
        ]
        + tables,
        compiler_params=params,
        cost_estimate=pl.CostEstimate(flops=0, bytes_accessed=0, transcendentals=0),
        name="early_blocks",
    )(centroids, *begun, *parts[plan["first"] : early], *pieces, *[in_vmem(piece) for piece in near])
    pieces += [in_vmem(piece) for piece in table]
    plan["pieces"] = len(pieces)

    arrived = []
    if late:
        far = after(far, *parts[1:], *near[2:], begun[1])
        arrived = [in_vmem(far), in_vmem(go(far, 0, 1))]
    fresh, expo, peak, part, *block = pl.pallas_call(
        functools.partial(late_kernel, dict(plan), scale),
        in_specs=[vmem] * (3 + late + len(pieces) + len(arrived)),
        out_specs=[vmem] * (4 + late),
        out_shape=[
            pltpu.VMEM((rows, dim), jnp.bfloat16),
            pltpu.VMEM((items, rows, nv), jnp.float32),
            pltpu.VMEM((items, nv), jnp.float32),
            pltpu.VMEM((items, nv), jnp.float32),
        ]
        + [pltpu.VMEM((nv, dim), jnp.bfloat16)] * late,
        compiler_params=params,
        cost_estimate=pl.CostEstimate(
            flops=(items + 2 * late) * flops,
            bytes_accessed=2 * late * nv * dim,
            transcendentals=(items + late) * nv * rows,
        ),
        name="late_blocks",
    )(centroids, in_vmem(total), in_vmem(mass), *parts[early:], *pieces, *arrived)
    pieces += [in_vmem(piece) for piece in block]

    if small:
        lse = merge_cent(part, go)
        parts = merge([lse] + [go(lse, mask) for mask in (1, 2, 3)])[None]
    else:
        gathered = lax.all_gather(part, "cent", axis=0, tiled=False)
        parts = lax.all_gather(merge([gathered[i] for i in range(cents)]), "item", axis=0, tiled=False)
    result, norm = pl.pallas_call(
        functools.partial(last_kernel, dict(plan)),
        in_specs=[vmem] * (4 + len(pieces)),
        out_specs=[vmem] * 2,
        out_shape=[
            jax.ShapeDtypeStruct((rows, dim), jnp.bfloat16),
            jax.ShapeDtypeStruct((nv,), jnp.float32),
        ],
        scratch_shapes=[pltpu.VMEM((items, nv), jnp.float32)],
        compiler_params=params,
        cost_estimate=pl.CostEstimate(flops=items * flops, bytes_accessed=2 * rows * dim, transcendentals=0),
        name="last_iteration",
    )(in_vmem(fresh), in_vmem(expo), in_vmem(peak), parts, *pieces)
    return (result, norm)


def solution(mesh):
    in_specs = (P("item", None), P("cent", None))
    out_specs = (P(("cent", "item"), None), P("item"))
    return jax.shard_map(shards, mesh=mesh, in_specs=in_specs, out_specs=out_specs, check_vma=False)
```

```python
import functools
import math

import jax
import jax.numpy as jnp
from jax import lax
from jax.experimental import pallas as pl
from jax.experimental.pallas import tpu as pltpu
from jax.sharding import PartitionSpec as P

BETA = 3.0
BOTH = ("item", "cent")
MIB = 1024 * 1024
NT = (((1,), (1,)), ((), ()))
NN = (((1,), (0,)), ((), ()))


def scores(rows, vectors, scale):
    raw = lax.dot_general(rows, vectors, NT, preferred_element_type=jnp.float32)
    sqnorm = jnp.sum(jnp.square(rows.astype(jnp.float32)), axis=1, keepdims=True)
    return scale * (raw - 0.5 * sqnorm)


def merge(parts):
    peak = functools.reduce(jnp.maximum, parts)
    terms = [jnp.exp(p - peak) for p in parts]
    while len(terms) > 1:
        terms = [sum(terms[i : i + 2]) for i in range(0, len(terms), 2)]
    return peak + jnp.log(terms[0])


def in_hbm(value):
    return pltpu.with_memory_space_constraint(value, pltpu.HBM)


def in_vmem(value):
    return pltpu.with_memory_space_constraint(value, pltpu.VMEM)


def copy_rows(pairs, sems):
    copies = [pltpu.make_async_copy(src, dst, sems.at[i]) for i, (src, dst) in enumerate(pairs)]
    for copy in copies:
        copy.start()
    for copy in copies:
        copy.wait()


def core_index():
    return lax.rem(lax.axis_index("cent"), 2)


def pair_index():
    return lax.rem(lax.axis_index("cent") // 2, 2)


def leads(nv, core):
    half, quarter = nv // 2, nv // 4
    rest = (1 - core) * half
    direct = rest + pair_index() * quarter
    swapped = rest + (1 - pair_index()) * quarter
    return [pl.multiple_of(lead, 64) for lead in (core * half, direct, swapped)]


def outgoing_kernel(v_hbm, out_ref, sems):
    half_lead, direct, _ = leads(v_hbm.shape[0], core_index())
    rows = out_ref.shape[0] // 3
    starts = (half_lead, half_lead + rows, direct)
    copy_rows(
        [
            (v_hbm.at[pl.ds(pl.multiple_of(start, 64), rows), :], out_ref.at[pl.ds(i * rows, rows), :])
            for i, start in enumerate(starts)
        ],
        sems,
    )


def outgoing(vectors):
    nv, dim = vectors.shape
    return pl.pallas_call(
        outgoing_kernel,
        in_specs=[pl.BlockSpec(memory_space=pl.ANY)],
        out_specs=pl.BlockSpec(memory_space=pltpu.VMEM),
        out_shape=pltpu.VMEM((3 * (nv // 4), dim), jnp.bfloat16),
        scratch_shapes=[pltpu.SemaphoreType.DMA((3,))],
        compiler_params=pltpu.CompilerParams(vmem_limit_bytes=2 * MIB),
        cost_estimate=pl.CostEstimate(flops=0, bytes_accessed=2 * nv * dim, transcendentals=0),
        name="outgoing",
    )(in_hbm(vectors))


def load_kernel(v_hbm, c_hbm, v_ref, c_ref, sems):
    pairs = []
    for src, dst, count in ((v_hbm, v_ref, 6), (c_hbm, c_ref, 8)):
        rows = dst.shape[0] // count
        pairs += [(src.at[pl.ds(i * rows, rows), :], dst.at[pl.ds(i * rows, rows), :]) for i in range(count)]
    copy_rows(pairs, sems)


def load(vectors, centroids):
    vmem = pl.BlockSpec(memory_space=pltpu.VMEM)
    hbm = pl.BlockSpec(memory_space=pl.ANY)
    return pl.pallas_call(
        load_kernel,
        in_specs=[hbm, hbm],
        out_specs=[vmem] * 2,
        out_shape=[pltpu.VMEM(vectors.shape, jnp.bfloat16), pltpu.VMEM(centroids.shape, jnp.bfloat16)],
        scratch_shapes=[pltpu.SemaphoreType.DMA((14,))],
        compiler_params=pltpu.CompilerParams(vmem_limit_bytes=2 * MIB),
        cost_estimate=pl.CostEstimate(
            flops=0, bytes_accessed=4 * (vectors.size + centroids.size), transcendentals=0
        ),
        name="load",
    )(in_hbm(vectors), in_hbm(centroids))


def partial_kernel(scale, rows, v_ref, c_ref, out_ref):
    parts = []
    for start in range(0, c_ref.shape[0], rows):
        logits = scores(c_ref[start : start + rows, :], v_ref[...], scale)
        peak = jnp.max(logits, axis=0, keepdims=True)
        parts.append(peak + jnp.log(jnp.sum(jnp.exp(logits - peak), axis=0, keepdims=True)))
    out_ref[...] = merge(parts)


def partial(vectors, centroids, scale):
    nv, dim = vectors.shape
    k = centroids.shape[0]
    vmem = pl.BlockSpec(memory_space=pltpu.VMEM)
    return pl.pallas_call(
        functools.partial(partial_kernel, scale, min(256, k)),
        in_specs=[vmem, vmem],
        out_specs=vmem,
        out_shape=jax.ShapeDtypeStruct((1, nv), jnp.float32),
        compiler_params=pltpu.CompilerParams(vmem_limit_bytes=12 * MIB),
        cost_estimate=pl.CostEstimate(
            flops=2 * nv * k * dim, bytes_accessed=2 * (nv + k) * dim, transcendentals=nv * k
        ),
        name="partial_lse",
    )(in_vmem(vectors), in_vmem(centroids))


def index_of(plan, place):
    if not plan["exchange"]:
        return place
    mask = (0, 1 + core_index(), 2 - core_index(), 3)[place]
    return lax.axis_index("item") ^ mask


def weigh(resp, vectors):
    term = lax.dot_general(resp, vectors, NN, preferred_element_type=jnp.float32)
    return term, jnp.sum(resp.astype(jnp.float32), axis=1, keepdims=True)


def updated(total, mass, old):
    return ((total + old.astype(jnp.float32)) / (mass + 1.0)).astype(jnp.bfloat16)


def own_rows(c_ref, rows):
    return c_ref[pl.ds(pl.multiple_of(lax.axis_index("item") * rows, rows), rows), :]


def absorb(own, vectors, lse, scale, total, mass):
    resp = jnp.exp(scores(own, vectors, scale) - lse).astype(jnp.bfloat16)
    term, weight = weigh(resp, vectors)
    return (term, weight) if total is None else (total + term, mass + weight)


def own_rows(c_ref, rows):
    return c_ref[pl.ds(pl.multiple_of(lax.axis_index("item") * rows, rows), rows), :]


def home_kernel(scale, c_ref, home, row, _, total, mass):
    own = own_rows(c_ref, total.shape[0])
    total[...], mass[...] = absorb(own, home[...], row[...], scale, None, None)


def early_kernel(plan, scale, c_ref, *refs):
    n = plan["pieces"]
    first = plan["first"]
    sums = weights = None
    if first:
        sums, weights, refs = refs[0][...], refs[1][...], refs[2:]
    rows, refs = refs[: plan["early"] - first], refs[plan["early"] - first :]
    pieces, arrived, outs = refs[:n], refs[n : n + plan["arrived"]], refs[n + plan["arrived"] :]
    total, mass = outs[:2]
    own = own_rows(c_ref, total.shape[0])
    if arrived:
        table, nv = outs[2], plan["nv"]
        core = core_index()
        half_lead, direct, swapped = leads(nv, core)
        quarter = nv // 4
        near, arrived = arrived[0], arrived[1:]
        table[pl.ds(half_lead, 2 * quarter), :] = near[: 2 * quarter, :]
        table[pl.ds(direct, quarter), :] = near[2 * quarter :, :]
        places = [swapped]
        half_lead, direct, swapped = leads(nv, 1 - core)
        places += [nv + half_lead, nv + half_lead + quarter, nv + direct, nv + swapped]
        for lead, ref in zip(places, arrived):
            table[pl.ds(pl.multiple_of(lead, 64), quarter), :] = ref[...]
        pieces += (table,)
    for place in range(first, plan["early"]):
        vectors = vectors_of(plan, place, pieces)
        sums, weights = absorb(own, vectors, rows[place - first][...], scale, sums, weights)
    total[...], mass[...] = sums, weights


def vectors_of(plan, place, pieces):
    operand, start = plan["blocks"][place]
    return pieces[operand][pl.ds(start, plan["nv"]), :]


def late_kernel(plan, scale, c_ref, total, mass, *refs):
    n, early = plan["pieces"], plan["early"]
    rows, refs = refs[: plan["places"] - early], refs[plan["places"] - early :]
    pieces, refs = refs[:n], refs[n:]
    sums, weights = total[...], mass[...]
    if early < plan["places"]:
        mine, other, new_ref, expo_ref, peak_ref, part_ref, block = refs
        pieces += (block,)
        half = mine.shape[0]
        block[pl.ds(pl.multiple_of(core_index() * half, half), half), :] = mine[...]
        block[pl.ds(pl.multiple_of((1 - core_index()) * half, half), half), :] = other[...]
    else:
        new_ref, expo_ref, peak_ref, part_ref = refs
    own = own_rows(c_ref, new_ref.shape[0])
    for place in range(early, plan["places"]):
        vectors = vectors_of(plan, place, pieces)
        sums, weights = absorb(own, vectors, rows[place - early][...], scale, sums, weights)
    new_ref[...] = updated(sums, weights, own)
    for place in range(plan["places"]):
        logits = scores(new_ref[...], vectors_of(plan, place, pieces), scale)
        peak = jnp.max(logits, axis=0, keepdims=True)
        expo = jnp.exp(logits - peak)
        expo_ref[place] = expo
        peak_ref[pl.ds(place, 1), :] = peak
        part_ref[pl.ds(index_of(plan, place), 1), :] = peak + jnp.log(jnp.sum(expo, axis=0, keepdims=True))


def last_kernel(plan, old_ref, expo_ref, peak_ref, parts, *refs):
    pieces, (new_ref, norm_ref, lse_ref) = refs[:-3], refs[-3:]
    lse_ref[...] = merge([parts[i] for i in range(parts.shape[0])])
    norm_ref[...] = lse_ref[pl.ds(lax.axis_index("item"), 1), :].reshape(norm_ref.shape)
    total = mass = None
    for place in range(plan["places"]):
        factor = jnp.exp(peak_ref[pl.ds(place, 1), :] - lse_ref[pl.ds(index_of(plan, place), 1), :])
        resp = (expo_ref[place] * factor).astype(jnp.bfloat16)
        term, weight = weigh(resp, vectors_of(plan, place, pieces))
        total = term if total is None else total + term
        mass = weight if mass is None else mass + weight
    new_ref[...] = updated(total, mass, old_ref[...])


def send(value, items, cents, item_mask, cent_mask=0, cores=(0, 1)):
    masks = item_mask if isinstance(item_mask, tuple) else (item_mask, item_mask)
    pairs = [
        (i * cents + c, (i ^ masks[c % 2]) * cents + (c ^ cent_mask))
        for i in range(items)
        for c in range(cents)
        if c % 2 in cores
    ]
    return lax.ppermute(value, BOTH, pairs)


def merge_cent(part, go):
    part = merge([part, go(part, 0, 1)])
    return merge([part] + [go(part, 0, mask) for mask in (2, 4, 6)])


def after(value, *others):
    vmem = pl.BlockSpec(memory_space=pltpu.VMEM)
    return pl.pallas_call(
        lambda *refs: None,
        in_specs=[vmem] + [pl.BlockSpec(memory_space=pl.ANY)] * len(others),
        out_specs=vmem,
        out_shape=pltpu.VMEM(value.shape, value.dtype),
        input_output_aliases={0: 0},
        compiler_params=pltpu.CompilerParams(vmem_limit_bytes=2 * MIB),
        name="after",
    )(in_vmem(value), *others)


def shards(vectors, centroids):
    items, cents = lax.axis_size("item"), lax.axis_size("cent")
    nv, dim = vectors.shape
    rows = centroids.shape[0] // items
    scale = BETA / math.sqrt(dim)

    def go(value, item_mask, cent_mask=0, cores=(0, 1)):
        return send(value, items, cents, item_mask, cent_mask, cores)

    small = items == 4 and cents == 8
    if small:
        near = go(outgoing(vectors), (1, 2))
        home, centroids = load(vectors, centroids)
        lse = merge_cent(partial(home, centroids, scale), go)
        parts = [lse, go(lse, (1, 2)), go(lse, (2, 1)), go(lse, 3)]
        near = after(near, lse)
        quarters = [near[i : i + nv // 4] for i in range(0, near.shape[0], nv // 4)]
        swapped = go(quarters[2], 0, 2)
        far = go(near[: nv // 2], (2, 1))
        near = [near, swapped] + [go(piece, 0, 1) for piece in quarters + [swapped]]
        pieces = [home]
        plan = dict(exchange=True, first=1, early=3, blocks=[(0, 0), (1, 0), (1, nv), (2, 0)])
    else:
        home, centroids = load(vectors, centroids)
        parts = lax.all_gather(partial(home, centroids, scale), "cent", axis=0, tiled=False)
        parts = merge([parts[i] for i in range(cents)])
        parts = lax.all_gather(parts, "item", axis=0, tiled=False)
        parts = [parts[i] for i in range(items)]
        pieces = [lax.all_gather(vectors, "item", axis=0, tiled=True)]
        near = []
        plan = dict(exchange=False, first=0, early=items, blocks=[(0, i * nv) for i in range(items)])
    plan.update(nv=nv, places=items, pieces=len(pieces), arrived=len(near))
    pieces = [in_vmem(piece) for piece in pieces]
    centroids = in_vmem(centroids)

    vmem = pl.BlockSpec(memory_space=pltpu.VMEM)
    flops = 2 * nv * rows * dim
    early, late = plan["early"], items - plan["early"]
    params = pltpu.CompilerParams(vmem_limit_bytes=16 * MIB)
    tables = [pltpu.VMEM((2 * nv, dim), jnp.bfloat16)] if near else []
    begun = []
    if plan["first"]:
        begun = pl.pallas_call(
            functools.partial(home_kernel, scale),
            in_specs=[vmem] * 3 + [pl.BlockSpec(memory_space=pl.ANY)],
            out_specs=[vmem] * 2,
            out_shape=[pltpu.VMEM((rows, dim), jnp.float32), pltpu.VMEM((rows, 1), jnp.float32)],
            compiler_params=params,
            cost_estimate=pl.CostEstimate(flops=2 * flops, bytes_accessed=2 * nv * dim, transcendentals=nv * rows),
            name="home_block",
        )(centroids, pieces[0], parts[0], near[2])
        begun = [in_vmem(value) for value in begun]
    total, mass, *table = pl.pallas_call(
        functools.partial(early_kernel, dict(plan), scale),
        in_specs=[vmem] * (1 + len(begun) + early - plan["first"] + len(pieces) + len(near)),
        out_specs=[vmem] * (2 + len(tables)),
        out_shape=[
            pltpu.VMEM((rows, dim), jnp.float32),
            pltpu.VMEM((rows, 1), jnp.float32),
        ]
        + tables,
        compiler_params=params,
        cost_estimate=pl.CostEstimate(flops=0, bytes_accessed=0, transcendentals=0),
        name="early_blocks",
    )(centroids, *begun, *parts[plan["first"] : early], *pieces, *[in_vmem(piece) for piece in near])
    pieces += [in_vmem(piece) for piece in table]
    plan["pieces"] = len(pieces)

    arrived = []
    if late:
        far = after(far, *parts[1:], *near[2:], begun[1])
        arrived = [in_vmem(far), in_vmem(go(far, 0, 1))]
    fresh, expo, peak, part, *block = pl.pallas_call(
        functools.partial(late_kernel, dict(plan), scale),
        in_specs=[vmem] * (3 + late + len(pieces) + len(arrived)),
        out_specs=[vmem] * (4 + late),
        out_shape=[
            pltpu.VMEM((rows, dim), jnp.bfloat16),
            pltpu.VMEM((items, rows, nv), jnp.float32),
            pltpu.VMEM((items, nv), jnp.float32),
            pltpu.VMEM((items, nv), jnp.float32),
        ]
        + [pltpu.VMEM((nv, dim), jnp.bfloat16)] * late,
        compiler_params=params,
        cost_estimate=pl.CostEstimate(
            flops=(items + 2 * late) * flops,
            bytes_accessed=2 * late * nv * dim,
            transcendentals=(items + late) * nv * rows,
        ),
        name="late_blocks",
    )(centroids, in_vmem(total), in_vmem(mass), *parts[early:], *pieces, *arrived)
    pieces += [in_vmem(piece) for piece in block]

    if small:
        lse = merge([part, go(part, 0, 1)])
        lse = merge([lse] + [go(lse, 0, mask, (1,)) for mask in (2, 4, 6)])
        lse = merge([lse] + [go(lse, mask, 0, (1,)) for mask in (1, 2, 3)])
        parts = jnp.where(core_index() == 1, lse, go(lse, 0, 1, (1,)))[None]
    else:
        gathered = lax.all_gather(part, "cent", axis=0, tiled=False)
        parts = lax.all_gather(merge([gathered[i] for i in range(cents)]), "item", axis=0, tiled=False)
    result, norm = pl.pallas_call(
        functools.partial(last_kernel, dict(plan)),
        in_specs=[vmem] * (4 + len(pieces)),
        out_specs=[vmem] * 2,
        out_shape=[
            jax.ShapeDtypeStruct((rows, dim), jnp.bfloat16),
            jax.ShapeDtypeStruct((nv,), jnp.float32),
        ],
        scratch_shapes=[pltpu.VMEM((items, nv), jnp.float32)],
        compiler_params=params,
        cost_estimate=pl.CostEstimate(flops=items * flops, bytes_accessed=2 * rows * dim, transcendentals=0),
        name="last_iteration",
    )(in_vmem(fresh), in_vmem(expo), in_vmem(peak), parts, *pieces)
    return (result, norm)


def solution(mesh):
    in_specs = (P("item", None), P("cent", None))
    out_specs = (P(("cent", "item"), None), P("item"))
    return jax.shard_map(shards, mesh=mesh, in_specs=in_specs, out_specs=out_specs, check_vma=False)
```

```python
import functools
import math

import jax
import jax.numpy as jnp
from jax import lax
from jax.experimental import pallas as pl
from jax.experimental.pallas import tpu as pltpu
from jax.sharding import PartitionSpec as P

BETA = 3.0
BOTH = ("item", "cent")
MIB = 1024 * 1024
NT = (((1,), (1,)), ((), ()))
NN = (((1,), (0,)), ((), ()))


def scores(rows, vectors, scale):
    raw = lax.dot_general(rows, vectors, NT, preferred_element_type=jnp.float32)
    sqnorm = jnp.sum(jnp.square(rows.astype(jnp.float32)), axis=1, keepdims=True)
    return scale * (raw - 0.5 * sqnorm)


def merge(parts):
    peak = functools.reduce(jnp.maximum, parts)
    terms = [jnp.exp(p - peak) for p in parts]
    while len(terms) > 1:
        terms = [sum(terms[i : i + 2]) for i in range(0, len(terms), 2)]
    return peak + jnp.log(terms[0])


def in_hbm(value):
    return pltpu.with_memory_space_constraint(value, pltpu.HBM)


def in_vmem(value):
    return pltpu.with_memory_space_constraint(value, pltpu.VMEM)


def copy_rows(pairs, sems):
    copies = [pltpu.make_async_copy(src, dst, sems.at[i]) for i, (src, dst) in enumerate(pairs)]
    for copy in copies:
        copy.start()
    for copy in copies:
        copy.wait()


def core_index():
    return lax.rem(lax.axis_index("cent"), 2)


def pair_index():
    return lax.rem(lax.axis_index("cent") // 2, 2)


def leads(nv, core):
    half, quarter = nv // 2, nv // 4
    rest = (1 - core) * half
    direct = rest + pair_index() * quarter
    swapped = rest + (1 - pair_index()) * quarter
    return [pl.multiple_of(lead, 64) for lead in (core * half, direct, swapped)]


def outgoing_kernel(v_hbm, out_ref, sems):
    half_lead, direct, _ = leads(v_hbm.shape[0], core_index())
    rows = out_ref.shape[0] // 3
    starts = (half_lead, half_lead + rows, direct)
    copy_rows(
        [
            (v_hbm.at[pl.ds(pl.multiple_of(start, 64), rows), :], out_ref.at[pl.ds(i * rows, rows), :])
            for i, start in enumerate(starts)
        ],
        sems,
    )


def outgoing(vectors):
    nv, dim = vectors.shape
    return pl.pallas_call(
        outgoing_kernel,
        in_specs=[pl.BlockSpec(memory_space=pl.ANY)],
        out_specs=pl.BlockSpec(memory_space=pltpu.VMEM),
        out_shape=pltpu.VMEM((3 * (nv // 4), dim), jnp.bfloat16),
        scratch_shapes=[pltpu.SemaphoreType.DMA((3,))],
        compiler_params=pltpu.CompilerParams(vmem_limit_bytes=2 * MIB),
        cost_estimate=pl.CostEstimate(flops=0, bytes_accessed=2 * nv * dim, transcendentals=0),
        name="outgoing",
    )(in_hbm(vectors))


def load_kernel(v_hbm, c_hbm, v_ref, c_ref, sems):
    pairs = []
    for src, dst, count in ((v_hbm, v_ref, 6), (c_hbm, c_ref, 8)):
        rows = dst.shape[0] // count
        pairs += [(src.at[pl.ds(i * rows, rows), :], dst.at[pl.ds(i * rows, rows), :]) for i in range(count)]
    copy_rows(pairs, sems)


def load(vectors, centroids):
    vmem = pl.BlockSpec(memory_space=pltpu.VMEM)
    hbm = pl.BlockSpec(memory_space=pl.ANY)
    return pl.pallas_call(
        load_kernel,
        in_specs=[hbm, hbm],
        out_specs=[vmem] * 2,
        out_shape=[pltpu.VMEM(vectors.shape, jnp.bfloat16), pltpu.VMEM(centroids.shape, jnp.bfloat16)],
        scratch_shapes=[pltpu.SemaphoreType.DMA((14,))],
        compiler_params=pltpu.CompilerParams(vmem_limit_bytes=2 * MIB),
        cost_estimate=pl.CostEstimate(
            flops=0, bytes_accessed=4 * (vectors.size + centroids.size), transcendentals=0
        ),
        name="load",
    )(in_hbm(vectors), in_hbm(centroids))


def partial_kernel(scale, rows, v_ref, c_ref, out_ref):
    parts = []
    for start in range(0, c_ref.shape[0], rows):
        logits = scores(c_ref[start : start + rows, :], v_ref[...], scale)
        peak = jnp.max(logits, axis=0, keepdims=True)
        parts.append(peak + jnp.log(jnp.sum(jnp.exp(logits - peak), axis=0, keepdims=True)))
    out_ref[...] = merge(parts)


def partial(vectors, centroids, scale):
    nv, dim = vectors.shape
    k = centroids.shape[0]
    vmem = pl.BlockSpec(memory_space=pltpu.VMEM)
    return pl.pallas_call(
        functools.partial(partial_kernel, scale, min(256, k)),
        in_specs=[vmem, vmem],
        out_specs=vmem,
        out_shape=jax.ShapeDtypeStruct((1, nv), jnp.float32),
        compiler_params=pltpu.CompilerParams(vmem_limit_bytes=12 * MIB),
        cost_estimate=pl.CostEstimate(
            flops=2 * nv * k * dim, bytes_accessed=2 * (nv + k) * dim, transcendentals=nv * k
        ),
        name="partial_lse",
    )(in_vmem(vectors), in_vmem(centroids))


def index_of(plan, place):
    if not plan["exchange"]:
        return place
    mask = (0, 1 + core_index(), 2 - core_index(), 3)[place]
    return lax.axis_index("item") ^ mask


def weigh(resp, vectors):
    term = lax.dot_general(resp, vectors, NN, preferred_element_type=jnp.float32)
    return term, jnp.sum(resp.astype(jnp.float32), axis=1, keepdims=True)


def updated(total, mass, old):
    return ((total + old.astype(jnp.float32)) / (mass + 1.0)).astype(jnp.bfloat16)


def own_rows(c_ref, rows):
    return c_ref[pl.ds(pl.multiple_of(lax.axis_index("item") * rows, rows), rows), :]


def absorb(own, vectors, lse, scale, total, mass):
    resp = jnp.exp(scores(own, vectors, scale) - lse).astype(jnp.bfloat16)
    term, weight = weigh(resp, vectors)
    return (term, weight) if total is None else (total + term, mass + weight)


def own_rows(c_ref, rows):
    return c_ref[pl.ds(pl.multiple_of(lax.axis_index("item") * rows, rows), rows), :]


def begin(centroids, home, lse, other, rows, scale):
    nv, dim = home.shape
    vmem = pl.BlockSpec(memory_space=pltpu.VMEM)
    return pl.pallas_call(
        functools.partial(home_kernel, scale),
        in_specs=[vmem] * 3 + [pl.BlockSpec(memory_space=pl.ANY)],
        out_specs=[vmem] * 2,
        out_shape=[pltpu.VMEM((rows, dim), jnp.float32), pltpu.VMEM((rows, 1), jnp.float32)],
        compiler_params=pltpu.CompilerParams(vmem_limit_bytes=16 * MIB),
        cost_estimate=pl.CostEstimate(
            flops=4 * nv * rows * dim, bytes_accessed=2 * nv * dim, transcendentals=nv * rows
        ),
        name="home_block",
    )(in_vmem(centroids), in_vmem(home), lse, other)


def home_kernel(scale, c_ref, home, row, _, total, mass):
    own = own_rows(c_ref, total.shape[0])
    total[...], mass[...] = absorb(own, home[...], row[...], scale, None, None)


def early_kernel(plan, scale, c_ref, *refs):
    n = plan["pieces"]
    first = plan["first"]
    sums = weights = None
    if first:
        sums, weights, refs = refs[0][...], refs[1][...], refs[2:]
    rows, refs = refs[: plan["early"] - first], refs[plan["early"] - first :]
    pieces, arrived, outs = refs[:n], refs[n : n + plan["arrived"]], refs[n + plan["arrived"] :]
    total, mass = outs[:2]
    own = own_rows(c_ref, total.shape[0])
    if arrived:
        table, nv = outs[2], plan["nv"]
        core = core_index()
        half_lead, direct, swapped = leads(nv, core)
        quarter = nv // 4
        near, arrived = arrived[0], arrived[1:]
        table[pl.ds(half_lead, 2 * quarter), :] = near[: 2 * quarter, :]
        table[pl.ds(direct, quarter), :] = near[2 * quarter :, :]
        places = [swapped]
        half_lead, direct, swapped = leads(nv, 1 - core)
        places += [nv + half_lead, nv + half_lead + quarter, nv + direct, nv + swapped]
        for lead, ref in zip(places, arrived):
            table[pl.ds(pl.multiple_of(lead, 64), quarter), :] = ref[...]
        pieces += (table,)
    for place in range(first, plan["early"]):
        vectors = vectors_of(plan, place, pieces)
        sums, weights = absorb(own, vectors, rows[place - first][...], scale, sums, weights)
    total[...], mass[...] = sums, weights


def vectors_of(plan, place, pieces):
    operand, start = plan["blocks"][place]
    return pieces[operand][pl.ds(start, plan["nv"]), :]


def late_kernel(plan, scale, c_ref, total, mass, *refs):
    n, early = plan["pieces"], plan["early"]
    rows, refs = refs[: plan["places"] - early], refs[plan["places"] - early :]
    pieces, refs = refs[:n], refs[n:]
    sums, weights = total[...], mass[...]
    if early < plan["places"]:
        mine, other, new_ref, expo_ref, peak_ref, part_ref, block = refs
        pieces += (block,)
        half = mine.shape[0]
        block[pl.ds(pl.multiple_of(core_index() * half, half), half), :] = mine[...]
        block[pl.ds(pl.multiple_of((1 - core_index()) * half, half), half), :] = other[...]
    else:
        new_ref, expo_ref, peak_ref, part_ref = refs
    own = own_rows(c_ref, new_ref.shape[0])
    for place in range(early, plan["places"]):
        vectors = vectors_of(plan, place, pieces)
        sums, weights = absorb(own, vectors, rows[place - early][...], scale, sums, weights)
    new_ref[...] = updated(sums, weights, own)
    for place in range(plan["places"]):
        logits = scores(new_ref[...], vectors_of(plan, place, pieces), scale)
        peak = jnp.max(logits, axis=0, keepdims=True)
        expo = jnp.exp(logits - peak)
        expo_ref[place] = expo
        peak_ref[pl.ds(place, 1), :] = peak
        part_ref[pl.ds(index_of(plan, place), 1), :] = peak + jnp.log(jnp.sum(expo, axis=0, keepdims=True))


def last_kernel(plan, old_ref, expo_ref, peak_ref, parts, *refs):
    pieces, (new_ref, norm_ref, lse_ref) = refs[:-3], refs[-3:]
    lse_ref[...] = merge([parts[i] for i in range(parts.shape[0])])
    norm_ref[...] = lse_ref[pl.ds(lax.axis_index("item"), 1), :].reshape(norm_ref.shape)
    total = mass = None
    for place in range(plan["places"]):
        factor = jnp.exp(peak_ref[pl.ds(place, 1), :] - lse_ref[pl.ds(index_of(plan, place), 1), :])
        resp = (expo_ref[place] * factor).astype(jnp.bfloat16)
        term, weight = weigh(resp, vectors_of(plan, place, pieces))
        total = term if total is None else total + term
        mass = weight if mass is None else mass + weight
    new_ref[...] = updated(total, mass, old_ref[...])


def send(value, items, cents, item_mask, cent_mask=0):
    masks = item_mask if isinstance(item_mask, tuple) else (item_mask, item_mask)
    pairs = [
        (i * cents + c, (i ^ masks[c % 2]) * cents + (c ^ cent_mask)) for i in range(items) for c in range(cents)
    ]
    return lax.ppermute(value, BOTH, pairs)


def merge_cent(part, go):
    part = merge([part, go(part, 0, 1)])
    return merge([part] + [go(part, 0, mask) for mask in (2, 4, 6)])


def after(value, *others):
    vmem = pl.BlockSpec(memory_space=pltpu.VMEM)
    return pl.pallas_call(
        lambda *refs: None,
        in_specs=[vmem] + [pl.BlockSpec(memory_space=pl.ANY)] * len(others),
        out_specs=vmem,
        out_shape=pltpu.VMEM(value.shape, value.dtype),
        input_output_aliases={0: 0},
        compiler_params=pltpu.CompilerParams(vmem_limit_bytes=2 * MIB),
        name="after",
    )(in_vmem(value), *others)


def shards(vectors, centroids):
    items, cents = lax.axis_size("item"), lax.axis_size("cent")
    nv, dim = vectors.shape
    rows = centroids.shape[0] // items
    scale = BETA / math.sqrt(dim)

    def go(value, item_mask, cent_mask=0):
        return send(value, items, cents, item_mask, cent_mask)

    small = items == 4 and cents == 8
    if small:
        near = go(outgoing(vectors), (1, 2))
        home, centroids = load(vectors, centroids)
        lse = merge_cent(partial(home, centroids, scale), go)
        parts = [lse, go(lse, (1, 2)), go(lse, (2, 1)), go(lse, 3)]
        near = after(near, lse)
        quarters = [near[i : i + nv // 4] for i in range(0, near.shape[0], nv // 4)]
        swapped = go(quarters[2], 0, 2)
        far = go(near[: nv // 2], (2, 1))
        begun = begin(centroids, home, lse, parts[3], rows, scale)
        swapped = after(swapped, begun[1])
        near = [near, swapped] + [go(piece, 0, 1) for piece in quarters + [swapped]]
        pieces = [home]
        plan = dict(exchange=True, first=1, early=3, blocks=[(0, 0), (1, 0), (1, nv), (2, 0)])
    else:
        home, centroids = load(vectors, centroids)
        parts = lax.all_gather(partial(home, centroids, scale), "cent", axis=0, tiled=False)
        parts = merge([parts[i] for i in range(cents)])
        parts = lax.all_gather(parts, "item", axis=0, tiled=False)
        parts = [parts[i] for i in range(items)]
        pieces = [lax.all_gather(vectors, "item", axis=0, tiled=True)]
        near = begun = []
        plan = dict(exchange=False, first=0, early=items, blocks=[(0, i * nv) for i in range(items)])
    plan.update(nv=nv, places=items, pieces=len(pieces), arrived=len(near))
    pieces = [in_vmem(piece) for piece in pieces]
    centroids = in_vmem(centroids)

    vmem = pl.BlockSpec(memory_space=pltpu.VMEM)
    flops = 2 * nv * rows * dim
    early, late = plan["early"], items - plan["early"]
    params = pltpu.CompilerParams(vmem_limit_bytes=16 * MIB)
    tables = [pltpu.VMEM((2 * nv, dim), jnp.bfloat16)] if near else []
    total, mass, *table = pl.pallas_call(
        functools.partial(early_kernel, dict(plan), scale),
        in_specs=[vmem] * (1 + len(begun) + early - plan["first"] + len(pieces) + len(near)),
        out_specs=[vmem] * (2 + len(tables)),
        out_shape=[
            pltpu.VMEM((rows, dim), jnp.float32),
            pltpu.VMEM((rows, 1), jnp.float32),
        ]
        + tables,
        compiler_params=params,
        cost_estimate=pl.CostEstimate(flops=0, bytes_accessed=0, transcendentals=0),
        name="early_blocks",
    )(centroids, *[in_vmem(value) for value in begun], *parts[plan["first"] : early], *pieces, *[in_vmem(piece) for piece in near])
    pieces += [in_vmem(piece) for piece in table]
    plan["pieces"] = len(pieces)

    arrived = []
    if late:
        far = after(far, *parts[1:], *near[2:])
        arrived = [in_vmem(far), in_vmem(go(far, 0, 1))]
    fresh, expo, peak, part, *block = pl.pallas_call(
        functools.partial(late_kernel, dict(plan), scale),
        in_specs=[vmem] * (3 + late + len(pieces) + len(arrived)),
        out_specs=[vmem] * (4 + late),
        out_shape=[
            pltpu.VMEM((rows, dim), jnp.bfloat16),
            pltpu.VMEM((items, rows, nv), jnp.float32),
            pltpu.VMEM((items, nv), jnp.float32),
            pltpu.VMEM((items, nv), jnp.float32),
        ]
        + [pltpu.VMEM((nv, dim), jnp.bfloat16)] * late,
        compiler_params=params,
        cost_estimate=pl.CostEstimate(
            flops=(items + 2 * late) * flops,
            bytes_accessed=2 * late * nv * dim,
            transcendentals=(items + late) * nv * rows,
        ),
        name="late_blocks",
    )(centroids, in_vmem(total), in_vmem(mass), *parts[early:], *pieces, *arrived)
    pieces += [in_vmem(piece) for piece in block]

    if small:
        lse = merge_cent(part, go)
        parts = merge([lse] + [go(lse, mask) for mask in (1, 2, 3)])[None]
    else:
        gathered = lax.all_gather(part, "cent", axis=0, tiled=False)
        parts = lax.all_gather(merge([gathered[i] for i in range(cents)]), "item", axis=0, tiled=False)
    result, norm = pl.pallas_call(
        functools.partial(last_kernel, dict(plan)),
        in_specs=[vmem] * (4 + len(pieces)),
        out_specs=[vmem] * 2,
        out_shape=[
            jax.ShapeDtypeStruct((rows, dim), jnp.bfloat16),
            jax.ShapeDtypeStruct((nv,), jnp.float32),
        ],
        scratch_shapes=[pltpu.VMEM((items, nv), jnp.float32)],
        compiler_params=params,
        cost_estimate=pl.CostEstimate(flops=items * flops, bytes_accessed=2 * rows * dim, transcendentals=0),
        name="last_iteration",
    )(in_vmem(fresh), in_vmem(expo), in_vmem(peak), parts, *pieces)
    return (result, norm)


def solution(mesh):
    in_specs = (P("item", None), P("cent", None))
    out_specs = (P(("cent", "item"), None), P("item"))
    return jax.shard_map(shards, mesh=mesh, in_specs=in_specs, out_specs=out_specs, check_vma=False)
```

```python
import functools
import math

import jax
import jax.numpy as jnp
from jax import lax
from jax.experimental import pallas as pl
from jax.experimental.pallas import tpu as pltpu
from jax.sharding import PartitionSpec as P

BETA = 3.0
BOTH = ("item", "cent")
MIB = 1024 * 1024
NT = (((1,), (1,)), ((), ()))
NN = (((1,), (0,)), ((), ()))


def scores(rows, vectors, scale):
    raw = lax.dot_general(rows, vectors, NT, preferred_element_type=jnp.float32)
    sqnorm = jnp.sum(jnp.square(rows.astype(jnp.float32)), axis=1, keepdims=True)
    return scale * (raw - 0.5 * sqnorm)


def merge(parts):
    peak = functools.reduce(jnp.maximum, parts)
    terms = [jnp.exp(p - peak) for p in parts]
    while len(terms) > 1:
        terms = [sum(terms[i : i + 2]) for i in range(0, len(terms), 2)]
    return peak + jnp.log(terms[0])


def in_hbm(value):
    return pltpu.with_memory_space_constraint(value, pltpu.HBM)


def in_vmem(value):
    return pltpu.with_memory_space_constraint(value, pltpu.VMEM)


def copy_rows(pairs, sems):
    copies = [pltpu.make_async_copy(src, dst, sems.at[i]) for i, (src, dst) in enumerate(pairs)]
    for copy in copies:
        copy.start()
    for copy in copies:
        copy.wait()


def core_index():
    return lax.rem(lax.axis_index("cent"), 2)


def pair_index():
    return lax.rem(lax.axis_index("cent") // 2, 2)


def leads(nv, core):
    half, quarter = nv // 2, nv // 4
    rest = (1 - core) * half
    direct = rest + pair_index() * quarter
    swapped = rest + (1 - pair_index()) * quarter
    return [pl.multiple_of(lead, 64) for lead in (core * half, direct, swapped)]


def outgoing_kernel(v_hbm, out_ref, sems):
    half_lead, direct, _ = leads(v_hbm.shape[0], core_index())
    rows = out_ref.shape[0] // 3
    starts = (half_lead, half_lead + rows, direct)
    copy_rows(
        [
            (v_hbm.at[pl.ds(pl.multiple_of(start, 64), rows), :], out_ref.at[pl.ds(i * rows, rows), :])
            for i, start in enumerate(starts)
        ],
        sems,
    )


def outgoing(vectors):
    nv, dim = vectors.shape
    return pl.pallas_call(
        outgoing_kernel,
        in_specs=[pl.BlockSpec(memory_space=pl.ANY)],
        out_specs=pl.BlockSpec(memory_space=pltpu.VMEM),
        out_shape=pltpu.VMEM((3 * (nv // 4), dim), jnp.bfloat16),
        scratch_shapes=[pltpu.SemaphoreType.DMA((3,))],
        compiler_params=pltpu.CompilerParams(vmem_limit_bytes=2 * MIB),
        cost_estimate=pl.CostEstimate(flops=0, bytes_accessed=2 * nv * dim, transcendentals=0),
        name="outgoing",
    )(in_hbm(vectors))


def load_kernel(v_hbm, c_hbm, v_ref, c_ref, sems):
    pairs = []
    for src, dst, count in ((v_hbm, v_ref, 6), (c_hbm, c_ref, 8)):
        rows = dst.shape[0] // count
        pairs += [(src.at[pl.ds(i * rows, rows), :], dst.at[pl.ds(i * rows, rows), :]) for i in range(count)]
    copy_rows(pairs, sems)


def load(vectors, centroids):
    vmem = pl.BlockSpec(memory_space=pltpu.VMEM)
    hbm = pl.BlockSpec(memory_space=pl.ANY)
    return pl.pallas_call(
        load_kernel,
        in_specs=[hbm, hbm],
        out_specs=[vmem] * 2,
        out_shape=[pltpu.VMEM(vectors.shape, jnp.bfloat16), pltpu.VMEM(centroids.shape, jnp.bfloat16)],
        scratch_shapes=[pltpu.SemaphoreType.DMA((14,))],
        compiler_params=pltpu.CompilerParams(vmem_limit_bytes=2 * MIB),
        cost_estimate=pl.CostEstimate(
            flops=0, bytes_accessed=4 * (vectors.size + centroids.size), transcendentals=0
        ),
        name="load",
    )(in_hbm(vectors), in_hbm(centroids))


def partial_kernel(scale, rows, v_ref, c_ref, out_ref):
    parts = []
    for start in range(0, c_ref.shape[0], rows):
        logits = scores(c_ref[start : start + rows, :], v_ref[...], scale)
        peak = jnp.max(logits, axis=0, keepdims=True)
        parts.append(peak + jnp.log(jnp.sum(jnp.exp(logits - peak), axis=0, keepdims=True)))
    out_ref[...] = merge(parts)


def partial(vectors, centroids, scale):
    nv, dim = vectors.shape
    k = centroids.shape[0]
    vmem = pl.BlockSpec(memory_space=pltpu.VMEM)
    return pl.pallas_call(
        functools.partial(partial_kernel, scale, min(256, k)),
        in_specs=[vmem, vmem],
        out_specs=vmem,
        out_shape=jax.ShapeDtypeStruct((1, nv), jnp.float32),
        compiler_params=pltpu.CompilerParams(vmem_limit_bytes=12 * MIB),
        cost_estimate=pl.CostEstimate(
            flops=2 * nv * k * dim, bytes_accessed=2 * (nv + k) * dim, transcendentals=nv * k
        ),
        name="partial_lse",
    )(in_vmem(vectors), in_vmem(centroids))


def index_of(plan, place):
    if not plan["exchange"]:
        return place
    mask = (0, 1 + core_index(), 2 - core_index(), 3)[place]
    return lax.axis_index("item") ^ mask


def weigh(resp, vectors):
    term = lax.dot_general(resp, vectors, NN, preferred_element_type=jnp.float32)
    return term, jnp.sum(resp.astype(jnp.float32), axis=1, keepdims=True)


def updated(total, mass, old):
    return ((total + old.astype(jnp.float32)) / (mass + 1.0)).astype(jnp.bfloat16)


def own_rows(c_ref, rows):
    return c_ref[pl.ds(pl.multiple_of(lax.axis_index("item") * rows, rows), rows), :]


def absorb(own, vectors, lse, scale, total, mass):
    resp = jnp.exp(scores(own, vectors, scale) - lse).astype(jnp.bfloat16)
    term, weight = weigh(resp, vectors)
    return (term, weight) if total is None else (total + term, mass + weight)


def own_rows(c_ref, rows):
    return c_ref[pl.ds(pl.multiple_of(lax.axis_index("item") * rows, rows), rows), :]


def begin(centroids, home, lse, other, rows, scale):
    nv, dim = home.shape
    vmem = pl.BlockSpec(memory_space=pltpu.VMEM)
    return pl.pallas_call(
        functools.partial(home_kernel, scale),
        in_specs=[vmem] * 3 + [pl.BlockSpec(memory_space=pl.ANY)],
        out_specs=[vmem] * 2,
        out_shape=[pltpu.VMEM((rows, dim), jnp.float32), pltpu.VMEM((rows, 1), jnp.float32)],
        compiler_params=pltpu.CompilerParams(vmem_limit_bytes=16 * MIB),
        cost_estimate=pl.CostEstimate(
            flops=4 * nv * rows * dim, bytes_accessed=2 * nv * dim, transcendentals=nv * rows
        ),
        name="home_block",
    )(in_vmem(centroids), in_vmem(home), lse, other)


def home_kernel(scale, c_ref, home, row, _, total, mass):
    own = own_rows(c_ref, total.shape[0])
    total[...], mass[...] = absorb(own, home[...], row[...], scale, None, None)


def early_kernel(plan, scale, c_ref, *refs):
    n = plan["pieces"]
    first = plan["first"]
    sums = weights = None
    if first:
        sums, weights, refs = refs[0][...], refs[1][...], refs[2:]
    rows, refs = refs[: plan["early"] - first], refs[plan["early"] - first :]
    pieces, arrived, outs = refs[:n], refs[n : n + plan["arrived"]], refs[n + plan["arrived"] :]
    total, mass = outs[:2]
    own = own_rows(c_ref, total.shape[0])
    if arrived:
        table, nv = outs[2], plan["nv"]
        core = core_index()
        half_lead, direct, swapped = leads(nv, core)
        quarter = nv // 4
        near, arrived = arrived[0], arrived[1:]
        table[pl.ds(half_lead, 2 * quarter), :] = near[: 2 * quarter, :]
        table[pl.ds(direct, quarter), :] = near[2 * quarter :, :]
        places = [swapped]
        half_lead, direct, swapped = leads(nv, 1 - core)
        places += [nv + half_lead, nv + half_lead + quarter, nv + direct, nv + swapped]
        for lead, ref in zip(places, arrived):
            table[pl.ds(pl.multiple_of(lead, 64), quarter), :] = ref[...]
        pieces += (table,)
    for place in range(first, plan["early"]):
        vectors = vectors_of(plan, place, pieces)
        sums, weights = absorb(own, vectors, rows[place - first][...], scale, sums, weights)
    total[...], mass[...] = sums, weights


def vectors_of(plan, place, pieces):
    operand, start = plan["blocks"][place]
    return pieces[operand][pl.ds(start, plan["nv"]), :]


def late_kernel(plan, scale, c_ref, total, mass, *refs):
    n, early = plan["pieces"], plan["early"]
    rows, refs = refs[: plan["places"] - early], refs[plan["places"] - early :]
    pieces, refs = refs[:n], refs[n:]
    sums, weights = total[...], mass[...]
    if early < plan["places"]:
        mine, other, new_ref, expo_ref, peak_ref, part_ref, block = refs
        pieces += (block,)
        half = mine.shape[0]
        block[pl.ds(pl.multiple_of(core_index() * half, half), half), :] = mine[...]
        block[pl.ds(pl.multiple_of((1 - core_index()) * half, half), half), :] = other[...]
    else:
        new_ref, expo_ref, peak_ref, part_ref = refs
    own = own_rows(c_ref, new_ref.shape[0])
    for place in range(early, plan["places"]):
        vectors = vectors_of(plan, place, pieces)
        sums, weights = absorb(own, vectors, rows[place - early][...], scale, sums, weights)
    new_ref[...] = updated(sums, weights, own)
    for place in range(plan["places"]):
        logits = scores(new_ref[...], vectors_of(plan, place, pieces), scale)
        peak = jnp.max(logits, axis=0, keepdims=True)
        expo = jnp.exp(logits - peak)
        expo_ref[place] = expo
        peak_ref[pl.ds(place, 1), :] = peak
        part_ref[pl.ds(index_of(plan, place), 1), :] = peak + jnp.log(jnp.sum(expo, axis=0, keepdims=True))


def last_kernel(plan, old_ref, expo_ref, peak_ref, parts, *refs):
    pieces, (new_ref, norm_ref, lse_ref) = refs[:-3], refs[-3:]
    lse_ref[...] = merge([parts[i] for i in range(parts.shape[0])])
    norm_ref[...] = lse_ref[pl.ds(lax.axis_index("item"), 1), :].reshape(norm_ref.shape)
    total = mass = None
    for place in range(plan["places"]):
        factor = jnp.exp(peak_ref[pl.ds(place, 1), :] - lse_ref[pl.ds(index_of(plan, place), 1), :])
        resp = (expo_ref[place] * factor).astype(jnp.bfloat16)
        term, weight = weigh(resp, vectors_of(plan, place, pieces))
        total = term if total is None else total + term
        mass = weight if mass is None else mass + weight
    new_ref[...] = updated(total, mass, old_ref[...])


def send(value, items, cents, item_mask, cent_mask=0):
    masks = item_mask if isinstance(item_mask, tuple) else (item_mask, item_mask)
    pairs = [
        (i * cents + c, (i ^ masks[c % 2]) * cents + (c ^ cent_mask)) for i in range(items) for c in range(cents)
    ]
    return lax.ppermute(value, BOTH, pairs)


def merge_cent(part, go):
    part = merge([part, go(part, 0, 1)])
    return merge([part] + [go(part, 0, mask) for mask in (2, 4, 6)])


def after(value, *others):
    vmem = pl.BlockSpec(memory_space=pltpu.VMEM)
    return pl.pallas_call(
        lambda *refs: None,
        in_specs=[vmem] + [pl.BlockSpec(memory_space=pl.ANY)] * len(others),
        out_specs=vmem,
        out_shape=pltpu.VMEM(value.shape, value.dtype),
        input_output_aliases={0: 0},
        compiler_params=pltpu.CompilerParams(vmem_limit_bytes=2 * MIB),
        name="after",
    )(in_vmem(value), *others)


def shards(vectors, centroids):
    items, cents = lax.axis_size("item"), lax.axis_size("cent")
    nv, dim = vectors.shape
    rows = centroids.shape[0] // items
    scale = BETA / math.sqrt(dim)

    def go(value, item_mask, cent_mask=0):
        return send(value, items, cents, item_mask, cent_mask)

    small = items == 4 and cents == 8
    if small:
        near = go(outgoing(vectors), (1, 2))
        home, centroids = load(vectors, centroids)
        lse = merge_cent(partial(home, centroids, scale), go)
        near = after(near, lse)
        quarters = [near[i : i + nv // 4] for i in range(0, near.shape[0], nv // 4)]
        swapped = go(quarters[2], 0, 2)
        far = go(near[: nv // 2], (2, 1))
        crossed = [go(piece, 0, 1) for piece in quarters]
        lse = after(lse, *crossed)
        parts = [lse, go(lse, (1, 2)), go(lse, (2, 1)), go(lse, 3)]
        begun = begin(centroids, home, lse, crossed[2], rows, scale)
        swapped = after(swapped, begun[1])
        near = [near, swapped] + crossed + [go(swapped, 0, 1)]
        pieces = [home]
        plan = dict(exchange=True, first=1, early=3, blocks=[(0, 0), (1, 0), (1, nv), (2, 0)])
    else:
        home, centroids = load(vectors, centroids)
        parts = lax.all_gather(partial(home, centroids, scale), "cent", axis=0, tiled=False)
        parts = merge([parts[i] for i in range(cents)])
        parts = lax.all_gather(parts, "item", axis=0, tiled=False)
        parts = [parts[i] for i in range(items)]
        pieces = [lax.all_gather(vectors, "item", axis=0, tiled=True)]
        near = begun = []
        plan = dict(exchange=False, first=0, early=items, blocks=[(0, i * nv) for i in range(items)])
    plan.update(nv=nv, places=items, pieces=len(pieces), arrived=len(near))
    pieces = [in_vmem(piece) for piece in pieces]
    centroids = in_vmem(centroids)

    vmem = pl.BlockSpec(memory_space=pltpu.VMEM)
    flops = 2 * nv * rows * dim
    early, late = plan["early"], items - plan["early"]
    params = pltpu.CompilerParams(vmem_limit_bytes=16 * MIB)
    tables = [pltpu.VMEM((2 * nv, dim), jnp.bfloat16)] if near else []
    total, mass, *table = pl.pallas_call(
        functools.partial(early_kernel, dict(plan), scale),
        in_specs=[vmem] * (1 + len(begun) + early - plan["first"] + len(pieces) + len(near)),
        out_specs=[vmem] * (2 + len(tables)),
        out_shape=[
            pltpu.VMEM((rows, dim), jnp.float32),
            pltpu.VMEM((rows, 1), jnp.float32),
        ]
        + tables,
        compiler_params=params,
        cost_estimate=pl.CostEstimate(flops=0, bytes_accessed=0, transcendentals=0),
        name="early_blocks",
    )(centroids, *[in_vmem(value) for value in begun], *parts[plan["first"] : early], *pieces, *[in_vmem(piece) for piece in near])
    pieces += [in_vmem(piece) for piece in table]
    plan["pieces"] = len(pieces)

    arrived = []
    if late:
        far = after(far, *parts[1:], *near[2:])
        arrived = [in_vmem(far), in_vmem(go(far, 0, 1))]
    fresh, expo, peak, part, *block = pl.pallas_call(
        functools.partial(late_kernel, dict(plan), scale),
        in_specs=[vmem] * (3 + late + len(pieces) + len(arrived)),
        out_specs=[vmem] * (4 + late),
        out_shape=[
            pltpu.VMEM((rows, dim), jnp.bfloat16),
            pltpu.VMEM((items, rows, nv), jnp.float32),
            pltpu.VMEM((items, nv), jnp.float32),
            pltpu.VMEM((items, nv), jnp.float32),
        ]
        + [pltpu.VMEM((nv, dim), jnp.bfloat16)] * late,
        compiler_params=params,
        cost_estimate=pl.CostEstimate(
            flops=(items + 2 * late) * flops,
            bytes_accessed=2 * late * nv * dim,
            transcendentals=(items + late) * nv * rows,
        ),
        name="late_blocks",
    )(centroids, in_vmem(total), in_vmem(mass), *parts[early:], *pieces, *arrived)
    pieces += [in_vmem(piece) for piece in block]

    if small:
        lse = merge_cent(part, go)
        parts = merge([lse] + [go(lse, mask) for mask in (1, 2, 3)])[None]
    else:
        gathered = lax.all_gather(part, "cent", axis=0, tiled=False)
        parts = lax.all_gather(merge([gathered[i] for i in range(cents)]), "item", axis=0, tiled=False)
    result, norm = pl.pallas_call(
        functools.partial(last_kernel, dict(plan)),
        in_specs=[vmem] * (4 + len(pieces)),
        out_specs=[vmem] * 2,
        out_shape=[
            jax.ShapeDtypeStruct((rows, dim), jnp.bfloat16),
            jax.ShapeDtypeStruct((nv,), jnp.float32),
        ],
        scratch_shapes=[pltpu.VMEM((items, nv), jnp.float32)],
        compiler_params=params,
        cost_estimate=pl.CostEstimate(flops=items * flops, bytes_accessed=2 * rows * dim, transcendentals=0),
        name="last_iteration",
    )(in_vmem(fresh), in_vmem(expo), in_vmem(peak), parts, *pieces)
    return (result, norm)


def solution(mesh):
    in_specs = (P("item", None), P("cent", None))
    out_specs = (P(("cent", "item"), None), P("item"))
    return jax.shard_map(shards, mesh=mesh, in_specs=in_specs, out_specs=out_specs, check_vma=False)
```

```python
import functools
import math

import jax
import jax.numpy as jnp
from jax import lax
from jax.experimental import pallas as pl
from jax.experimental.pallas import tpu as pltpu
from jax.sharding import PartitionSpec as P

BETA = 3.0
BOTH = ("item", "cent")
MIB = 1024 * 1024
NT = (((1,), (1,)), ((), ()))
NN = (((1,), (0,)), ((), ()))


def scores(rows, vectors, scale):
    raw = lax.dot_general(rows, vectors, NT, preferred_element_type=jnp.float32)
    sqnorm = jnp.sum(jnp.square(rows.astype(jnp.float32)), axis=1, keepdims=True)
    return scale * (raw - 0.5 * sqnorm)


def merge(parts):
    peak = functools.reduce(jnp.maximum, parts)
    terms = [jnp.exp(p - peak) for p in parts]
    while len(terms) > 1:
        terms = [sum(terms[i : i + 2]) for i in range(0, len(terms), 2)]
    return peak + jnp.log(terms[0])


def in_hbm(value):
    return pltpu.with_memory_space_constraint(value, pltpu.HBM)


def in_vmem(value):
    return pltpu.with_memory_space_constraint(value, pltpu.VMEM)


def copy_rows(pairs, sems):
    copies = [pltpu.make_async_copy(src, dst, sems.at[i]) for i, (src, dst) in enumerate(pairs)]
    for copy in copies:
        copy.start()
    for copy in copies:
        copy.wait()


def core_index():
    return lax.rem(lax.axis_index("cent"), 2)


def pair_index():
    return lax.rem(lax.axis_index("cent") // 2, 2)


def leads(nv, core):
    half, quarter = nv // 2, nv // 4
    rest = (1 - core) * half
    direct = rest + pair_index() * quarter
    swapped = rest + (1 - pair_index()) * quarter
    return [pl.multiple_of(lead, 64) for lead in (core * half, direct, swapped)]


def outgoing_kernel(v_hbm, out_ref, sems):
    half_lead, direct, _ = leads(v_hbm.shape[0], core_index())
    rows = out_ref.shape[0] // 3
    starts = (half_lead, half_lead + rows, direct)
    copy_rows(
        [
            (v_hbm.at[pl.ds(pl.multiple_of(start, 64), rows), :], out_ref.at[pl.ds(i * rows, rows), :])
            for i, start in enumerate(starts)
        ],
        sems,
    )


def outgoing(vectors):
    nv, dim = vectors.shape
    return pl.pallas_call(
        outgoing_kernel,
        in_specs=[pl.BlockSpec(memory_space=pl.ANY)],
        out_specs=pl.BlockSpec(memory_space=pltpu.VMEM),
        out_shape=pltpu.VMEM((3 * (nv // 4), dim), jnp.bfloat16),
        scratch_shapes=[pltpu.SemaphoreType.DMA((3,))],
        compiler_params=pltpu.CompilerParams(vmem_limit_bytes=2 * MIB),
        cost_estimate=pl.CostEstimate(flops=0, bytes_accessed=2 * nv * dim, transcendentals=0),
        name="outgoing",
    )(in_hbm(vectors))


def load_kernel(v_hbm, c_hbm, v_ref, c_ref, sems):
    pairs = []
    for src, dst, count in ((v_hbm, v_ref, 6), (c_hbm, c_ref, 8)):
        rows = dst.shape[0] // count
        pairs += [(src.at[pl.ds(i * rows, rows), :], dst.at[pl.ds(i * rows, rows), :]) for i in range(count)]
    copy_rows(pairs, sems)


def load(vectors, centroids):
    vmem = pl.BlockSpec(memory_space=pltpu.VMEM)
    hbm = pl.BlockSpec(memory_space=pl.ANY)
    return pl.pallas_call(
        load_kernel,
        in_specs=[hbm, hbm],
        out_specs=[vmem] * 2,
        out_shape=[pltpu.VMEM(vectors.shape, jnp.bfloat16), pltpu.VMEM(centroids.shape, jnp.bfloat16)],
        scratch_shapes=[pltpu.SemaphoreType.DMA((14,))],
        compiler_params=pltpu.CompilerParams(vmem_limit_bytes=2 * MIB),
        cost_estimate=pl.CostEstimate(
            flops=0, bytes_accessed=4 * (vectors.size + centroids.size), transcendentals=0
        ),
        name="load",
    )(in_hbm(vectors), in_hbm(centroids))


def partial_kernel(scale, rows, v_ref, c_ref, out_ref):
    parts = []
    for start in range(0, c_ref.shape[0], rows):
        logits = scores(c_ref[start : start + rows, :], v_ref[...], scale)
        peak = jnp.max(logits, axis=0, keepdims=True)
        parts.append(peak + jnp.log(jnp.sum(jnp.exp(logits - peak), axis=0, keepdims=True)))
    out_ref[...] = merge(parts)


def partial(vectors, centroids, scale):
    nv, dim = vectors.shape
    k = centroids.shape[0]
    vmem = pl.BlockSpec(memory_space=pltpu.VMEM)
    return pl.pallas_call(
        functools.partial(partial_kernel, scale, min(256, k)),
        in_specs=[vmem, vmem],
        out_specs=vmem,
        out_shape=jax.ShapeDtypeStruct((1, nv), jnp.float32),
        compiler_params=pltpu.CompilerParams(vmem_limit_bytes=12 * MIB),
        cost_estimate=pl.CostEstimate(
            flops=2 * nv * k * dim, bytes_accessed=2 * (nv + k) * dim, transcendentals=nv * k
        ),
        name="partial_lse",
    )(in_vmem(vectors), in_vmem(centroids))


def index_of(plan, place):
    if not plan["exchange"]:
        return place
    mask = (0, 1 + core_index(), 2 - core_index(), 3)[place]
    return lax.axis_index("item") ^ mask


def weigh(resp, vectors):
    term = lax.dot_general(resp, vectors, NN, preferred_element_type=jnp.float32)
    return term, jnp.sum(resp.astype(jnp.float32), axis=1, keepdims=True)


def updated(total, mass, old):
    return ((total + old.astype(jnp.float32)) / (mass + 1.0)).astype(jnp.bfloat16)


def own_rows(c_ref, rows):
    return c_ref[pl.ds(pl.multiple_of(lax.axis_index("item") * rows, rows), rows), :]


def absorb(own, vectors, lse, scale, total, mass):
    resp = jnp.exp(scores(own, vectors, scale) - lse).astype(jnp.bfloat16)
    term, weight = weigh(resp, vectors)
    return (term, weight) if total is None else (total + term, mass + weight)


def own_rows(c_ref, rows):
    return c_ref[pl.ds(pl.multiple_of(lax.axis_index("item") * rows, rows), rows), :]


def begin(centroids, home, lse, other, rows, scale):
    nv, dim = home.shape
    vmem = pl.BlockSpec(memory_space=pltpu.VMEM)
    return pl.pallas_call(
        functools.partial(home_kernel, scale),
        in_specs=[vmem] * 3 + [pl.BlockSpec(memory_space=pl.ANY)],
        out_specs=[vmem] * 2,
        out_shape=[pltpu.VMEM((rows, dim), jnp.float32), pltpu.VMEM((rows, 1), jnp.float32)],
        compiler_params=pltpu.CompilerParams(vmem_limit_bytes=16 * MIB),
        cost_estimate=pl.CostEstimate(
            flops=4 * nv * rows * dim, bytes_accessed=2 * nv * dim, transcendentals=nv * rows
        ),
        name="home_block",
    )(in_vmem(centroids), in_vmem(home), lse, other)


def home_kernel(scale, c_ref, home, row, _, total, mass):
    own = own_rows(c_ref, total.shape[0])
    total[...], mass[...] = absorb(own, home[...], row[...], scale, None, None)


def early_kernel(plan, scale, c_ref, *refs):
    n = plan["pieces"]
    first = plan["first"]
    sums = weights = None
    if first:
        sums, weights, refs = refs[0][...], refs[1][...], refs[2:]
    rows, refs = refs[: plan["early"] - first], refs[plan["early"] - first :]
    pieces, arrived, outs = refs[:n], refs[n : n + plan["arrived"]], refs[n + plan["arrived"] :]
    total, mass = outs[:2]
    own = own_rows(c_ref, total.shape[0])
    if arrived:
        table, nv = outs[2], plan["nv"]
        core = core_index()
        half_lead, direct, swapped = leads(nv, core)
        quarter = nv // 4
        near, arrived = arrived[0], arrived[1:]
        table[pl.ds(half_lead, 2 * quarter), :] = near[: 2 * quarter, :]
        table[pl.ds(direct, quarter), :] = near[2 * quarter :, :]
        places = [swapped]
        half_lead, direct, swapped = leads(nv, 1 - core)
        places += [nv + half_lead, nv + half_lead + quarter, nv + direct, nv + swapped]
        for lead, ref in zip(places, arrived):
            table[pl.ds(pl.multiple_of(lead, 64), quarter), :] = ref[...]
        pieces += (table,)
    for place in range(first, plan["early"]):
        vectors = vectors_of(plan, place, pieces)
        sums, weights = absorb(own, vectors, rows[place - first][...], scale, sums, weights)
    total[...], mass[...] = sums, weights


def vectors_of(plan, place, pieces):
    operand, start = plan["blocks"][place]
    return pieces[operand][pl.ds(start, plan["nv"]), :]


def late_kernel(plan, scale, c_ref, total, mass, *refs):
    n, early = plan["pieces"], plan["early"]
    rows, refs = refs[: plan["places"] - early], refs[plan["places"] - early :]
    pieces, refs = refs[:n], refs[n:]
    sums, weights = total[...], mass[...]
    if early < plan["places"]:
        mine, other, new_ref, expo_ref, peak_ref, part_ref, block = refs
        pieces += (block,)
        half = mine.shape[0]
        block[pl.ds(pl.multiple_of(core_index() * half, half), half), :] = mine[...]
        block[pl.ds(pl.multiple_of((1 - core_index()) * half, half), half), :] = other[...]
    else:
        new_ref, expo_ref, peak_ref, part_ref = refs
    own = own_rows(c_ref, new_ref.shape[0])
    for place in range(early, plan["places"]):
        vectors = vectors_of(plan, place, pieces)
        sums, weights = absorb(own, vectors, rows[place - early][...], scale, sums, weights)
    new_ref[...] = updated(sums, weights, own)
    for place in range(plan["places"]):
        logits = scores(new_ref[...], vectors_of(plan, place, pieces), scale)
        peak = jnp.max(logits, axis=0, keepdims=True)
        expo = jnp.exp(logits - peak)
        expo_ref[place] = expo
        peak_ref[pl.ds(place, 1), :] = peak
        part_ref[pl.ds(index_of(plan, place), 1), :] = peak + jnp.log(jnp.sum(expo, axis=0, keepdims=True))


def last_kernel(plan, old_ref, expo_ref, peak_ref, parts, *refs):
    pieces, (new_ref, norm_ref, lse_ref) = refs[:-3], refs[-3:]
    lse_ref[...] = merge([parts[i] for i in range(parts.shape[0])])
    norm_ref[...] = lse_ref[pl.ds(lax.axis_index("item"), 1), :].reshape(norm_ref.shape)
    total = mass = None
    for place in range(plan["places"]):
        factor = jnp.exp(peak_ref[pl.ds(place, 1), :] - lse_ref[pl.ds(index_of(plan, place), 1), :])
        resp = (expo_ref[place] * factor).astype(jnp.bfloat16)
        term, weight = weigh(resp, vectors_of(plan, place, pieces))
        total = term if total is None else total + term
        mass = weight if mass is None else mass + weight
    new_ref[...] = updated(total, mass, old_ref[...])


def send(value, items, cents, item_mask, cent_mask=0):
    masks = item_mask if isinstance(item_mask, tuple) else (item_mask, item_mask)
    pairs = [
        (i * cents + c, (i ^ masks[c % 2]) * cents + (c ^ cent_mask)) for i in range(items) for c in range(cents)
    ]
    return lax.ppermute(value, BOTH, pairs)


def merge_cent(part, go):
    part = merge([part, go(part, 0, 1)])
    return merge([part] + [go(part, 0, mask) for mask in (2, 4, 6)])


def after(value, *others):
    vmem = pl.BlockSpec(memory_space=pltpu.VMEM)
    return pl.pallas_call(
        lambda *refs: None,
        in_specs=[vmem] + [pl.BlockSpec(memory_space=pl.ANY)] * len(others),
        out_specs=vmem,
        out_shape=pltpu.VMEM(value.shape, value.dtype),
        input_output_aliases={0: 0},
        compiler_params=pltpu.CompilerParams(vmem_limit_bytes=2 * MIB),
        name="after",
    )(in_vmem(value), *others)


def shards(vectors, centroids):
    items, cents = lax.axis_size("item"), lax.axis_size("cent")
    nv, dim = vectors.shape
    rows = centroids.shape[0] // items
    scale = BETA / math.sqrt(dim)

    def go(value, item_mask, cent_mask=0):
        return send(value, items, cents, item_mask, cent_mask)

    small = items == 4 and cents == 8
    if small:
        near = go(outgoing(vectors), (1, 2))
        home, centroids = load(vectors, centroids)
        lse = merge_cent(partial(home, centroids, scale), go)
        near = after(near, lse)
        quarters = [near[i : i + nv // 4] for i in range(0, near.shape[0], nv // 4)]
        swapped = go(quarters[2], 0, 2)
        far = go(near[: nv // 2], (2, 1))
        crossed = [go(piece, 0, 1) for piece in quarters]
        lse = after(lse, *crossed)
        parts = [lse, go(lse, (1, 2)), go(lse, (2, 1)), go(lse, 3)]
        begun = begin(centroids, home, lse, crossed[2], rows, scale)
        swapped = after(swapped, begun[1], *parts[1:])
        near = [near, swapped] + crossed + [go(swapped, 0, 1)]
        pieces = [home]
        plan = dict(exchange=True, first=1, early=3, blocks=[(0, 0), (1, 0), (1, nv), (2, 0)])
    else:
        home, centroids = load(vectors, centroids)
        parts = lax.all_gather(partial(home, centroids, scale), "cent", axis=0, tiled=False)
        parts = merge([parts[i] for i in range(cents)])
        parts = lax.all_gather(parts, "item", axis=0, tiled=False)
        parts = [parts[i] for i in range(items)]
        pieces = [lax.all_gather(vectors, "item", axis=0, tiled=True)]
        near = begun = []
        plan = dict(exchange=False, first=0, early=items, blocks=[(0, i * nv) for i in range(items)])
    plan.update(nv=nv, places=items, pieces=len(pieces), arrived=len(near))
    pieces = [in_vmem(piece) for piece in pieces]
    centroids = in_vmem(centroids)

    vmem = pl.BlockSpec(memory_space=pltpu.VMEM)
    flops = 2 * nv * rows * dim
    early, late = plan["early"], items - plan["early"]
    params = pltpu.CompilerParams(vmem_limit_bytes=16 * MIB)
    tables = [pltpu.VMEM((2 * nv, dim), jnp.bfloat16)] if near else []
    total, mass, *table = pl.pallas_call(
        functools.partial(early_kernel, dict(plan), scale),
        in_specs=[vmem] * (1 + len(begun) + early - plan["first"] + len(pieces) + len(near)),
        out_specs=[vmem] * (2 + len(tables)),
        out_shape=[
            pltpu.VMEM((rows, dim), jnp.float32),
            pltpu.VMEM((rows, 1), jnp.float32),
        ]
        + tables,
        compiler_params=params,
        cost_estimate=pl.CostEstimate(flops=0, bytes_accessed=0, transcendentals=0),
        name="early_blocks",
    )(centroids, *[in_vmem(value) for value in begun], *parts[plan["first"] : early], *pieces, *[in_vmem(piece) for piece in near])
    pieces += [in_vmem(piece) for piece in table]
    plan["pieces"] = len(pieces)

    arrived = []
    if late:
        far = after(far, *parts[1:], *near[2:])
        arrived = [in_vmem(far), in_vmem(go(far, 0, 1))]
    fresh, expo, peak, part, *block = pl.pallas_call(
        functools.partial(late_kernel, dict(plan), scale),
        in_specs=[vmem] * (3 + late + len(pieces) + len(arrived)),
        out_specs=[vmem] * (4 + late),
        out_shape=[
            pltpu.VMEM((rows, dim), jnp.bfloat16),
            pltpu.VMEM((items, rows, nv), jnp.float32),
            pltpu.VMEM((items, nv), jnp.float32),
            pltpu.VMEM((items, nv), jnp.float32),
        ]
        + [pltpu.VMEM((nv, dim), jnp.bfloat16)] * late,
        compiler_params=params,
        cost_estimate=pl.CostEstimate(
            flops=(items + 2 * late) * flops,
            bytes_accessed=2 * late * nv * dim,
            transcendentals=(items + late) * nv * rows,
        ),
        name="late_blocks",
    )(centroids, in_vmem(total), in_vmem(mass), *parts[early:], *pieces, *arrived)
    pieces += [in_vmem(piece) for piece in block]

    if small:
        lse = merge_cent(part, go)
        parts = merge([lse] + [go(lse, mask) for mask in (1, 2, 3)])[None]
    else:
        gathered = lax.all_gather(part, "cent", axis=0, tiled=False)
        parts = lax.all_gather(merge([gathered[i] for i in range(cents)]), "item", axis=0, tiled=False)
    result, norm = pl.pallas_call(
        functools.partial(last_kernel, dict(plan)),
        in_specs=[vmem] * (4 + len(pieces)),
        out_specs=[vmem] * 2,
        out_shape=[
            jax.ShapeDtypeStruct((rows, dim), jnp.bfloat16),
            jax.ShapeDtypeStruct((nv,), jnp.float32),
        ],
        scratch_shapes=[pltpu.VMEM((items, nv), jnp.float32)],
        compiler_params=params,
        cost_estimate=pl.CostEstimate(flops=items * flops, bytes_accessed=2 * rows * dim, transcendentals=0),
        name="last_iteration",
    )(in_vmem(fresh), in_vmem(expo), in_vmem(peak), parts, *pieces)
    return (result, norm)


def solution(mesh):
    in_specs = (P("item", None), P("cent", None))
    out_specs = (P(("cent", "item"), None), P("item"))
    return jax.shard_map(shards, mesh=mesh, in_specs=in_specs, out_specs=out_specs, check_vma=False)
```

```python
import functools
import math

import jax
import jax.numpy as jnp
from jax import lax
from jax.experimental import pallas as pl
from jax.experimental.pallas import tpu as pltpu
from jax.sharding import PartitionSpec as P

BETA = 3.0
BOTH = ("item", "cent")
MIB = 1024 * 1024
NT = (((1,), (1,)), ((), ()))
NN = (((1,), (0,)), ((), ()))


def scores(rows, vectors, scale):
    raw = lax.dot_general(rows, vectors, NT, preferred_element_type=jnp.float32)
    sqnorm = jnp.sum(jnp.square(rows.astype(jnp.float32)), axis=1, keepdims=True)
    return scale * (raw - 0.5 * sqnorm)


def merge(parts):
    peak = functools.reduce(jnp.maximum, parts)
    terms = [jnp.exp(p - peak) for p in parts]
    while len(terms) > 1:
        terms = [sum(terms[i : i + 2]) for i in range(0, len(terms), 2)]
    return peak + jnp.log(terms[0])


def in_hbm(value):
    return pltpu.with_memory_space_constraint(value, pltpu.HBM)


def in_vmem(value):
    return pltpu.with_memory_space_constraint(value, pltpu.VMEM)


def copy_rows(pairs, sems):
    copies = [pltpu.make_async_copy(src, dst, sems.at[i]) for i, (src, dst) in enumerate(pairs)]
    for copy in copies:
        copy.start()
    for copy in copies:
        copy.wait()


def core_index():
    return lax.rem(lax.axis_index("cent"), 2)


def pair_index():
    return lax.rem(lax.axis_index("cent") // 2, 2)


def leads(nv, core):
    half, quarter = nv // 2, nv // 4
    rest = (1 - core) * half
    direct = rest + pair_index() * quarter
    swapped = rest + (1 - pair_index()) * quarter
    return [pl.multiple_of(lead, 64) for lead in (core * half, direct, swapped)]


def outgoing_kernel(v_hbm, out_ref, sems):
    half_lead, direct, _ = leads(v_hbm.shape[0], core_index())
    rows = out_ref.shape[0] // 3
    starts = (half_lead, half_lead + rows, direct)
    copy_rows(
        [
            (v_hbm.at[pl.ds(pl.multiple_of(start, 64), rows), :], out_ref.at[pl.ds(i * rows, rows), :])
            for i, start in enumerate(starts)
        ],
        sems,
    )


def outgoing(vectors):
    nv, dim = vectors.shape
    return pl.pallas_call(
        outgoing_kernel,
        in_specs=[pl.BlockSpec(memory_space=pl.ANY)],
        out_specs=pl.BlockSpec(memory_space=pltpu.VMEM),
        out_shape=pltpu.VMEM((3 * (nv // 4), dim), jnp.bfloat16),
        scratch_shapes=[pltpu.SemaphoreType.DMA((3,))],
        compiler_params=pltpu.CompilerParams(vmem_limit_bytes=2 * MIB),
        cost_estimate=pl.CostEstimate(flops=0, bytes_accessed=2 * nv * dim, transcendentals=0),
        name="outgoing",
    )(in_hbm(vectors))


def load_kernel(v_hbm, c_hbm, v_ref, c_ref, sems):
    pairs = []
    for src, dst, count in ((v_hbm, v_ref, 6), (c_hbm, c_ref, 8)):
        rows = dst.shape[0] // count
        pairs += [(src.at[pl.ds(i * rows, rows), :], dst.at[pl.ds(i * rows, rows), :]) for i in range(count)]
    copy_rows(pairs, sems)


def load(vectors, centroids):
    vmem = pl.BlockSpec(memory_space=pltpu.VMEM)
    hbm = pl.BlockSpec(memory_space=pl.ANY)
    return pl.pallas_call(
        load_kernel,
        in_specs=[hbm, hbm],
        out_specs=[vmem] * 2,
        out_shape=[pltpu.VMEM(vectors.shape, jnp.bfloat16), pltpu.VMEM(centroids.shape, jnp.bfloat16)],
        scratch_shapes=[pltpu.SemaphoreType.DMA((14,))],
        compiler_params=pltpu.CompilerParams(vmem_limit_bytes=2 * MIB),
        cost_estimate=pl.CostEstimate(
            flops=0, bytes_accessed=4 * (vectors.size + centroids.size), transcendentals=0
        ),
        name="load",
    )(in_hbm(vectors), in_hbm(centroids))


def partial_kernel(scale, rows, v_ref, c_ref, out_ref):
    parts = []
    for start in range(0, c_ref.shape[0], rows):
        logits = scores(c_ref[start : start + rows, :], v_ref[...], scale)
        peak = jnp.max(logits, axis=0, keepdims=True)
        parts.append(peak + jnp.log(jnp.sum(jnp.exp(logits - peak), axis=0, keepdims=True)))
    out_ref[...] = merge(parts)


def partial(vectors, centroids, scale):
    nv, dim = vectors.shape
    k = centroids.shape[0]
    vmem = pl.BlockSpec(memory_space=pltpu.VMEM)
    return pl.pallas_call(
        functools.partial(partial_kernel, scale, min(256, k)),
        in_specs=[vmem, vmem],
        out_specs=vmem,
        out_shape=jax.ShapeDtypeStruct((1, nv), jnp.float32),
        compiler_params=pltpu.CompilerParams(vmem_limit_bytes=12 * MIB),
        cost_estimate=pl.CostEstimate(
            flops=2 * nv * k * dim, bytes_accessed=2 * (nv + k) * dim, transcendentals=nv * k
        ),
        name="partial_lse",
    )(in_vmem(vectors), in_vmem(centroids))


def index_of(plan, place):
    if not plan["exchange"]:
        return place
    mask = (0, 1 + core_index(), 2 - core_index(), 3)[place]
    return lax.axis_index("item") ^ mask


def weigh(resp, vectors):
    term = lax.dot_general(resp, vectors, NN, preferred_element_type=jnp.float32)
    return term, jnp.sum(resp.astype(jnp.float32), axis=1, keepdims=True)


def updated(total, mass, old):
    return ((total + old.astype(jnp.float32)) / (mass + 1.0)).astype(jnp.bfloat16)


def own_rows(c_ref, rows):
    return c_ref[pl.ds(pl.multiple_of(lax.axis_index("item") * rows, rows), rows), :]


def absorb(own, vectors, lse, scale, total, mass):
    resp = jnp.exp(scores(own, vectors, scale) - lse).astype(jnp.bfloat16)
    term, weight = weigh(resp, vectors)
    return (term, weight) if total is None else (total + term, mass + weight)


def own_rows(c_ref, rows):
    return c_ref[pl.ds(pl.multiple_of(lax.axis_index("item") * rows, rows), rows), :]


def begin(centroids, home, lse, other, rows, scale):
    nv, dim = home.shape
    vmem = pl.BlockSpec(memory_space=pltpu.VMEM)
    return pl.pallas_call(
        functools.partial(home_kernel, scale),
        in_specs=[vmem] * 3 + [pl.BlockSpec(memory_space=pl.ANY)],
        out_specs=[vmem] * 2,
        out_shape=[pltpu.VMEM((rows, dim), jnp.float32), pltpu.VMEM((rows, 1), jnp.float32)],
        compiler_params=pltpu.CompilerParams(vmem_limit_bytes=16 * MIB),
        cost_estimate=pl.CostEstimate(
            flops=4 * nv * rows * dim, bytes_accessed=2 * nv * dim, transcendentals=nv * rows
        ),
        name="home_block",
    )(in_vmem(centroids), in_vmem(home), lse, other)


def home_kernel(scale, c_ref, home, row, _, total, mass):
    own = own_rows(c_ref, total.shape[0])
    total[...], mass[...] = absorb(own, home[...], row[...], scale, None, None)


def early_kernel(plan, scale, c_ref, *refs):
    n = plan["pieces"]
    first = plan["first"]
    sums = weights = None
    if first:
        sums, weights, refs = refs[0][...], refs[1][...], refs[2:]
    rows, refs = refs[: plan["early"] - first], refs[plan["early"] - first :]
    pieces, arrived, outs = refs[:n], refs[n : n + plan["arrived"]], refs[n + plan["arrived"] :]
    total, mass = outs[:2]
    own = own_rows(c_ref, total.shape[0])
    if arrived:
        table, nv = outs[2], plan["nv"]
        core = core_index()
        half_lead, direct, swapped = leads(nv, core)
        quarter = nv // 4
        near, arrived = arrived[0], arrived[1:]
        table[pl.ds(half_lead, 2 * quarter), :] = near[: 2 * quarter, :]
        table[pl.ds(direct, quarter), :] = near[2 * quarter :, :]
        places = [swapped]
        half_lead, direct, swapped = leads(nv, 1 - core)
        places += [nv + half_lead, nv + half_lead + quarter, nv + direct, nv + swapped]
        for lead, ref in zip(places, arrived):
            table[pl.ds(pl.multiple_of(lead, 64), quarter), :] = ref[...]
        pieces += (table,)
    for place in range(first, plan["early"]):
        vectors = vectors_of(plan, place, pieces)
        sums, weights = absorb(own, vectors, rows[place - first][...], scale, sums, weights)
    total[...], mass[...] = sums, weights


def vectors_of(plan, place, pieces):
    operand, start = plan["blocks"][place]
    return pieces[operand][pl.ds(start, plan["nv"]), :]


def late_kernel(plan, scale, c_ref, total, mass, *refs):
    n, early = plan["pieces"], plan["early"]
    rows, refs = refs[: plan["places"] - early], refs[plan["places"] - early :]
    pieces, refs = refs[:n], refs[n:]
    sums, weights = total[...], mass[...]
    if early < plan["places"]:
        mine, other, new_ref, expo_ref, peak_ref, part_ref, block = refs
        pieces += (block,)
        half = mine.shape[0]
        block[pl.ds(pl.multiple_of(core_index() * half, half), half), :] = mine[...]
        block[pl.ds(pl.multiple_of((1 - core_index()) * half, half), half), :] = other[...]
    else:
        new_ref, expo_ref, peak_ref, part_ref = refs
    own = own_rows(c_ref, new_ref.shape[0])
    for place in range(early, plan["places"]):
        vectors = vectors_of(plan, place, pieces)
        sums, weights = absorb(own, vectors, rows[place - early][...], scale, sums, weights)
    new_ref[...] = updated(sums, weights, own)
    for place in range(plan["places"]):
        logits = scores(new_ref[...], vectors_of(plan, place, pieces), scale)
        peak = jnp.max(logits, axis=0, keepdims=True)
        expo = jnp.exp(logits - peak)
        expo_ref[place] = expo
        peak_ref[pl.ds(place, 1), :] = peak
        part_ref[pl.ds(index_of(plan, place), 1), :] = peak + jnp.log(jnp.sum(expo, axis=0, keepdims=True))


def last_kernel(plan, old_ref, expo_ref, peak_ref, parts, *refs):
    pieces, (new_ref, norm_ref, lse_ref) = refs[:-3], refs[-3:]
    lse_ref[...] = merge([parts[i] for i in range(parts.shape[0])])
    norm_ref[...] = lse_ref[pl.ds(lax.axis_index("item"), 1), :].reshape(norm_ref.shape)
    total = mass = None
    for place in range(plan["places"]):
        factor = jnp.exp(peak_ref[pl.ds(place, 1), :] - lse_ref[pl.ds(index_of(plan, place), 1), :])
        resp = (expo_ref[place] * factor).astype(jnp.bfloat16)
        term, weight = weigh(resp, vectors_of(plan, place, pieces))
        total = term if total is None else total + term
        mass = weight if mass is None else mass + weight
    new_ref[...] = updated(total, mass, old_ref[...])


def send(value, items, cents, item_mask, cent_mask=0):
    masks = item_mask if isinstance(item_mask, tuple) else (item_mask, item_mask)
    pairs = [
        (i * cents + c, (i ^ masks[c % 2]) * cents + (c ^ cent_mask)) for i in range(items) for c in range(cents)
    ]
    return lax.ppermute(value, BOTH, pairs)


def merge_cent(part, go):
    part = merge([part, go(part, 0, 1)])
    return merge([part] + [go(part, 0, mask) for mask in (2, 4, 6)])


def after(value, *others):
    vmem = pl.BlockSpec(memory_space=pltpu.VMEM)
    return pl.pallas_call(
        lambda *refs: None,
        in_specs=[vmem] + [pl.BlockSpec(memory_space=pl.ANY)] * len(others),
        out_specs=vmem,
        out_shape=pltpu.VMEM(value.shape, value.dtype),
        input_output_aliases={0: 0},
        compiler_params=pltpu.CompilerParams(vmem_limit_bytes=2 * MIB),
        name="after",
    )(in_vmem(value), *others)


def shards(vectors, centroids):
    items, cents = lax.axis_size("item"), lax.axis_size("cent")
    nv, dim = vectors.shape
    rows = centroids.shape[0] // items
    scale = BETA / math.sqrt(dim)

    def go(value, item_mask, cent_mask=0):
        return send(value, items, cents, item_mask, cent_mask)

    small = items == 4 and cents == 8
    if small:
        near = go(outgoing(vectors), (1, 2))
        home, centroids = load(vectors, centroids)
        lse = merge_cent(partial(home, centroids, scale), go)
        near = after(near, lse)
        quarters = [near[i : i + nv // 4] for i in range(0, near.shape[0], nv // 4)]
        swapped = go(quarters[2], 0, 2)
        far = go(near[: nv // 2], (2, 1))
        crossed = [go(piece, 0, 1) for piece in quarters]
        lse = after(lse, *crossed)
        parts = [lse, go(lse, (1, 2)), go(lse, (2, 1)), go(lse, 3)]
        begun = begin(centroids, home, lse, parts[3], rows, scale)
        swapped = after(swapped, begun[1])
        near = [near, swapped] + crossed + [go(swapped, 0, 1)]
        pieces = [home]
        plan = dict(exchange=True, first=1, early=3, blocks=[(0, 0), (1, 0), (1, nv), (2, 0)])
    else:
        home, centroids = load(vectors, centroids)
        parts = lax.all_gather(partial(home, centroids, scale), "cent", axis=0, tiled=False)
        parts = merge([parts[i] for i in range(cents)])
        parts = lax.all_gather(parts, "item", axis=0, tiled=False)
        parts = [parts[i] for i in range(items)]
        pieces = [lax.all_gather(vectors, "item", axis=0, tiled=True)]
        near = begun = []
        plan = dict(exchange=False, first=0, early=items, blocks=[(0, i * nv) for i in range(items)])
    plan.update(nv=nv, places=items, pieces=len(pieces), arrived=len(near))
    pieces = [in_vmem(piece) for piece in pieces]
    centroids = in_vmem(centroids)

    vmem = pl.BlockSpec(memory_space=pltpu.VMEM)
    flops = 2 * nv * rows * dim
    early, late = plan["early"], items - plan["early"]
    params = pltpu.CompilerParams(vmem_limit_bytes=16 * MIB)
    tables = [pltpu.VMEM((2 * nv, dim), jnp.bfloat16)] if near else []
    total, mass, *table = pl.pallas_call(
        functools.partial(early_kernel, dict(plan), scale),
        in_specs=[vmem] * (1 + len(begun) + early - plan["first"] + len(pieces) + len(near)),
        out_specs=[vmem] * (2 + len(tables)),
        out_shape=[
            pltpu.VMEM((rows, dim), jnp.float32),
            pltpu.VMEM((rows, 1), jnp.float32),
        ]
        + tables,
        compiler_params=params,
        cost_estimate=pl.CostEstimate(flops=0, bytes_accessed=0, transcendentals=0),
        name="early_blocks",
    )(centroids, *[in_vmem(value) for value in begun], *parts[plan["first"] : early], *pieces, *[in_vmem(piece) for piece in near])
    pieces += [in_vmem(piece) for piece in table]
    plan["pieces"] = len(pieces)

    arrived = []
    if late:
        far = after(far, *parts[1:], *near[2:])
        arrived = [in_vmem(far), in_vmem(go(far, 0, 1))]
    fresh, expo, peak, part, *block = pl.pallas_call(
        functools.partial(late_kernel, dict(plan), scale),
        in_specs=[vmem] * (3 + late + len(pieces) + len(arrived)),
        out_specs=[vmem] * (4 + late),
        out_shape=[
            pltpu.VMEM((rows, dim), jnp.bfloat16),
            pltpu.VMEM((items, rows, nv), jnp.float32),
            pltpu.VMEM((items, nv), jnp.float32),
            pltpu.VMEM((items, nv), jnp.float32),
        ]
        + [pltpu.VMEM((nv, dim), jnp.bfloat16)] * late,
        compiler_params=params,
        cost_estimate=pl.CostEstimate(
            flops=(items + 2 * late) * flops,
            bytes_accessed=2 * late * nv * dim,
            transcendentals=(items + late) * nv * rows,
        ),
        name="late_blocks",
    )(centroids, in_vmem(total), in_vmem(mass), *parts[early:], *pieces, *arrived)
    pieces += [in_vmem(piece) for piece in block]

    if small:
        lse = merge_cent(part, go)
        parts = merge([lse] + [go(lse, mask) for mask in (1, 2, 3)])[None]
    else:
        gathered = lax.all_gather(part, "cent", axis=0, tiled=False)
        parts = lax.all_gather(merge([gathered[i] for i in range(cents)]), "item", axis=0, tiled=False)
    result, norm = pl.pallas_call(
        functools.partial(last_kernel, dict(plan)),
        in_specs=[vmem] * (4 + len(pieces)),
        out_specs=[vmem] * 2,
        out_shape=[
            jax.ShapeDtypeStruct((rows, dim), jnp.bfloat16),
            jax.ShapeDtypeStruct((nv,), jnp.float32),
        ],
        scratch_shapes=[pltpu.VMEM((items, nv), jnp.float32)],
        compiler_params=params,
        cost_estimate=pl.CostEstimate(flops=items * flops, bytes_accessed=2 * rows * dim, transcendentals=0),
        name="last_iteration",
    )(in_vmem(fresh), in_vmem(expo), in_vmem(peak), parts, *pieces)
    return (result, norm)


def solution(mesh):
    in_specs = (P("item", None), P("cent", None))
    out_specs = (P(("cent", "item"), None), P("item"))
    return jax.shard_map(shards, mesh=mesh, in_specs=in_specs, out_specs=out_specs, check_vma=False)
```

```python
import functools
import math

import jax
import jax.numpy as jnp
from jax import lax
from jax.experimental import pallas as pl
from jax.experimental.pallas import tpu as pltpu
from jax.sharding import PartitionSpec as P

BETA = 3.0
BOTH = ("item", "cent")
MIB = 1024 * 1024
NT = (((1,), (1,)), ((), ()))
NN = (((1,), (0,)), ((), ()))


def scores(rows, vectors, scale):
    raw = lax.dot_general(rows, vectors, NT, preferred_element_type=jnp.float32)
    sqnorm = jnp.sum(jnp.square(rows.astype(jnp.float32)), axis=1, keepdims=True)
    return scale * (raw - 0.5 * sqnorm)


def merge(parts):
    peak = functools.reduce(jnp.maximum, parts)
    terms = [jnp.exp(p - peak) for p in parts]
    while len(terms) > 1:
        terms = [sum(terms[i : i + 2]) for i in range(0, len(terms), 2)]
    return peak + jnp.log(terms[0])


def in_hbm(value):
    return pltpu.with_memory_space_constraint(value, pltpu.HBM)


def in_vmem(value):
    return pltpu.with_memory_space_constraint(value, pltpu.VMEM)


def copy_rows(pairs, sems):
    copies = [pltpu.make_async_copy(src, dst, sems.at[i]) for i, (src, dst) in enumerate(pairs)]
    for copy in copies:
        copy.start()
    for copy in copies:
        copy.wait()


def core_index():
    return lax.rem(lax.axis_index("cent"), 2)


def pair_index():
    return lax.rem(lax.axis_index("cent") // 2, 2)


def leads(nv, core):
    half, quarter = nv // 2, nv // 4
    rest = (1 - core) * half
    direct = rest + pair_index() * quarter
    swapped = rest + (1 - pair_index()) * quarter
    return [pl.multiple_of(lead, 64) for lead in (core * half, direct, swapped)]


def outgoing_kernel(v_hbm, out_ref, sems):
    half_lead, direct, _ = leads(v_hbm.shape[0], core_index())
    rows = out_ref.shape[0] // 3
    starts = (half_lead, half_lead + rows, direct)
    copy_rows(
        [
            (v_hbm.at[pl.ds(pl.multiple_of(start, 64), rows), :], out_ref.at[pl.ds(i * rows, rows), :])
            for i, start in enumerate(starts)
        ],
        sems,
    )


def outgoing(vectors):
    nv, dim = vectors.shape
    return pl.pallas_call(
        outgoing_kernel,
        in_specs=[pl.BlockSpec(memory_space=pl.ANY)],
        out_specs=pl.BlockSpec(memory_space=pltpu.VMEM),
        out_shape=pltpu.VMEM((3 * (nv // 4), dim), jnp.bfloat16),
        scratch_shapes=[pltpu.SemaphoreType.DMA((3,))],
        compiler_params=pltpu.CompilerParams(vmem_limit_bytes=2 * MIB),
        cost_estimate=pl.CostEstimate(flops=0, bytes_accessed=2 * nv * dim, transcendentals=0),
        name="outgoing",
    )(in_hbm(vectors))


def load_kernel(v_hbm, c_hbm, v_ref, c_ref, sems):
    pairs = []
    for src, dst, count in ((v_hbm, v_ref, 6), (c_hbm, c_ref, 8)):
        rows = dst.shape[0] // count
        pairs += [(src.at[pl.ds(i * rows, rows), :], dst.at[pl.ds(i * rows, rows), :]) for i in range(count)]
    copy_rows(pairs, sems)


def load(vectors, centroids):
    vmem = pl.BlockSpec(memory_space=pltpu.VMEM)
    hbm = pl.BlockSpec(memory_space=pl.ANY)
    return pl.pallas_call(
        load_kernel,
        in_specs=[hbm, hbm],
        out_specs=[vmem] * 2,
        out_shape=[pltpu.VMEM(vectors.shape, jnp.bfloat16), pltpu.VMEM(centroids.shape, jnp.bfloat16)],
        scratch_shapes=[pltpu.SemaphoreType.DMA((14,))],
        compiler_params=pltpu.CompilerParams(vmem_limit_bytes=2 * MIB),
        cost_estimate=pl.CostEstimate(
            flops=0, bytes_accessed=4 * (vectors.size + centroids.size), transcendentals=0
        ),
        name="load",
    )(in_hbm(vectors), in_hbm(centroids))


def partial_kernel(scale, rows, v_ref, c_ref, out_ref):
    parts = []
    for start in range(0, c_ref.shape[0], rows):
        logits = scores(c_ref[start : start + rows, :], v_ref[...], scale)
        peak = jnp.max(logits, axis=0, keepdims=True)
        parts.append(peak + jnp.log(jnp.sum(jnp.exp(logits - peak), axis=0, keepdims=True)))
    out_ref[...] = merge(parts)


def partial(vectors, centroids, scale):
    nv, dim = vectors.shape
    k = centroids.shape[0]
    vmem = pl.BlockSpec(memory_space=pltpu.VMEM)
    return pl.pallas_call(
        functools.partial(partial_kernel, scale, min(256, k)),
        in_specs=[vmem, vmem],
        out_specs=vmem,
        out_shape=jax.ShapeDtypeStruct((1, nv), jnp.float32),
        compiler_params=pltpu.CompilerParams(vmem_limit_bytes=12 * MIB),
        cost_estimate=pl.CostEstimate(
            flops=2 * nv * k * dim, bytes_accessed=2 * (nv + k) * dim, transcendentals=nv * k
        ),
        name="partial_lse",
    )(in_vmem(vectors), in_vmem(centroids))


def index_of(plan, place):
    if not plan["exchange"]:
        return place
    mask = (0, 1 + core_index(), 2 - core_index(), 3)[place]
    return lax.axis_index("item") ^ mask


def weigh(resp, vectors):
    term = lax.dot_general(resp, vectors, NN, preferred_element_type=jnp.float32)
    return term, jnp.sum(resp.astype(jnp.float32), axis=1, keepdims=True)


def updated(total, mass, old):
    return ((total + old.astype(jnp.float32)) / (mass + 1.0)).astype(jnp.bfloat16)


def own_rows(c_ref, rows):
    return c_ref[pl.ds(pl.multiple_of(lax.axis_index("item") * rows, rows), rows), :]


def absorb(own, vectors, lse, scale, total, mass):
    resp = jnp.exp(scores(own, vectors, scale) - lse).astype(jnp.bfloat16)
    term, weight = weigh(resp, vectors)
    return (term, weight) if total is None else (total + term, mass + weight)


def own_rows(c_ref, rows):
    return c_ref[pl.ds(pl.multiple_of(lax.axis_index("item") * rows, rows), rows), :]


def begin(centroids, home, lse, other, rows, scale):
    nv, dim = home.shape
    vmem = pl.BlockSpec(memory_space=pltpu.VMEM)
    return pl.pallas_call(
        functools.partial(home_kernel, scale),
        in_specs=[vmem] * 3 + [pl.BlockSpec(memory_space=pl.ANY)],
        out_specs=[vmem] * 2,
        out_shape=[pltpu.VMEM((rows, dim), jnp.float32), pltpu.VMEM((rows, 1), jnp.float32)],
        compiler_params=pltpu.CompilerParams(vmem_limit_bytes=16 * MIB),
        cost_estimate=pl.CostEstimate(
            flops=4 * nv * rows * dim, bytes_accessed=2 * nv * dim, transcendentals=nv * rows
        ),
        name="home_block",
    )(in_vmem(centroids), in_vmem(home), lse, other)


def near_kernel(scale, c_ref, near, last, row, total, mass, table, new_total, new_mass):
    half_lead, direct, swapped = leads(table.shape[0], core_index())
    quarter = last.shape[0]
    table[pl.ds(half_lead, 2 * quarter), :] = near[: 2 * quarter, :]
    table[pl.ds(direct, quarter), :] = near[2 * quarter :, :]
    table[pl.ds(swapped, quarter), :] = last[...]
    own = own_rows(c_ref, total.shape[0])
    new_total[...], new_mass[...] = absorb(own, table[...], row[...], scale, total[...], mass[...])


def add_near(centroids, near, swapped, row, begun, scale):
    quarter, dim = swapped.shape
    rows = begun[0].shape[0]
    vmem = pl.BlockSpec(memory_space=pltpu.VMEM)
    return pl.pallas_call(
        functools.partial(near_kernel, scale),
        in_specs=[vmem] * 6,
        out_specs=[vmem] * 3,
        out_shape=[
            pltpu.VMEM((4 * quarter, dim), jnp.bfloat16),
            pltpu.VMEM((rows, dim), jnp.float32),
            pltpu.VMEM((rows, 1), jnp.float32),
        ],
        compiler_params=pltpu.CompilerParams(vmem_limit_bytes=16 * MIB),
        cost_estimate=pl.CostEstimate(
            flops=16 * quarter * rows * dim, bytes_accessed=8 * quarter * dim, transcendentals=4 * quarter * rows
        ),
        name="near_block",
    )(in_vmem(centroids), in_vmem(near), in_vmem(swapped), row, *[in_vmem(value) for value in begun])


def home_kernel(scale, c_ref, home, row, _, total, mass):
    own = own_rows(c_ref, total.shape[0])
    total[...], mass[...] = absorb(own, home[...], row[...], scale, None, None)


def early_kernel(plan, scale, c_ref, *refs):
    n = plan["pieces"]
    first = plan["first"]
    sums = weights = None
    if first:
        sums, weights, refs = refs[0][...], refs[1][...], refs[2:]
    rows, refs = refs[: plan["early"] - first], refs[plan["early"] - first :]
    pieces, arrived, outs = refs[:n], refs[n : n + plan["arrived"]], refs[n + plan["arrived"] :]
    total, mass = outs[:2]
    own = own_rows(c_ref, total.shape[0])
    if arrived:
        table, nv = outs[2], plan["nv"]
        quarter = nv // 4
        half_lead, direct, swapped = leads(nv, 1 - core_index())
        for lead, ref in zip((half_lead, half_lead + quarter, direct, swapped), arrived):
            table[pl.ds(pl.multiple_of(lead, 64), quarter), :] = ref[...]
        pieces += (table,)
    for place in range(first, plan["early"]):
        vectors = vectors_of(plan, place, pieces)
        sums, weights = absorb(own, vectors, rows[place - first][...], scale, sums, weights)
    total[...], mass[...] = sums, weights


def vectors_of(plan, place, pieces):
    operand, start = plan["blocks"][place]
    return pieces[operand][pl.ds(start, plan["nv"]), :]


def late_kernel(plan, scale, c_ref, total, mass, *refs):
    n, early = plan["pieces"], plan["early"]
    rows, refs = refs[: plan["places"] - early], refs[plan["places"] - early :]
    pieces, refs = refs[:n], refs[n:]
    sums, weights = total[...], mass[...]
    if early < plan["places"]:
        mine, other, new_ref, expo_ref, peak_ref, part_ref, block = refs
        pieces += (block,)
        half = mine.shape[0]
        block[pl.ds(pl.multiple_of(core_index() * half, half), half), :] = mine[...]
        block[pl.ds(pl.multiple_of((1 - core_index()) * half, half), half), :] = other[...]
    else:
        new_ref, expo_ref, peak_ref, part_ref = refs
    own = own_rows(c_ref, new_ref.shape[0])
    for place in range(early, plan["places"]):
        vectors = vectors_of(plan, place, pieces)
        sums, weights = absorb(own, vectors, rows[place - early][...], scale, sums, weights)
    new_ref[...] = updated(sums, weights, own)
    for place in range(plan["places"]):
        logits = scores(new_ref[...], vectors_of(plan, place, pieces), scale)
        peak = jnp.max(logits, axis=0, keepdims=True)
        expo = jnp.exp(logits - peak)
        expo_ref[place] = expo
        peak_ref[pl.ds(place, 1), :] = peak
        part_ref[pl.ds(index_of(plan, place), 1), :] = peak + jnp.log(jnp.sum(expo, axis=0, keepdims=True))


def last_kernel(plan, old_ref, expo_ref, peak_ref, parts, *refs):
    pieces, (new_ref, norm_ref, lse_ref) = refs[:-3], refs[-3:]
    lse_ref[...] = merge([parts[i] for i in range(parts.shape[0])])
    norm_ref[...] = lse_ref[pl.ds(lax.axis_index("item"), 1), :].reshape(norm_ref.shape)
    total = mass = None
    for place in range(plan["places"]):
        factor = jnp.exp(peak_ref[pl.ds(place, 1), :] - lse_ref[pl.ds(index_of(plan, place), 1), :])
        resp = (expo_ref[place] * factor).astype(jnp.bfloat16)
        term, weight = weigh(resp, vectors_of(plan, place, pieces))
        total = term if total is None else total + term
        mass = weight if mass is None else mass + weight
    new_ref[...] = updated(total, mass, old_ref[...])


def send(value, items, cents, item_mask, cent_mask=0):
    masks = item_mask if isinstance(item_mask, tuple) else (item_mask, item_mask)
    pairs = [
        (i * cents + c, (i ^ masks[c % 2]) * cents + (c ^ cent_mask)) for i in range(items) for c in range(cents)
    ]
    return lax.ppermute(value, BOTH, pairs)


def merge_cent(part, go):
    part = merge([part, go(part, 0, 1)])
    return merge([part] + [go(part, 0, mask) for mask in (2, 4, 6)])


def after(value, *others):
    vmem = pl.BlockSpec(memory_space=pltpu.VMEM)
    return pl.pallas_call(
        lambda *refs: None,
        in_specs=[vmem] + [pl.BlockSpec(memory_space=pl.ANY)] * len(others),
        out_specs=vmem,
        out_shape=pltpu.VMEM(value.shape, value.dtype),
        input_output_aliases={0: 0},
        compiler_params=pltpu.CompilerParams(vmem_limit_bytes=2 * MIB),
        name="after",
    )(in_vmem(value), *others)


def shards(vectors, centroids):
    items, cents = lax.axis_size("item"), lax.axis_size("cent")
    nv, dim = vectors.shape
    rows = centroids.shape[0] // items
    scale = BETA / math.sqrt(dim)

    def go(value, item_mask, cent_mask=0):
        return send(value, items, cents, item_mask, cent_mask)

    small = items == 4 and cents == 8
    if small:
        near = go(outgoing(vectors), (1, 2))
        home, centroids = load(vectors, centroids)
        lse = merge_cent(partial(home, centroids, scale), go)
        near = after(near, lse)
        quarters = [near[i : i + nv // 4] for i in range(0, near.shape[0], nv // 4)]
        swapped = go(quarters[2], 0, 2)
        far = go(near[: nv // 2], (2, 1))
        crossed = [go(piece, 0, 1) for piece in quarters]
        lse = after(lse, *crossed)
        parts = [lse, go(lse, (1, 2)), go(lse, (2, 1)), go(lse, 3)]
        begun = begin(centroids, home, lse, crossed[2], rows, scale)
        swapped = after(swapped, begun[1], *parts[1:])
        crossed = crossed + [go(swapped, 0, 1)]
        near, *begun = add_near(centroids, near, swapped, parts[1], begun, scale)
        home, near = [home, near], crossed
        pieces = home
        plan = dict(exchange=True, first=2, early=3, blocks=[(i, 0) for i in range(4)])
    else:
        home, centroids = load(vectors, centroids)
        parts = lax.all_gather(partial(home, centroids, scale), "cent", axis=0, tiled=False)
        parts = merge([parts[i] for i in range(cents)])
        parts = lax.all_gather(parts, "item", axis=0, tiled=False)
        parts = [parts[i] for i in range(items)]
        pieces = [lax.all_gather(vectors, "item", axis=0, tiled=True)]
        near = begun = []
        plan = dict(exchange=False, first=0, early=items, blocks=[(0, i * nv) for i in range(items)])
    plan.update(nv=nv, places=items, pieces=len(pieces), arrived=len(near))
    pieces = [in_vmem(piece) for piece in pieces]
    centroids = in_vmem(centroids)

    vmem = pl.BlockSpec(memory_space=pltpu.VMEM)
    flops = 2 * nv * rows * dim
    early, late = plan["early"], items - plan["early"]
    params = pltpu.CompilerParams(vmem_limit_bytes=16 * MIB)
    tables = [pltpu.VMEM((nv, dim), jnp.bfloat16)] if near else []
    total, mass, *table = pl.pallas_call(
        functools.partial(early_kernel, dict(plan), scale),
        in_specs=[vmem] * (1 + len(begun) + early - plan["first"] + len(pieces) + len(near)),
        out_specs=[vmem] * (2 + len(tables)),
        out_shape=[
            pltpu.VMEM((rows, dim), jnp.float32),
            pltpu.VMEM((rows, 1), jnp.float32),
        ]
        + tables,
        compiler_params=params,
        cost_estimate=pl.CostEstimate(flops=0, bytes_accessed=0, transcendentals=0),
        name="early_blocks",
    )(centroids, *[in_vmem(value) for value in begun], *parts[plan["first"] : early], *pieces, *[in_vmem(piece) for piece in near])
    pieces += [in_vmem(piece) for piece in table]
    plan["pieces"] = len(pieces)

    arrived = []
    if late:
        far = after(far, swapped)
        arrived = [in_vmem(far), in_vmem(go(far, 0, 1))]
    fresh, expo, peak, part, *block = pl.pallas_call(
        functools.partial(late_kernel, dict(plan), scale),
        in_specs=[vmem] * (3 + late + len(pieces) + len(arrived)),
        out_specs=[vmem] * (4 + late),
        out_shape=[
            pltpu.VMEM((rows, dim), jnp.bfloat16),
            pltpu.VMEM((items, rows, nv), jnp.float32),
            pltpu.VMEM((items, nv), jnp.float32),
            pltpu.VMEM((items, nv), jnp.float32),
        ]
        + [pltpu.VMEM((nv, dim), jnp.bfloat16)] * late,
        compiler_params=params,
        cost_estimate=pl.CostEstimate(
            flops=(items + 2 * late) * flops,
            bytes_accessed=2 * late * nv * dim,
            transcendentals=(items + late) * nv * rows,
        ),
        name="late_blocks",
    )(centroids, in_vmem(total), in_vmem(mass), *parts[early:], *pieces, *arrived)
    pieces += [in_vmem(piece) for piece in block]

    if small:
        lse = merge_cent(part, go)
        parts = merge([lse] + [go(lse, mask) for mask in (1, 2, 3)])[None]
    else:
        gathered = lax.all_gather(part, "cent", axis=0, tiled=False)
        parts = lax.all_gather(merge([gathered[i] for i in range(cents)]), "item", axis=0, tiled=False)
    result, norm = pl.pallas_call(
        functools.partial(last_kernel, dict(plan)),
        in_specs=[vmem] * (4 + len(pieces)),
        out_specs=[vmem] * 2,
        out_shape=[
            jax.ShapeDtypeStruct((rows, dim), jnp.bfloat16),
            jax.ShapeDtypeStruct((nv,), jnp.float32),
        ],
        scratch_shapes=[pltpu.VMEM((items, nv), jnp.float32)],
        compiler_params=params,
        cost_estimate=pl.CostEstimate(flops=items * flops, bytes_accessed=2 * rows * dim, transcendentals=0),
        name="last_iteration",
    )(in_vmem(fresh), in_vmem(expo), in_vmem(peak), parts, *pieces)
    return (result, norm)


def solution(mesh):
    in_specs = (P("item", None), P("cent", None))
    out_specs = (P(("cent", "item"), None), P("item"))
    return jax.shard_map(shards, mesh=mesh, in_specs=in_specs, out_specs=out_specs, check_vma=False)
```

```python
import functools
import math

import jax
import jax.numpy as jnp
from jax import lax
from jax.experimental import pallas as pl
from jax.experimental.pallas import tpu as pltpu
from jax.sharding import PartitionSpec as P

BETA = 3.0
BOTH = ("item", "cent")
MIB = 1024 * 1024
NT = (((1,), (1,)), ((), ()))
NN = (((1,), (0,)), ((), ()))


def scores(rows, vectors, scale):
    raw = lax.dot_general(rows, vectors, NT, preferred_element_type=jnp.float32)
    sqnorm = jnp.sum(jnp.square(rows.astype(jnp.float32)), axis=1, keepdims=True)
    return scale * (raw - 0.5 * sqnorm)


def merge(parts):
    peak = functools.reduce(jnp.maximum, parts)
    terms = [jnp.exp(p - peak) for p in parts]
    while len(terms) > 1:
        terms = [sum(terms[i : i + 2]) for i in range(0, len(terms), 2)]
    return peak + jnp.log(terms[0])


def in_hbm(value):
    return pltpu.with_memory_space_constraint(value, pltpu.HBM)


def in_vmem(value):
    return pltpu.with_memory_space_constraint(value, pltpu.VMEM)


def copy_rows(pairs, sems):
    copies = [pltpu.make_async_copy(src, dst, sems.at[i]) for i, (src, dst) in enumerate(pairs)]
    for copy in copies:
        copy.start()
    for copy in copies:
        copy.wait()


def core_index():
    return lax.rem(lax.axis_index("cent"), 2)


def pair_index():
    return lax.rem(lax.axis_index("cent") // 2, 2)


def leads(nv, core):
    half, quarter = nv // 2, nv // 4
    rest = (1 - core) * half
    direct = rest + pair_index() * quarter
    swapped = rest + (1 - pair_index()) * quarter
    return [pl.multiple_of(lead, 64) for lead in (core * half, direct, swapped)]


def outgoing_kernel(v_hbm, out_ref, sems):
    half_lead, direct, _ = leads(v_hbm.shape[0], core_index())
    rows = out_ref.shape[0] // 3
    starts = (half_lead, half_lead + rows, direct)
    copy_rows(
        [
            (v_hbm.at[pl.ds(pl.multiple_of(start, 64), rows), :], out_ref.at[pl.ds(i * rows, rows), :])
            for i, start in enumerate(starts)
        ],
        sems,
    )


def outgoing(vectors):
    nv, dim = vectors.shape
    return pl.pallas_call(
        outgoing_kernel,
        in_specs=[pl.BlockSpec(memory_space=pl.ANY)],
        out_specs=pl.BlockSpec(memory_space=pltpu.VMEM),
        out_shape=pltpu.VMEM((3 * (nv // 4), dim), jnp.bfloat16),
        scratch_shapes=[pltpu.SemaphoreType.DMA((3,))],
        compiler_params=pltpu.CompilerParams(vmem_limit_bytes=2 * MIB),
        cost_estimate=pl.CostEstimate(flops=0, bytes_accessed=2 * nv * dim, transcendentals=0),
        name="outgoing",
    )(in_hbm(vectors))


def load_kernel(v_hbm, c_hbm, v_ref, c_ref, sems):
    pairs = []
    for src, dst, count in ((v_hbm, v_ref, 6), (c_hbm, c_ref, 8)):
        rows = dst.shape[0] // count
        pairs += [(src.at[pl.ds(i * rows, rows), :], dst.at[pl.ds(i * rows, rows), :]) for i in range(count)]
    copy_rows(pairs, sems)


def load(vectors, centroids):
    vmem = pl.BlockSpec(memory_space=pltpu.VMEM)
    hbm = pl.BlockSpec(memory_space=pl.ANY)
    return pl.pallas_call(
        load_kernel,
        in_specs=[hbm, hbm],
        out_specs=[vmem] * 2,
        out_shape=[pltpu.VMEM(vectors.shape, jnp.bfloat16), pltpu.VMEM(centroids.shape, jnp.bfloat16)],
        scratch_shapes=[pltpu.SemaphoreType.DMA((14,))],
        compiler_params=pltpu.CompilerParams(vmem_limit_bytes=2 * MIB),
        cost_estimate=pl.CostEstimate(
            flops=0, bytes_accessed=4 * (vectors.size + centroids.size), transcendentals=0
        ),
        name="load",
    )(in_hbm(vectors), in_hbm(centroids))


def partial_kernel(scale, rows, v_ref, c_ref, out_ref):
    parts = []
    for start in range(0, c_ref.shape[0], rows):
        logits = scores(c_ref[start : start + rows, :], v_ref[...], scale)
        peak = jnp.max(logits, axis=0, keepdims=True)
        parts.append(peak + jnp.log(jnp.sum(jnp.exp(logits - peak), axis=0, keepdims=True)))
    out_ref[...] = merge(parts)


def partial(vectors, centroids, scale):
    nv, dim = vectors.shape
    k = centroids.shape[0]
    vmem = pl.BlockSpec(memory_space=pltpu.VMEM)
    return pl.pallas_call(
        functools.partial(partial_kernel, scale, min(256, k)),
        in_specs=[vmem, vmem],
        out_specs=vmem,
        out_shape=jax.ShapeDtypeStruct((1, nv), jnp.float32),
        compiler_params=pltpu.CompilerParams(vmem_limit_bytes=12 * MIB),
        cost_estimate=pl.CostEstimate(
            flops=2 * nv * k * dim, bytes_accessed=2 * (nv + k) * dim, transcendentals=nv * k
        ),
        name="partial_lse",
    )(in_vmem(vectors), in_vmem(centroids))


def index_of(plan, place):
    if not plan["exchange"]:
        return place
    mask = (0, 1 + core_index(), 2 - core_index(), 3)[place]
    return lax.axis_index("item") ^ mask


def weigh(resp, vectors):
    term = lax.dot_general(resp, vectors, NN, preferred_element_type=jnp.float32)
    return term, jnp.sum(resp.astype(jnp.float32), axis=1, keepdims=True)


def updated(total, mass, old):
    return ((total + old.astype(jnp.float32)) / (mass + 1.0)).astype(jnp.bfloat16)


def own_rows(c_ref, rows):
    return c_ref[pl.ds(pl.multiple_of(lax.axis_index("item") * rows, rows), rows), :]


def absorb(own, vectors, lse, scale, total, mass):
    resp = jnp.exp(scores(own, vectors, scale) - lse).astype(jnp.bfloat16)
    term, weight = weigh(resp, vectors)
    return (term, weight) if total is None else (total + term, mass + weight)


def own_rows(c_ref, rows):
    return c_ref[pl.ds(pl.multiple_of(lax.axis_index("item") * rows, rows), rows), :]


def begin(centroids, home, lse, other, rows, scale):
    nv, dim = home.shape
    vmem = pl.BlockSpec(memory_space=pltpu.VMEM)
    return pl.pallas_call(
        functools.partial(home_kernel, scale),
        in_specs=[vmem] * 3 + [pl.BlockSpec(memory_space=pl.ANY)],
        out_specs=[vmem] * 2,
        out_shape=[pltpu.VMEM((rows, dim), jnp.float32), pltpu.VMEM((rows, 1), jnp.float32)],
        compiler_params=pltpu.CompilerParams(vmem_limit_bytes=16 * MIB),
        cost_estimate=pl.CostEstimate(
            flops=4 * nv * rows * dim, bytes_accessed=2 * nv * dim, transcendentals=nv * rows
        ),
        name="home_block",
    )(in_vmem(centroids), in_vmem(home), lse, other)


def near_kernel(scale, c_ref, near, last, row, total, mass, table, new_total, new_mass):
    half_lead, direct, swapped = leads(table.shape[0], core_index())
    quarter = last.shape[0]
    table[pl.ds(half_lead, 2 * quarter), :] = near[: 2 * quarter, :]
    table[pl.ds(direct, quarter), :] = near[2 * quarter :, :]
    table[pl.ds(swapped, quarter), :] = last[...]
    own = own_rows(c_ref, total.shape[0])
    new_total[...], new_mass[...] = absorb(own, table[...], row[...], scale, total[...], mass[...])


def add_near(centroids, near, swapped, row, begun, scale):
    quarter, dim = swapped.shape
    rows = begun[0].shape[0]
    vmem = pl.BlockSpec(memory_space=pltpu.VMEM)
    return pl.pallas_call(
        functools.partial(near_kernel, scale),
        in_specs=[vmem] * 6,
        out_specs=[vmem] * 3,
        out_shape=[
            pltpu.VMEM((4 * quarter, dim), jnp.bfloat16),
            pltpu.VMEM((rows, dim), jnp.float32),
            pltpu.VMEM((rows, 1), jnp.float32),
        ],
        compiler_params=pltpu.CompilerParams(vmem_limit_bytes=16 * MIB),
        cost_estimate=pl.CostEstimate(
            flops=16 * quarter * rows * dim, bytes_accessed=8 * quarter * dim, transcendentals=4 * quarter * rows
        ),
        name="near_block",
    )(in_vmem(centroids), in_vmem(near), in_vmem(swapped), row, *[in_vmem(value) for value in begun])


def home_kernel(scale, c_ref, home, row, _, total, mass):
    own = own_rows(c_ref, total.shape[0])
    total[...], mass[...] = absorb(own, home[...], row[...], scale, None, None)


def early_kernel(plan, scale, c_ref, *refs):
    n = plan["pieces"]
    first = plan["first"]
    sums = weights = None
    if first:
        sums, weights, refs = refs[0][...], refs[1][...], refs[2:]
    rows, refs = refs[: plan["early"] - first], refs[plan["early"] - first :]
    pieces, arrived, outs = refs[:n], refs[n : n + plan["arrived"]], refs[n + plan["arrived"] :]
    total, mass = outs[:2]
    own = own_rows(c_ref, total.shape[0])
    if arrived:
        table, nv = outs[2], plan["nv"]
        quarter = nv // 4
        half_lead, direct, swapped = leads(nv, 1 - core_index())
        for lead, ref in zip((half_lead, half_lead + quarter, direct, swapped), arrived):
            table[pl.ds(pl.multiple_of(lead, 64), quarter), :] = ref[...]
        pieces += (table,)
    for place in range(first, plan["early"]):
        vectors = vectors_of(plan, place, pieces)
        sums, weights = absorb(own, vectors, rows[place - first][...], scale, sums, weights)
    total[...], mass[...] = sums, weights


def vectors_of(plan, place, pieces):
    operand, start = plan["blocks"][place]
    return pieces[operand][pl.ds(start, plan["nv"]), :]


def late_kernel(plan, scale, c_ref, total, mass, *refs):
    n, early = plan["pieces"], plan["early"]
    rows, refs = refs[: plan["places"] - early], refs[plan["places"] - early :]
    pieces, refs = refs[:n], refs[n:]
    sums, weights = total[...], mass[...]
    if early < plan["places"]:
        mine, other, new_ref, expo_ref, peak_ref, part_ref, block = refs
        pieces += (block,)
        half = mine.shape[0]
        block[pl.ds(pl.multiple_of(core_index() * half, half), half), :] = mine[...]
        block[pl.ds(pl.multiple_of((1 - core_index()) * half, half), half), :] = other[...]
    else:
        new_ref, expo_ref, peak_ref, part_ref = refs
    own = own_rows(c_ref, new_ref.shape[0])
    for place in range(early, plan["places"]):
        vectors = vectors_of(plan, place, pieces)
        sums, weights = absorb(own, vectors, rows[place - early][...], scale, sums, weights)
    new_ref[...] = updated(sums, weights, own)
    for place in range(plan["places"]):
        logits = scores(new_ref[...], vectors_of(plan, place, pieces), scale)
        peak = jnp.max(logits, axis=0, keepdims=True)
        expo = jnp.exp(logits - peak)
        expo_ref[place] = expo
        peak_ref[pl.ds(place, 1), :] = peak
        part_ref[pl.ds(index_of(plan, place), 1), :] = peak + jnp.log(jnp.sum(expo, axis=0, keepdims=True))


def last_kernel(plan, old_ref, expo_ref, peak_ref, parts, *refs):
    pieces, (new_ref, norm_ref, lse_ref) = refs[:-3], refs[-3:]
    lse_ref[...] = merge([parts[i] for i in range(parts.shape[0])])
    norm_ref[...] = lse_ref[pl.ds(lax.axis_index("item"), 1), :].reshape(norm_ref.shape)
    total = mass = None
    for place in range(plan["places"]):
        factor = jnp.exp(peak_ref[pl.ds(place, 1), :] - lse_ref[pl.ds(index_of(plan, place), 1), :])
        resp = (expo_ref[place] * factor).astype(jnp.bfloat16)
        term, weight = weigh(resp, vectors_of(plan, place, pieces))
        total = term if total is None else total + term
        mass = weight if mass is None else mass + weight
    new_ref[...] = updated(total, mass, old_ref[...])


def send(value, items, cents, item_mask, cent_mask=0):
    masks = item_mask if isinstance(item_mask, tuple) else (item_mask, item_mask)
    pairs = [
        (i * cents + c, (i ^ masks[c % 2]) * cents + (c ^ cent_mask)) for i in range(items) for c in range(cents)
    ]
    return lax.ppermute(value, BOTH, pairs)


def merge_cent(part, go):
    part = merge([part, go(part, 0, 1)])
    return merge([part] + [go(part, 0, mask) for mask in (2, 4, 6)])


def after(value, *others):
    vmem = pl.BlockSpec(memory_space=pltpu.VMEM)
    return pl.pallas_call(
        lambda *refs: None,
        in_specs=[vmem] + [pl.BlockSpec(memory_space=pl.ANY)] * len(others),
        out_specs=vmem,
        out_shape=pltpu.VMEM(value.shape, value.dtype),
        input_output_aliases={0: 0},
        compiler_params=pltpu.CompilerParams(vmem_limit_bytes=2 * MIB),
        name="after",
    )(in_vmem(value), *others)


def shards(vectors, centroids):
    items, cents = lax.axis_size("item"), lax.axis_size("cent")
    nv, dim = vectors.shape
    rows = centroids.shape[0] // items
    scale = BETA / math.sqrt(dim)

    def go(value, item_mask, cent_mask=0):
        return send(value, items, cents, item_mask, cent_mask)

    small = items == 4 and cents == 8
    if small:
        near = go(outgoing(vectors), (1, 2))
        home, centroids = load(vectors, centroids)
        lse = merge_cent(partial(home, centroids, scale), go)
        near = after(near, lse)
        quarters = [near[i : i + nv // 4] for i in range(0, near.shape[0], nv // 4)]
        swapped = go(quarters[2], 0, 2)
        far = go(near[: nv // 2], (2, 1))
        crossed = [go(piece, 0, 1) for piece in quarters]
        lse = after(lse, *crossed)
        parts = [lse, go(lse, (1, 2)), go(lse, (2, 1)), go(lse, 3)]
        begun = begin(centroids, home, lse, crossed[2], rows, scale)
        swapped = after(swapped, begun[1], *parts[1:])
        crossed = crossed + [go(swapped, 0, 1)]
        near, *begun = add_near(centroids, near, swapped, parts[1], begun, scale)
        home, near = [home, near], crossed
        pieces = home
        plan = dict(exchange=True, first=2, early=3, blocks=[(i, 0) for i in range(4)])
    else:
        home, centroids = load(vectors, centroids)
        parts = lax.all_gather(partial(home, centroids, scale), "cent", axis=0, tiled=False)
        parts = merge([parts[i] for i in range(cents)])
        parts = lax.all_gather(parts, "item", axis=0, tiled=False)
        parts = [parts[i] for i in range(items)]
        pieces = [lax.all_gather(vectors, "item", axis=0, tiled=True)]
        near = begun = []
        plan = dict(exchange=False, first=0, early=items, blocks=[(0, i * nv) for i in range(items)])
    plan.update(nv=nv, places=items, pieces=len(pieces), arrived=len(near))
    pieces = [in_vmem(piece) for piece in pieces]
    centroids = in_vmem(centroids)

    vmem = pl.BlockSpec(memory_space=pltpu.VMEM)
    flops = 2 * nv * rows * dim
    early, late = plan["early"], items - plan["early"]
    params = pltpu.CompilerParams(vmem_limit_bytes=16 * MIB)
    tables = [pltpu.VMEM((nv, dim), jnp.bfloat16)] if near else []
    total, mass, *table = pl.pallas_call(
        functools.partial(early_kernel, dict(plan), scale),
        in_specs=[vmem] * (1 + len(begun) + early - plan["first"] + len(pieces) + len(near)),
        out_specs=[vmem] * (2 + len(tables)),
        out_shape=[
            pltpu.VMEM((rows, dim), jnp.float32),
            pltpu.VMEM((rows, 1), jnp.float32),
        ]
        + tables,
        compiler_params=params,
        cost_estimate=pl.CostEstimate(flops=0, bytes_accessed=0, transcendentals=0),
        name="early_blocks",
    )(centroids, *[in_vmem(value) for value in begun], *parts[plan["first"] : early], *pieces, *[in_vmem(piece) for piece in near])
    pieces += [in_vmem(piece) for piece in table]
    plan["pieces"] = len(pieces)

    arrived = []
    if late:
        far = after(far, begun[1])
        arrived = [in_vmem(far), in_vmem(go(far, 0, 1))]
    fresh, expo, peak, part, *block = pl.pallas_call(
        functools.partial(late_kernel, dict(plan), scale),
        in_specs=[vmem] * (3 + late + len(pieces) + len(arrived)),
        out_specs=[vmem] * (4 + late),
        out_shape=[
            pltpu.VMEM((rows, dim), jnp.bfloat16),
            pltpu.VMEM((items, rows, nv), jnp.float32),
            pltpu.VMEM((items, nv), jnp.float32),
            pltpu.VMEM((items, nv), jnp.float32),
        ]
        + [pltpu.VMEM((nv, dim), jnp.bfloat16)] * late,
        compiler_params=params,
        cost_estimate=pl.CostEstimate(
            flops=(items + 2 * late) * flops,
            bytes_accessed=2 * late * nv * dim,
            transcendentals=(items + late) * nv * rows,
        ),
        name="late_blocks",
    )(centroids, in_vmem(total), in_vmem(mass), *parts[early:], *pieces, *arrived)
    pieces += [in_vmem(piece) for piece in block]

    if small:
        lse = merge_cent(part, go)
        parts = merge([lse] + [go(lse, mask) for mask in (1, 2, 3)])[None]
    else:
        gathered = lax.all_gather(part, "cent", axis=0, tiled=False)
        parts = lax.all_gather(merge([gathered[i] for i in range(cents)]), "item", axis=0, tiled=False)
    result, norm = pl.pallas_call(
        functools.partial(last_kernel, dict(plan)),
        in_specs=[vmem] * (4 + len(pieces)),
        out_specs=[vmem] * 2,
        out_shape=[
            jax.ShapeDtypeStruct((rows, dim), jnp.bfloat16),
            jax.ShapeDtypeStruct((nv,), jnp.float32),
        ],
        scratch_shapes=[pltpu.VMEM((items, nv), jnp.float32)],
        compiler_params=params,
        cost_estimate=pl.CostEstimate(flops=items * flops, bytes_accessed=2 * rows * dim, transcendentals=0),
        name="last_iteration",
    )(in_vmem(fresh), in_vmem(expo), in_vmem(peak), parts, *pieces)
    return (result, norm)


def solution(mesh):
    in_specs = (P("item", None), P("cent", None))
    out_specs = (P(("cent", "item"), None), P("item"))
    return jax.shard_map(shards, mesh=mesh, in_specs=in_specs, out_specs=out_specs, check_vma=False)
```
